512 devices in a mesh: img: 32 (over y, z_lo, core), txt: 16 (over z_hi, x).
Axes of the slice: x: 4, y: 8, z: 8 (z_hi: 4, z_lo: 2; z = z_hi * 2 + z_lo), core: 2. Of those that a mesh axis runs over, the one named last changes fastest.
Arguments:
- image_emb: float32 [8192, 1152], P(('img', 'txt')), may hold values from -30 to 30
- text_emb: float32 [8192, 1152], P(('img', 'txt')), may hold values from -30 to 30
Outputs:
- loss: float32 [], replicated
- image_grad: float32 [8192, 1152], P(('img', 'txt'))
- text_grad: float32 [8192, 1152], P(('img', 'txt'))
The draws below stay inside these ranges and needn't reach their ends.
All inputs are finite; a program needn't handle non-finite values.
Results may differ from the reference program's by a relative error of at most 0.0003.
Values sent between devices are 32-bit elements; how exact they have to be, the bound alone decides.
No kernel may reach another device: no remote copies, remote signals or barrier semaphores. Data moves between devices by JAX's collectives and lax.ppermute only.
A program may use at most 64 MiB of HBM per device.

```python
import math
import jax
import jax.numpy as jnp
from jax import lax

D = 1152
PAIRS = 8192


def noise_rows(key, count):
    sample = jnp.clip(jax.random.normal(key, (count, D), jnp.float32), -6.0, 6.0)
    return sample / jnp.sqrt(jnp.float32(D))


def shared_parts(key):
    common = jax.random.normal(jax.random.fold_in(key, 5), (1, D), jnp.float32)
    common = common / jnp.sqrt(jnp.sum(common * common))
    image_noise = noise_rows(jax.random.fold_in(key, 7), PAIRS)
    return (common, image_noise)


def row_scales(key):
    return jnp.exp(jax.random.uniform(key, (PAIRS, 1), jnp.float32, jnp.log(0.5), jnp.log(5.0)))


def draw_image_emb(key, part):
    common, image_noise = shared_parts(key)
    key = jax.random.fold_in(key, 11)
    return row_scales(key) * (0.67 * common + 0.74 * image_noise)


def draw_text_emb(key, part):
    common, image_noise = shared_parts(key)
    key = jax.random.fold_in(key, 23)
    key_noise, key_scale = jax.random.split(key)
    own_noise = noise_rows(key_noise, PAIRS)
    mixed = 0.4 * image_noise + 0.92 * own_noise
    return row_scales(key_scale) * (0.67 * common + 0.74 * mixed)


def setup_inputs(seed: int = 0) -> dict:
    key_of = jax.random.split(jax.random.key(seed), 3)
    image_emb = draw_image_emb(jax.random.fold_in(key_of[2], 71), 0)
    text_emb = draw_text_emb(jax.random.fold_in(key_of[2], 71), 0)
    return dict(image_emb=image_emb, text_emb=text_emb)


LOGIT_MULT = 16.0
LOGIT_SHIFT = -10.0
EPSILON = 1e-06

def normalize(values):
    length = jnp.sqrt(lax.optimization_barrier(jnp.sum(values * values, axis=1, keepdims=True)) + EPSILON)
    return (values / length, length)

def project_back(unit, direction, length):
    inner = lax.optimization_barrier(jnp.sum(unit * direction, axis=1, keepdims=True))
    return (direction - unit * inner) / length

def reference(image_emb, text_emb):
    pair_count, feature_count = image_emb.shape
    logit_mult = LOGIT_MULT
    image_unit, image_norm = normalize(image_emb)
    text_unit, text_norm = normalize(text_emb)
    stride = math.gcd(pair_count, 512)
    text_index = jnp.arange(pair_count, dtype=jnp.int32)

    def one_block(state_now, block_index):
        offset = (block_index * stride).astype(jnp.int32)
        image_block = lax.dynamic_slice_in_dim(image_unit, offset, stride, 0)
        logits = logit_mult * jnp.dot(image_block, text_unit.T, precision=lax.Precision.HIGHEST, preferred_element_type=jnp.float32) + LOGIT_SHIFT
        image_index = offset + jnp.arange(stride, dtype=jnp.int32)
        target = jnp.where(image_index[:, None] == text_index[None, :], 1.0, -1.0).astype(jnp.float32)
        loss_part = jnp.sum(jax.nn.softplus(-target * logits))
        slope = -target * jax.nn.sigmoid(-target * logits) / pair_count
        image_dir = logit_mult * jnp.dot(slope, text_unit, precision=lax.Precision.HIGHEST, preferred_element_type=jnp.float32)
        text_acc = state_now[0] + logit_mult * jnp.dot(slope.T, image_block, precision=lax.Precision.HIGHEST, preferred_element_type=jnp.float32)
        return ((text_acc, state_now[1] + loss_part), image_dir)
    initial = (jnp.zeros((pair_count, feature_count), jnp.float32), jnp.zeros((), jnp.float32))
    (text_dir, loss_total), image_blocks = lax.scan(one_block, initial, jnp.arange(pair_count // stride, dtype=jnp.int32))
    image_dir = image_blocks.reshape(pair_count, feature_count)
    loss = loss_total / pair_count
    return (loss, project_back(image_unit, image_dir, image_norm), project_back(text_unit, text_dir, text_norm))
```

```python
import jax
import jax.numpy as jnp
from jax import lax
from jax.sharding import Mesh, PartitionSpec as P

LOGIT_MULT = 16.0
LOGIT_SHIFT = -10.0
EPSILON = 1e-06

AXES = ("y", "zl", "c", "zh", "x")
SIZES = (8, 2, 2, 4, 4)
LANES = 128


def normalize(values):
    length = jnp.sqrt(jnp.sum(values * values, axis=1, keepdims=True) + EPSILON)
    return (values / length, length)


def project_back(unit, direction, length):
    inner = jnp.sum(unit * direction, axis=1, keepdims=True)
    return (direction - unit * inner) / length


def full_dot(left, right):
    return jnp.dot(left, right, precision=lax.Precision.HIGHEST, preferred_element_type=jnp.float32)


def shifted(values, axis, step):
    count = lax.axis_size(axis)
    return lax.ppermute(values, axis, [(i, (i + step) % count) for i in range(count)])


def exchange(values, axes):
    return lax.all_to_all(values, axes, 0, 0, tiled=True)


def on_device(image_emb, text_emb):
    rows, features = image_emb.shape
    y_count = lax.axis_size("y")
    pair_count = rows * lax.axis_size(AXES)
    text_unit, text_norm = normalize(text_emb)
    image_unit, image_norm = normalize(image_emb)

    text_y = exchange(jnp.tile(text_unit, (y_count, 1)), "y")
    image_z = jnp.concatenate([image_unit] + [shifted(image_unit, "zh", k) for k in range(1, 4)])
    image_block = jnp.concatenate([image_z] + [shifted(image_z, "x", k) for k in range(1, 4)])
    text_z = jnp.concatenate([text_y, shifted(text_y, "zl", 1)])
    text_block = jnp.concatenate([text_z, shifted(text_z, "c", 1)])

    own = lax.axis_index("y") * rows
    image_index = jnp.arange(image_block.shape[0], dtype=jnp.int32)
    text_index = jnp.arange(text_block.shape[0], dtype=jnp.int32) - own
    matched = (image_index[:, None] == text_index[None, :]) & (image_index[:, None] < rows)
    target = jnp.where(matched, 1.0, -1.0).astype(jnp.float32)
    logits = LOGIT_MULT * full_dot(image_block, text_block.T) + LOGIT_SHIFT
    loss_part = jnp.sum(jax.nn.softplus(-target * logits))
    slope = -target * jax.nn.sigmoid(-target * logits) / pair_count

    group = ("zl", "c", "zh", "x")
    losses = exchange(jnp.full((lax.axis_size(group), LANES), loss_part), group)
    loss_group = jnp.sum(losses[:, 0])

    text_term = LOGIT_MULT * full_dot(slope.T, image_block)
    image_term = LOGIT_MULT * full_dot(slope, text_block)

    half = text_term.shape[0] // 2
    text_c = text_term[:half] + shifted(text_term[half:], "c", 1)
    quarter = half // 2
    text_zl = text_c[:quarter] + shifted(text_c[quarter:], "zl", 1)

    parts = image_term.reshape(4, -1, features)
    image_x = parts[0] + sum(shifted(parts[k], "x", -k) for k in range(1, 4))
    parts = image_x.reshape(4, -1, features)
    image_dir = parts[0] + sum(shifted(parts[k], "zh", -k) for k in range(1, 4))

    packed = text_zl.reshape(y_count, rows * features // LANES, LANES)
    packed = jnp.concatenate([packed, jnp.full((y_count, 8, LANES), loss_group)], axis=1)
    packed = jnp.sum(exchange(packed, "y"), axis=0)
    text_dir = packed[:-8].reshape(rows, features)
    loss = packed[-1, 0] / pair_count
    return (
        loss,
        project_back(image_unit, image_dir, image_norm),
        project_back(text_unit, text_dir, text_norm),
    )


def solution(mesh):
    split = Mesh(mesh.devices.reshape(SIZES), AXES)
    return jax.shard_map(
        on_device,
        mesh=split,
        in_specs=(P(AXES, None), P(AXES, None)),
        out_specs=(P(), P(AXES, None), P(AXES, None)),
        check_vma=False,
    )
```

```python
import jax
import jax.numpy as jnp
from jax import lax
from jax.experimental import pallas as pl
from jax.experimental.pallas import tpu as pltpu
from jax.sharding import Mesh, PartitionSpec as P

LOGIT_MULT = 16.0
LOGIT_SHIFT = -10.0
EPSILON = 1e-06

AXES = ("y", "zl", "c", "zh", "x")
SIZES = (8, 2, 2, 4, 4)
NY, NZH, NX = 8, 4, 4
ROWS, FEATURES, LANES = 16, 1152, 128
COLS = FEATURES // LANES
PACK = COLS * ROWS
PAIRS = 8192
F32, BF16 = jnp.float32, jnp.bfloat16

VMEM = pl.BlockSpec(memory_space=pltpu.VMEM)
ANY = pl.BlockSpec(memory_space=pl.ANY)
SMEM = pl.BlockSpec(memory_space=pltpu.SMEM)


def shape(*dims):
    return jax.ShapeDtypeStruct(dims, F32)


def call(kernel, ins, outs, in_specs=None, out_specs=None, flops=0, **kw):
    moved = 4 * sum(a.size for a in list(ins) + list(outs))
    return pl.pallas_call(
        kernel,
        out_shape=outs,
        in_specs=in_specs or [VMEM] * len(ins),
        out_specs=out_specs or [VMEM] * len(outs),
        cost_estimate=pl.CostEstimate(flops=flops, bytes_accessed=moved, transcendentals=0),
        compiler_params=pltpu.CompilerParams(vmem_limit_bytes=40 * 2**20),
        **kw,
    )(*ins)


def shifted(values, axis, step):
    count = lax.axis_size(axis)
    return lax.ppermute(values, axis, [(i, (i + step) % count) for i in range(count)])


def exchange(values, axes):
    return lax.all_to_all(values, axes, 0, 0, tiled=True)


def normalize(values):
    length = jnp.sqrt(jnp.sum(values * values, axis=1, keepdims=True) + EPSILON)
    return values / length, length


def project_back(unit, direction, length):
    inner = jnp.sum(unit * direction, axis=1, keepdims=True)
    return (direction - unit * inner) / length


def halves(values):
    high = values.astype(BF16)
    return high, (values - high.astype(F32)).astype(BF16)


def dot3(left, right, dims):
    def dot(a, b):
        return lax.dot_general(a, b, (dims, ((), ())), preferred_element_type=F32)

    return dot(left[1], right[0]) + dot(left[0], right[1]) + dot(left[0], right[0])


def normalize_kernel(image_ref, text_ref, image_out, text_out):
    image_out[...] = normalize(image_ref[...])[0]
    text_unit = normalize(text_ref[...])[0]
    for y in range(NY):
        text_out[pl.ds(y * ROWS, ROWS), :] = text_unit


def spread_kernel(z0, z1, z2, z3, text_ref, image_out, text_out):
    for x in range(NX):
        for k, part in enumerate((z0, z1, z2, z3)):
            image_out[pl.ds((x * NZH + k) * ROWS, ROWS), :] = part[...]


def logits_kernel(place, image_ref, a_ref, b_ref, c_ref, d_ref, slope_out, other_out, loss_out):
    image = halves(image_ref[...])
    quarter = a_ref.shape[0]
    count = image_ref.shape[0]
    row = lax.broadcasted_iota(jnp.int32, (count, quarter), 0) - place[0]
    column = lax.broadcasted_iota(jnp.int32, (count, quarter), 1) - place[1]
    matched = (row == column) & (row >= 0) & (row < ROWS)
    total = jnp.zeros((), F32)
    for k, ref in enumerate((c_ref, d_ref, a_ref, b_ref)):
        logits = LOGIT_MULT * dot3(image, halves(ref[...]), ((1,), (1,))) + LOGIT_SHIFT
        if ref is a_ref:
            logits = jnp.where(matched, -logits, logits)
        small = jnp.exp(-jnp.abs(logits))
        total += jnp.sum(jnp.maximum(logits, 0.0) + jnp.log1p(small))
        slope = jnp.where(logits >= 0.0, 1.0, small) / (1.0 + small) * (LOGIT_MULT / PAIRS)
        if ref is a_ref:
            slope = jnp.where(matched, -slope, slope)
        slope_out[:, pl.ds((k + 2) % 4 * quarter, quarter)] = slope
        if k < 2:
            other_out[pl.ds(k * quarter, quarter), :] = dot3(halves(slope), image, ((0,), (0,)))
    loss_out[...] = jnp.full(loss_out.shape, total)


def image_kernel(slope_ref, a_ref, b_ref, c_ref, d_ref, out):
    quarter = a_ref.shape[0]
    total = None
    for k, ref in enumerate((a_ref, b_ref, c_ref, d_ref)):
        slope = slope_ref[:, pl.ds(k * quarter, quarter)]
        term = dot3(halves(slope), halves(ref[...]), ((1,), (0,)))
        total = term if total is None else total + term
    out[...] = total


def text_kernel(slope_ref, image_ref, other_ref, keep_out, send_out):
    image = halves(image_ref[...])
    quarter = keep_out.shape[0]
    for k, out in ((1, send_out), (0, keep_out)):
        rows = pl.ds(k * quarter, quarter)
        out[...] = dot3(halves(slope_ref[:, rows]), image, ((0,), (0,))) + other_ref[rows, :]


def join_kernel(image_ref, keep_ref, received_ref, losses_ref, packed_out, *zs):
    count = image_ref.shape[0] // NX
    for k, out in enumerate(zs):
        rows = [pl.ds(x * count + k * ROWS, ROWS) for x in range(NX)]
        out[...] = (image_ref[rows[0], :] + image_ref[rows[1], :]) + (image_ref[rows[2], :] + image_ref[rows[3], :])
    loss = jnp.sum(losses_ref[:, 0:1])
    for y in range(NY):
        rows = pl.ds(y * ROWS, ROWS)
        for k in range(COLS):
            lanes = pl.ds(k * LANES, LANES)
            packed_out[y, pl.ds(k * ROWS, ROWS), :] = keep_ref[rows, lanes] + received_ref[rows, lanes]
        packed_out[y, pl.ds(PACK, 8), :] = jnp.full((8, LANES), loss)


def image_grad_kernel(emb_ref, z0, z1, z2, z3, out):
    unit, length = normalize(emb_ref[...])
    out[...] = project_back(unit, (z0[...] + z1[...]) + (z2[...] + z3[...]), length)


def text_grad_kernel(emb_ref, packed_ref, out, loss_out):
    unit, length = normalize(emb_ref[...])
    total = packed_ref[0]
    for y in range(1, NY):
        total = total + packed_ref[y]
    direction = jnp.concatenate([total[k * ROWS : (k + 1) * ROWS] for k in range(COLS)], axis=1)
    out[...] = project_back(unit, direction, length)
    loss_out[...] = total[PACK:] / PAIRS


def on_device(image_emb, text_emb):
    rows, features = image_emb.shape
    image_unit, text_tiled = call(
        normalize_kernel, (image_emb, text_emb), [shape(rows, features), shape(NY * rows, features)]
    )
    text_y = exchange(text_tiled, "y")
    zs = [image_unit] + [shifted(image_unit, "zh", k) for k in range(1, NZH)]
    image_tiled, text_a = call(
        spread_kernel,
        (*zs, text_y),
        [shape(NX * NZH * rows, features), shape(*text_y.shape)],
        in_specs=[VMEM] * 4 + [ANY],
        out_specs=[VMEM, ANY],
        input_output_aliases={4: 1},
    )
    image = exchange(image_tiled, "x")
    text_b = shifted(text_a, "zl", 1)
    text_c = shifted(text_a, "c", 1)
    text_d = shifted(text_b, "c", 1)

    place = jnp.stack([lax.axis_index("x") * (NZH * rows), lax.axis_index("y") * rows]).astype(jnp.int32)
    count, quarter = image.shape[0], text_a.shape[0]
    product = 2 * count * quarter * features * 3
    slope, other, loss = call(
        logits_kernel,
        (place, image, text_a, text_b, text_c, text_d),
        [shape(count, 4 * quarter), shape(2 * quarter, features), shape(64, LANES)],
        in_specs=[SMEM] + [VMEM] * 5,
        flops=6 * product,
    )
    received = shifted(other, "c", 1)
    losses = exchange(loss, ("zl", "c", "zh", "x"))
    (image_term,) = call(
        image_kernel, (slope, text_a, text_b, text_c, text_d), [shape(count, features)], flops=4 * product
    )
    image_x = exchange(image_term, "x")
    keep, send = call(
        text_kernel, (slope, image, received), [shape(quarter, features)] * 2, flops=2 * product
    )
    received = shifted(send, "zl", 1)
    packed, *zs = call(
        join_kernel,
        (image_x, keep, received, losses),
        [shape(NY, PACK + 8, LANES)] + [shape(rows, features)] * NZH,
    )
    packed = exchange(packed, "y")
    zs = [zs[0]] + [shifted(zs[k], "zh", -k) for k in range(1, NZH)]
    (image_grad,) = call(image_grad_kernel, (image_emb, *zs), [shape(rows, features)])
    text_grad, loss = call(text_grad_kernel, (text_emb, packed), [shape(rows, features), shape(8, LANES)])
    return loss[0, 0], image_grad, text_grad


def solution(mesh):
    split = Mesh(mesh.devices.reshape(SIZES), AXES)
    return jax.shard_map(
        on_device,
        mesh=split,
        in_specs=(P(AXES, None), P(AXES, None)),
        out_specs=(P(), P(AXES, None), P(AXES, None)),
        check_vma=False,
    )
```

```python
import jax
import jax.numpy as jnp
from jax import lax
from jax.experimental import pallas as pl
from jax.experimental.pallas import tpu as pltpu
from jax.sharding import Mesh, PartitionSpec as P

LOGIT_MULT = 16.0
LOGIT_SHIFT = -10.0
EPSILON = 1e-06

AXES = ("y", "zl", "c", "zh", "x")
SIZES = (8, 2, 2, 4, 4)
NY, NZH, NX = 8, 4, 4
ROWS, FEATURES, LANES = 16, 1152, 128
COLS = FEATURES // LANES
PACK = COLS * ROWS
PAIRS = 8192
F32, BF16 = jnp.float32, jnp.bfloat16

VMEM = pl.BlockSpec(memory_space=pltpu.VMEM)
ANY = pl.BlockSpec(memory_space=pl.ANY)
SMEM = pl.BlockSpec(memory_space=pltpu.SMEM)


def shape(*dims):
    return jax.ShapeDtypeStruct(dims, F32)


def call(kernel, ins, outs, in_specs=None, out_specs=None, flops=0, **kw):
    moved = 4 * sum(a.size for a in list(ins) + list(outs))
    return pl.pallas_call(
        kernel,
        out_shape=outs,
        in_specs=in_specs or [VMEM] * len(ins),
        out_specs=out_specs or [VMEM] * len(outs),
        cost_estimate=pl.CostEstimate(flops=flops, bytes_accessed=moved, transcendentals=0),
        compiler_params=pltpu.CompilerParams(vmem_limit_bytes=24 * 2**20),
        **kw,
    )(*ins)


def exchange(values, axes):
    return lax.all_to_all(values, axes, 0, 0, tiled=True)


def turned(values, axis, step):
    count = lax.axis_size(axis)
    pairs = [(c * count + i, c * count + (i + (1 - 2 * c) * step) % count) for c in range(2) for i in range(count)]
    return lax.ppermute(values, ("c", axis), pairs)


def planes(values, step):
    pairs = []
    for c in range(2):
        for z in range(2 * NZH):
            to = (z + (1 - 2 * c) * step) % (2 * NZH)
            pairs.append((((z % 2) * 2 + c) * NZH + z // 2, ((to % 2) * 2 + c) * NZH + to // 2))
    return lax.ppermute(values, ("zl", "c", "zh"), pairs)


def other_core(values):
    return lax.ppermute(values, "c", [(0, 1), (1, 0)])


def ring_gather(values, axis):
    back = turned(values, axis, 1)
    ahead = turned(values, axis, -1)
    return values, back, ahead, turned(back, axis, 1)


def normalize(values):
    length = jnp.sqrt(jnp.sum(values * values, axis=1, keepdims=True) + EPSILON)
    return values / length, length


def project_back(unit, direction, length):
    inner = jnp.sum(unit * direction, axis=1, keepdims=True)
    return (direction - unit * inner) / length


def halves(values):
    high = values.astype(BF16)
    return high, (values - high.astype(F32)).astype(BF16)


def dot3(left, right, dims):
    def dot(a, b):
        return lax.dot_general(a, b, (dims, ((), ())), preferred_element_type=F32)

    return dot(left[1], right[0]) + dot(left[0], right[1]) + dot(left[0], right[0])


def normalize_kernel(image_ref, text_ref, image_out, text_out):
    image_out[...] = normalize(image_ref[...])[0]
    text_unit = normalize(text_ref[...])[0]
    for y in range(NY):
        text_out[pl.ds(y * ROWS, ROWS), :] = text_unit


def stack_kernel(*refs):
    for k, part in enumerate(refs[:-1]):
        refs[-1][pl.ds(k * ROWS, ROWS), :] = part[...]


def tie_kernel(*refs):
    pass


def stacked(*refs):
    return jnp.concatenate([ref[...] for ref in refs], axis=0)


def logits_kernel(place, i0, i1, i2, i3, a_ref, b_ref, c_ref, d_ref, slope_out, other_out, loss_out):
    image = halves(stacked(i0, i1, i2, i3))
    quarter = a_ref.shape[0]
    count = NX * i0.shape[0]
    row = lax.broadcasted_iota(jnp.int32, (count, quarter), 0)
    column = lax.broadcasted_iota(jnp.int32, (count, quarter), 1) - place[0]
    matched = (row == column) & (row < ROWS)
    total = jnp.zeros((), F32)
    for k, ref in enumerate((c_ref, d_ref, a_ref, b_ref)):
        logits = LOGIT_MULT * dot3(image, halves(ref[...]), ((1,), (1,))) + LOGIT_SHIFT
        if ref is a_ref:
            logits = jnp.where(matched, -logits, logits)
        small = jnp.exp(-jnp.abs(logits))
        total += jnp.sum(jnp.maximum(logits, 0.0) + jnp.log1p(small))
        slope = jnp.where(logits >= 0.0, 1.0, small) / (1.0 + small) * (LOGIT_MULT / PAIRS)
        if ref is a_ref:
            slope = jnp.where(matched, -slope, slope)
        slope_out[:, pl.ds((k + 2) % 4 * quarter, quarter)] = slope
        if k < 2:
            other_out[pl.ds(k * quarter, quarter), :] = dot3(halves(slope), image, ((0,), (0,)))
    loss_out[...] = jnp.full(loss_out.shape, total)


def image_kernel(slope_ref, a_ref, b_ref, c_ref, d_ref, *outs):
    quarter = a_ref.shape[0]
    total = None
    for k, ref in enumerate((a_ref, b_ref, c_ref, d_ref)):
        slope = slope_ref[:, pl.ds(k * quarter, quarter)]
        term = dot3(halves(slope), halves(ref[...]), ((1,), (0,)))
        total = term if total is None else total + term
    rows = total.shape[0] // NX
    for k, out in enumerate(outs):
        out[...] = total[k * rows : (k + 1) * rows]


def text_kernel(slope_ref, i0, i1, i2, i3, other_ref, keep_out, send_out):
    image = halves(stacked(i0, i1, i2, i3))
    quarter = keep_out.shape[0]
    for k, out in ((1, send_out), (0, keep_out)):
        rows = pl.ds(k * quarter, quarter)
        out[...] = dot3(halves(slope_ref[:, rows]), image, ((0,), (0,))) + other_ref[rows, :]


def add_kernel(left, right, out):
    out[...] = left[...] + right[...]


def join_kernel(x0, x1, x2, keep_ref, received_ref, losses_ref, packed_out, *zs):
    for k, out in enumerate(zs):
        rows = pl.ds(k * ROWS, ROWS)
        out[...] = x0[rows, :] + (x1[rows, :] + x2[rows, :])
    loss = jnp.sum(losses_ref[:, 0:1])
    for y in range(NY):
        rows = pl.ds(y * ROWS, ROWS)
        for k in range(COLS):
            lanes = pl.ds(k * LANES, LANES)
            packed_out[y, pl.ds(k * ROWS, ROWS), :] = keep_ref[rows, lanes] + received_ref[rows, lanes]
        packed_out[y, pl.ds(PACK, 8), :] = jnp.full((8, LANES), loss)


def image_grad_kernel(emb_ref, z0, z1, z2, out):
    unit, length = normalize(emb_ref[...])
    out[...] = project_back(unit, z0[...] + (z1[...] + z2[...]), length)


def text_grad_kernel(emb_ref, packed_ref, out, loss_out):
    unit, length = normalize(emb_ref[...])
    total = packed_ref[0]
    for y in range(1, NY):
        total = total + packed_ref[y]
    direction = jnp.concatenate([total[k * ROWS : (k + 1) * ROWS] for k in range(COLS)], axis=1)
    out[...] = project_back(unit, direction, length)
    loss_out[...] = total[PACK:] / PAIRS


def on_device(image_emb, text_emb):
    rows, features = image_emb.shape
    image_unit, text_tiled = call(
        normalize_kernel, (image_emb, text_emb), [shape(rows, features), shape(NY * rows, features)]
    )
    text_y = exchange(text_tiled, "y")
    (image_z,) = call(stack_kernel, ring_gather(image_unit, "zh"), [shape(NZH * rows, features)])
    images = ring_gather(image_z, "x")
    (text_a,) = call(
        tie_kernel, (text_y, image_z), [shape(*text_y.shape)], [ANY] * 2, [ANY], input_output_aliases={0: 0}
    )
    text_b = planes(text_a, -1)
    text_c = other_core(text_a)
    text_d = other_core(text_b)
    texts = (text_a, text_b, text_c, text_d)

    place = (lax.axis_index("y") * rows).astype(jnp.int32).reshape(1)
    part, quarter = image_z.shape[0], text_a.shape[0]
    product = 2 * NX * part * quarter * features * 3
    slope, other, loss = call(
        logits_kernel,
        (place, *images, *texts),
        [shape(NX * part, 4 * quarter), shape(2 * quarter, features), shape(64, LANES)],
        in_specs=[SMEM] + [VMEM] * 8,
        flops=6 * product,
    )
    received = other_core(other)
    xs = call(image_kernel, (slope, *texts), [shape(part, features)] * NX, flops=4 * product)
    relay = turned(xs[3], "x", -1)
    ahead = turned(xs[2], "x", 1)
    keep, send = call(
        text_kernel, (slope, *images, received), [shape(quarter, features)] * 2, flops=2 * product
    )
    received = planes(send, 1)
    (relay,) = call(add_kernel, (xs[1], relay), [shape(part, features)])
    back = turned(relay, "x", -1)
    losses = exchange(loss, ("zl", "c", "zh", "x"))
    packed, *zs = call(
        join_kernel,
        (xs[0], back, ahead, keep, received, losses),
        [shape(NY, PACK + 8, LANES)] + [shape(rows, features)] * NZH,
    )
    packed = exchange(packed, "y")
    relay = turned(zs[3], "zh", -1)
    ahead = turned(zs[2], "zh", 1)
    (relay,) = call(add_kernel, (zs[1], relay), [shape(rows, features)])
    back = turned(relay, "zh", -1)
    (image_grad,) = call(image_grad_kernel, (image_emb, zs[0], back, ahead), [shape(rows, features)])
    text_grad, loss = call(text_grad_kernel, (text_emb, packed), [shape(rows, features), shape(8, LANES)])
    return loss[0, 0], image_grad, text_grad


def solution(mesh):
    split = Mesh(mesh.devices.reshape(SIZES), AXES)
    return jax.shard_map(
        on_device,
        mesh=split,
        in_specs=(P(AXES, None), P(AXES, None)),
        out_specs=(P(), P(AXES, None), P(AXES, None)),
        check_vma=False,
    )
```

```python
import jax
import jax.numpy as jnp
from jax import lax
from jax.experimental import pallas as pl
from jax.experimental.pallas import tpu as pltpu
from jax.sharding import Mesh, PartitionSpec as P

LOGIT_MULT = 16.0
LOGIT_SHIFT = -10.0
EPSILON = 1e-06

AXES = ("y", "zl", "c", "zh", "x")
SIZES = (8, 2, 2, 4, 4)
NY, NZH, NX = 8, 4, 4
ROWS, FEATURES, LANES = 16, 1152, 128
COLS = FEATURES // LANES
PACK = COLS * ROWS
PAIRS = 8192
F32, BF16 = jnp.float32, jnp.bfloat16

VMEM = pl.BlockSpec(memory_space=pltpu.VMEM)
ANY = pl.BlockSpec(memory_space=pl.ANY)
SMEM = pl.BlockSpec(memory_space=pltpu.SMEM)
HBM = pl.BlockSpec(memory_space=pltpu.HBM)


def shape(*dims):
    return jax.ShapeDtypeStruct(dims, F32)


def call(kernel, ins, outs, in_specs=None, out_specs=None, flops=0, **kw):
    moved = 4 * sum(a.size for a in list(ins) + list(outs))
    return pl.pallas_call(
        kernel,
        out_shape=outs,
        in_specs=in_specs or [VMEM] * len(ins),
        out_specs=out_specs or [VMEM] * len(outs),
        cost_estimate=pl.CostEstimate(flops=flops, bytes_accessed=moved, transcendentals=0),
        compiler_params=pltpu.CompilerParams(vmem_limit_bytes=24 * 2**20),
        **kw,
    )(*ins)


def exchange(values, axes):
    return lax.all_to_all(values, axes, 0, 0, tiled=True)


def turned(values, axis, step):
    count = lax.axis_size(axis)
    pairs = [(c * count + i, c * count + (i + (1 - 2 * c) * step) % count) for c in range(2) for i in range(count)]
    return lax.ppermute(values, ("c", axis), pairs)


def planes(values, step):
    pairs = []
    for c in range(2):
        for z in range(2 * NZH):
            to = (z + (1 - 2 * c) * step) % (2 * NZH)
            pairs.append((((z % 2) * 2 + c) * NZH + z // 2, ((to % 2) * 2 + c) * NZH + to // 2))
    return lax.ppermute(values, ("zl", "c", "zh"), pairs)


def other_core(values):
    return lax.ppermute(values, "c", [(0, 1), (1, 0)])


def ring_gather(values, axis):
    back = turned(values, axis, 1)
    ahead = turned(values, axis, -1)
    return values, back, ahead, turned(back, axis, 1)


def normalize(values):
    length = jnp.sqrt(jnp.sum(values * values, axis=1, keepdims=True) + EPSILON)
    return values / length, length


def project_back(unit, direction, length):
    inner = jnp.sum(unit * direction, axis=1, keepdims=True)
    return (direction - unit * inner) / length


def halves(values):
    high = values.astype(BF16)
    return high, (values - high.astype(F32)).astype(BF16)


def dot3(left, right, dims):
    def dot(a, b):
        return lax.dot_general(a, b, (dims, ((), ())), preferred_element_type=F32)

    return dot(left[1], right[0]) + dot(left[0], right[1]) + dot(left[0], right[0])


def normalize_kernel(image_hbm, text_hbm, image_out, text_out, image_ref, text_ref, sems):
    copies = [
        pltpu.make_async_copy(text_hbm, text_ref, sems.at[0]),
        pltpu.make_async_copy(image_hbm, image_ref, sems.at[1]),
    ]
    for copy in copies:
        copy.start()
    copies[0].wait()
    text_unit = normalize(text_ref[...])[0]
    for y in range(NY):
        text_out[pl.ds(y * ROWS, ROWS), :] = text_unit
    copies[1].wait()
    image_out[...] = normalize(image_ref[...])[0]


def stack_kernel(*refs):
    for k, part in enumerate(refs[:-1]):
        refs[-1][pl.ds(k * ROWS, ROWS), :] = part[...]


def tie_kernel(*refs):
    pass


def pair_kernel(a_ref, b_ref, x1, x2, out):
    half = a_ref.shape[0]
    out[pl.ds(0, half), :] = a_ref[...]
    out[pl.ds(half, half), :] = b_ref[...]


def stacked(*refs):
    return jnp.concatenate([ref[...] for ref in refs], axis=0)


def logits_kernel(place, i0, i1, i2, i3, own_ref, far_ref, slope_out, other_out, loss_out):
    image = halves(stacked(i0, i1, i2, i3))
    quarter = own_ref.shape[0] // 2
    count = NX * i0.shape[0]
    row = lax.broadcasted_iota(jnp.int32, (count, quarter), 0)
    column = lax.broadcasted_iota(jnp.int32, (count, quarter), 1) - place[0]
    matched = (row == column) & (row < ROWS)
    total = jnp.zeros((), F32)
    for k, (ref, half) in enumerate(((far_ref, 0), (far_ref, 1), (own_ref, 0), (own_ref, 1))):
        text = halves(ref[pl.ds(half * quarter, quarter), :])
        logits = LOGIT_MULT * dot3(image, text, ((1,), (1,))) + LOGIT_SHIFT
        if k == 2:
            logits = jnp.where(matched, -logits, logits)
        small = jnp.exp(-jnp.abs(logits))
        total += jnp.sum(jnp.maximum(logits, 0.0) + jnp.log1p(small))
        slope = jnp.where(logits >= 0.0, 1.0, small) / (1.0 + small) * (LOGIT_MULT / PAIRS)
        if k == 2:
            slope = jnp.where(matched, -slope, slope)
        slope_out[:, pl.ds((k + 2) % 4 * quarter, quarter)] = slope
        if k < 2:
            other_out[pl.ds(k * quarter, quarter), :] = dot3(halves(slope), image, ((0,), (0,)))
    loss_out[...] = jnp.full(loss_out.shape, total)


def image_kernel(slope_ref, own_ref, far_ref, *outs):
    half = own_ref.shape[0]
    total = None
    for k, ref in enumerate((own_ref, far_ref)):
        slope = slope_ref[:, pl.ds(k * half, half)]
        term = dot3(halves(slope), halves(ref[...]), ((1,), (0,)))
        total = term if total is None else total + term
    rows = total.shape[0] // NX
    for k, out in enumerate(outs):
        out[...] = total[k * rows : (k + 1) * rows]


def text_kernel(slope_ref, i0, i1, i2, i3, other_ref, keep_out, send_out):
    image = halves(stacked(i0, i1, i2, i3))
    quarter = keep_out.shape[0]
    for k, out in ((1, send_out), (0, keep_out)):
        rows = pl.ds(k * quarter, quarter)
        out[...] = dot3(halves(slope_ref[:, rows]), image, ((0,), (0,))) + other_ref[rows, :]


def add_kernel(left, right, *refs):
    refs[-1][...] = left[...] + right[...]


def join_kernel(x0, x1, x2, keep_ref, received_ref, losses_ref, packed_out, *zs):
    for k, out in enumerate(zs):
        rows = pl.ds(k * ROWS, ROWS)
        out[...] = x0[rows, :] + (x1[rows, :] + x2[rows, :])
    loss = jnp.sum(losses_ref[:, 0:1])
    for y in range(NY):
        rows = pl.ds(y * ROWS, ROWS)
        for k in range(COLS):
            lanes = pl.ds(k * LANES, LANES)
            packed_out[y, pl.ds(k * ROWS, ROWS), :] = keep_ref[rows, lanes] + received_ref[rows, lanes]
        packed_out[y, pl.ds(PACK, 8), :] = jnp.full((8, LANES), loss)


def image_grad_kernel(emb_ref, z0, z1, z2, out):
    unit, length = normalize(emb_ref[...])
    out[...] = project_back(unit, z0[...] + (z1[...] + z2[...]), length)


def text_grad_kernel(emb_ref, packed_ref, out, loss_out):
    unit, length = normalize(emb_ref[...])
    total = packed_ref[0]
    for y in range(1, NY):
        total = total + packed_ref[y]
    direction = jnp.concatenate([total[k * ROWS : (k + 1) * ROWS] for k in range(COLS)], axis=1)
    out[...] = project_back(unit, direction, length)
    loss_out[0, 0] = jnp.max(total[PACK:]) / PAIRS


def on_device(image_emb, text_emb):
    rows, features = image_emb.shape
    image_unit, text_tiled = call(
        normalize_kernel,
        (image_emb, text_emb),
        [shape(rows, features), shape(NY * rows, features)],
        in_specs=[HBM] * 2,
        scratch_shapes=[pltpu.VMEM((rows, features), F32)] * 2 + [pltpu.SemaphoreType.DMA((2,))],
    )
    text_a = exchange(text_tiled, "y")
    (image_z,) = call(stack_kernel, ring_gather(image_unit, "zh"), [shape(NZH * rows, features)])
    images = ring_gather(image_z, "x")
    (text_a,) = call(
        tie_kernel, (text_a, image_z), [shape(*text_a.shape)], [ANY] * 2, [ANY], input_output_aliases={0: 0}
    )
    quarter = text_a.shape[0]
    (own,) = call(
        pair_kernel,
        (text_a, planes(text_a, -1), *images[1:3]),
        [shape(2 * quarter, features)],
        in_specs=[VMEM] * 2 + [ANY] * 2,
    )
    texts = (own, other_core(own))

    place = (lax.axis_index("y") * rows).astype(jnp.int32).reshape(1)
    part = image_z.shape[0]
    product = 2 * NX * part * quarter * features * 3
    slope, other, loss = call(
        logits_kernel,
        (place, *images, *texts),
        [shape(NX * part, 4 * quarter), shape(2 * quarter, features), shape(64, LANES)],
        in_specs=[SMEM] + [VMEM] * 6,
        flops=6 * product,
    )
    received = other_core(other)
    xs = call(image_kernel, (slope, *texts), [shape(part, features)] * NX, flops=4 * product)
    relay = turned(xs[3], "x", -1)
    ahead = turned(xs[2], "x", 1)
    keep, send = call(
        text_kernel, (slope, *images, received), [shape(quarter, features)] * 2, flops=2 * product
    )
    received = planes(send, 1)
    losses = exchange(loss, ("zl", "c", "zh", "x"))
    (relay,) = call(
        add_kernel, (xs[1], relay, losses), [shape(part, features)], in_specs=[VMEM] * 2 + [ANY]
    )
    back = turned(relay, "x", -1)
    packed, *zs = call(
        join_kernel,
        (xs[0], back, ahead, keep, received, losses),
        [shape(NY, PACK + 8, LANES)] + [shape(rows, features)] * NZH,
    )
    packed = exchange(packed, "y")
    relay = turned(zs[3], "zh", -1)
    ahead = turned(zs[2], "zh", 1)
    (relay,) = call(add_kernel, (zs[1], relay), [shape(rows, features)])
    back = turned(relay, "zh", -1)
    (image_grad,) = call(image_grad_kernel, (image_emb, zs[0], back, ahead), [shape(rows, features)])
    text_grad, loss = call(
        text_grad_kernel,
        (text_emb, packed),
        [shape(rows, features), shape(1, 1)],
        out_specs=[VMEM, SMEM],
    )
    return loss.reshape(()), image_grad, text_grad


def solution(mesh):
    split = Mesh(mesh.devices.reshape(SIZES), AXES)
    return jax.shard_map(
        on_device,
        mesh=split,
        in_specs=(P(AXES, None), P(AXES, None)),
        out_specs=(P(), P(AXES, None), P(AXES, None)),
        check_vma=False,
    )
```

```python
import jax
import jax.numpy as jnp
from jax import lax
from jax.experimental import pallas as pl
from jax.experimental.pallas import tpu as pltpu
from jax.sharding import Mesh, PartitionSpec as P

LOGIT_MULT = 16.0
LOGIT_SHIFT = -10.0
EPSILON = 1e-06

AXES = ("y", "zl", "c", "zh", "x")
SIZES = (8, 2, 2, 4, 4)
NY, NZH, NX = 8, 4, 4
ROWS, FEATURES, LANES = 16, 1152, 128
COLS = FEATURES // LANES
PACK = COLS * ROWS
PAIRS = 8192
F32, BF16 = jnp.float32, jnp.bfloat16

VMEM = pl.BlockSpec(memory_space=pltpu.VMEM)
ANY = pl.BlockSpec(memory_space=pl.ANY)
SMEM = pl.BlockSpec(memory_space=pltpu.SMEM)
HBM = pl.BlockSpec(memory_space=pltpu.HBM)


def shape(*dims):
    return jax.ShapeDtypeStruct(dims, F32)


def call(kernel, ins, outs, in_specs=None, out_specs=None, flops=0, vmem=8, **kw):
    moved = 4 * sum(a.size for a in list(ins) + list(outs))
    return pl.pallas_call(
        kernel,
        out_shape=outs,
        in_specs=in_specs or [VMEM] * len(ins),
        out_specs=out_specs or [VMEM] * len(outs),
        cost_estimate=pl.CostEstimate(flops=flops, bytes_accessed=moved, transcendentals=0),
        compiler_params=pltpu.CompilerParams(vmem_limit_bytes=vmem * 2**20),
        **kw,
    )(*ins)


def exchange(values, axes):
    return lax.all_to_all(values, axes, 0, 0, tiled=True)


def turned(values, axis, step):
    count = lax.axis_size(axis)
    pairs = [(c * count + i, c * count + (i + (1 - 2 * c) * step) % count) for c in range(2) for i in range(count)]
    return lax.ppermute(values, ("c", axis), pairs)


def planes(values, step):
    pairs = []
    for c in range(2):
        for z in range(2 * NZH):
            to = (z + (1 - 2 * c) * step) % (2 * NZH)
            pairs.append((((z % 2) * 2 + c) * NZH + z // 2, ((to % 2) * 2 + c) * NZH + to // 2))
    return lax.ppermute(values, ("zl", "c", "zh"), pairs)


def other_core(values):
    return lax.ppermute(values, "c", [(0, 1), (1, 0)])


def ring_gather(values, axis):
    back = turned(values, axis, 1)
    ahead = turned(values, axis, -1)
    return values, back, ahead, turned(back, axis, 1)


def normalize(values):
    length = jnp.sqrt(jnp.sum(values * values, axis=1, keepdims=True) + EPSILON)
    return values / length, length


def project_back(unit, direction, length):
    inner = jnp.sum(unit * direction, axis=1, keepdims=True)
    return (direction - unit * inner) / length


def halves(values):
    high = values.astype(BF16)
    return high, (values - high.astype(F32)).astype(BF16)


def dot3(left, right, dims):
    def dot(a, b):
        return lax.dot_general(a, b, (dims, ((), ())), preferred_element_type=F32)

    return dot(left[1], right[0]) + dot(left[0], right[1]) + dot(left[0], right[0])


def normalize_kernel(image_hbm, text_hbm, image_out, text_out, image_ref, text_ref, sems):
    copies = [
        pltpu.make_async_copy(text_hbm, text_ref, sems.at[0]),
        pltpu.make_async_copy(image_hbm, image_ref, sems.at[1]),
    ]
    for copy in copies:
        copy.start()
    copies[0].wait()
    text_unit = normalize(text_ref[...])[0]
    for y in range(NY):
        text_out[pl.ds(y * ROWS, ROWS), :] = text_unit
    copies[1].wait()
    image_out[...] = normalize(image_ref[...])[0]


def spread_kernel(*refs):
    for x in range(NX):
        for k, part in enumerate(refs[:-1]):
            refs[-1][pl.ds((x * NZH + k) * ROWS, ROWS), :] = part[...]


def tie_kernel(*refs):
    pass


def in_turn(place, image_ref):
    rows = image_ref.shape[0] // NX
    starts = [pl.multiple_of(place[1 + k] * rows, rows) for k in range(NX)]
    return halves(jnp.concatenate([image_ref[pl.ds(start, rows), :] for start in starts], axis=0))


def tile_kernel(place, image_ref, a_ref, b_ref, c_ref, d_ref, other_out, a_out, b_out, loss_out, *x_outs):
    image = in_turn(place, image_ref)
    quarter = a_ref.shape[0]
    count = image_ref.shape[0]
    row = lax.broadcasted_iota(jnp.int32, (count, quarter), 0)
    column = lax.broadcasted_iota(jnp.int32, (count, quarter), 1) - place[0]
    matched = (row == column) & (row < ROWS)
    lower, upper = other_out.at[pl.ds(0, quarter), :], other_out.at[pl.ds(quarter, quarter), :]
    total = jnp.zeros((), F32)
    image_dir = None
    for ref, out in ((c_ref, lower), (d_ref, upper), (a_ref, a_out), (b_ref, b_out)):
        text = halves(ref[...])
        logits = LOGIT_MULT * dot3(image, text, ((1,), (1,))) + LOGIT_SHIFT
        if ref is a_ref:
            logits = jnp.where(matched, -logits, logits)
        small = jnp.exp(-jnp.abs(logits))
        total += jnp.sum(jnp.maximum(logits, 0.0) + jnp.log1p(small))
        slope = jnp.where(logits >= 0.0, 1.0, small) / (1.0 + small) * (LOGIT_MULT / PAIRS)
        if ref is a_ref:
            slope = jnp.where(matched, -slope, slope)
        slope = halves(slope)
        out[...] = dot3(slope, image, ((0,), (0,)))
        term = dot3(slope, text, ((1,), (0,)))
        image_dir = term if image_dir is None else image_dir + term
    rows = count // NX
    for k, out in enumerate(x_outs):
        out[...] = image_dir[k * rows : (k + 1) * rows]
    loss_out[...] = jnp.full(loss_out.shape, total)


def add_kernel(b_ref, received_ref, back_ref, relay_ref, losses_ref, send_out, back_out):
    quarter = b_ref.shape[0]
    send_out[...] = b_ref[...] + received_ref[pl.ds(quarter, quarter), :]
    back_out[...] = back_ref[...] + relay_ref[...]


def relay_kernel(left, right, out):
    out[...] = left[...] + right[...]


def join_kernel(x0, x1, x2, a_ref, core_ref, plane_ref, losses_ref, packed_out, *zs):
    for k, out in enumerate(zs):
        rows = pl.ds(k * ROWS, ROWS)
        out[...] = x0[rows, :] + (x1[rows, :] + x2[rows, :])
    loss = jnp.sum(losses_ref[:, 0:1])
    for y in range(NY):
        rows = pl.ds(y * ROWS, ROWS)
        for k in range(COLS):
            lanes = pl.ds(k * LANES, LANES)
            packed_out[y, pl.ds(k * ROWS, ROWS), :] = (
                a_ref[rows, lanes] + core_ref[rows, lanes] + plane_ref[rows, lanes]
            )
        packed_out[y, pl.ds(PACK, 8), :] = jnp.full((8, LANES), loss)


def image_grad_kernel(emb_ref, z0, z1, z2, out):
    unit, length = normalize(emb_ref[...])
    out[...] = project_back(unit, z0[...] + (z1[...] + z2[...]), length)


def text_grad_kernel(emb_ref, packed_ref, out, loss_out):
    unit, length = normalize(emb_ref[...])
    total = packed_ref[0]
    for y in range(1, NY):
        total = total + packed_ref[y]
    direction = jnp.concatenate([total[k * ROWS : (k + 1) * ROWS] for k in range(COLS)], axis=1)
    out[...] = project_back(unit, direction, length)
    loss_out[0, 0] = jnp.max(total[PACK:]) / PAIRS


def on_device(image_emb, text_emb):
    rows, features = image_emb.shape
    image_unit, text_tiled = call(
        normalize_kernel,
        (image_emb, text_emb),
        [shape(rows, features), shape(NY * rows, features)],
        in_specs=[HBM] * 2,
        scratch_shapes=[pltpu.VMEM((rows, features), F32)] * 2 + [pltpu.SemaphoreType.DMA((2,))],
    )
    text_a = exchange(text_tiled, "y")
    (image_tiled,) = call(spread_kernel, ring_gather(image_unit, "zh"), [shape(NX * NZH * rows, features)])
    (text_a,) = call(
        tie_kernel, (text_a, image_tiled), [shape(*text_a.shape)], [ANY] * 2, [ANY], input_output_aliases={0: 0}
    )
    image = exchange(image_tiled, "x")
    text_b = planes(text_a, -1)
    texts = (text_a, text_b, other_core(text_a), other_core(text_b))

    count, quarter = image.shape[0], text_a.shape[0]
    part = count // NX
    x, turn = lax.axis_index("x"), 1 - 2 * lax.axis_index("c")
    blocks = [x, (x - turn) % NX, (x + turn) % NX, (x + 2) % NX]
    place = jnp.stack([lax.axis_index("y") * rows, *blocks]).astype(jnp.int32)
    product = 2 * count * quarter * features * 3
    other, text_a, text_b, loss, *xs = call(
        tile_kernel,
        (place, image, *texts),
        [shape(2 * quarter, features)]
        + [shape(quarter, features)] * 2
        + [shape(64, LANES)]
        + [shape(part, features)] * NX,
        in_specs=[SMEM] + [VMEM] * 5,
        flops=12 * product,
        vmem=24,
    )
    received = other_core(other)
    relay = turned(xs[3], "x", -1)
    losses = exchange(loss, ("zl", "c", "zh", "x"))
    send, relay = call(
        add_kernel,
        (text_b, received, xs[1], relay, losses),
        [shape(quarter, features), shape(part, features)],
        in_specs=[VMEM] * 4 + [ANY],
    )
    plane = planes(send, 1)
    back = turned(relay, "x", -1)
    ahead = turned(xs[2], "x", 1)
    packed, *zs = call(
        join_kernel,
        (xs[0], back, ahead, text_a, received, plane, losses),
        [shape(NY, PACK + 8, LANES)] + [shape(rows, features)] * NZH,
    )
    packed = exchange(packed, "y")
    relay = turned(zs[3], "zh", -1)
    ahead = turned(zs[2], "zh", 1)
    (relay,) = call(relay_kernel, (zs[1], relay), [shape(rows, features)])
    back = turned(relay, "zh", -1)
    (image_grad,) = call(image_grad_kernel, (image_emb, zs[0], back, ahead), [shape(rows, features)])
    text_grad, loss = call(
        text_grad_kernel,
        (text_emb, packed),
        [shape(rows, features), shape(1, 1)],
        out_specs=[VMEM, SMEM],
    )
    return loss.reshape(()), image_grad, text_grad


def solution(mesh):
    split = Mesh(mesh.devices.reshape(SIZES), AXES)
    return jax.shard_map(
        on_device,
        mesh=split,
        in_specs=(P(AXES, None), P(AXES, None)),
        out_specs=(P(), P(AXES, None), P(AXES, None)),
        check_vma=False,
    )
```

```python
import jax
import jax.numpy as jnp
from jax import lax
from jax.experimental import pallas as pl
from jax.experimental.pallas import tpu as pltpu
from jax.sharding import Mesh, PartitionSpec as P

LOGIT_MULT = 16.0
LOGIT_SHIFT = -10.0
EPSILON = 1e-06

AXES = ("y", "zl", "c", "zh", "x")
SIZES = (8, 2, 2, 4, 4)
NY, NZH, NX = 8, 4, 4
ROWS, FEATURES, LANES = 16, 1152, 128
COLS = FEATURES // LANES
PACK = COLS * ROWS
PAIRS = 8192
F32, BF16 = jnp.float32, jnp.bfloat16

VMEM = pl.BlockSpec(memory_space=pltpu.VMEM)
ANY = pl.BlockSpec(memory_space=pl.ANY)
SMEM = pl.BlockSpec(memory_space=pltpu.SMEM)
HBM = pl.BlockSpec(memory_space=pltpu.HBM)


def shape(*dims):
    return jax.ShapeDtypeStruct(dims, F32)


def call(kernel, ins, outs, in_specs=None, out_specs=None, flops=0, vmem=8, **kw):
    moved = 4 * sum(a.size for a in list(ins) + list(outs))
    return pl.pallas_call(
        kernel,
        out_shape=outs,
        in_specs=in_specs or [VMEM] * len(ins),
        out_specs=out_specs or [VMEM] * len(outs),
        cost_estimate=pl.CostEstimate(flops=flops, bytes_accessed=moved, transcendentals=0),
        compiler_params=pltpu.CompilerParams(vmem_limit_bytes=vmem * 2**20),
        **kw,
    )(*ins)


def exchange(values, axes):
    return lax.all_to_all(values, axes, 0, 0, tiled=True)


def turned(values, axis, step):
    count = lax.axis_size(axis)
    pairs = [(c * count + i, c * count + (i + (1 - 2 * c) * step) % count) for c in range(2) for i in range(count)]
    return lax.ppermute(values, ("c", axis), pairs)


def planes(values, step):
    pairs = []
    for c in range(2):
        for z in range(2 * NZH):
            to = (z + (1 - 2 * c) * step) % (2 * NZH)
            pairs.append((((z % 2) * 2 + c) * NZH + z // 2, ((to % 2) * 2 + c) * NZH + to // 2))
    return lax.ppermute(values, ("zl", "c", "zh"), pairs)


def other_core(values):
    return lax.ppermute(values, "c", [(0, 1), (1, 0)])


def ring_gather(values, axis):
    back = turned(values, axis, 1)
    ahead = turned(values, axis, -1)
    return values, back, ahead, turned(back, axis, 1)


def normalize(values):
    length = jnp.sqrt(jnp.sum(values * values, axis=1, keepdims=True) + EPSILON)
    return values / length, length


def project_back(unit, direction, length):
    inner = jnp.sum(unit * direction, axis=1, keepdims=True)
    return (direction - unit * inner) / length


def halves(values):
    high = values.astype(BF16)
    return high, (values - high.astype(F32)).astype(BF16)


def dot3(left, right, dims):
    def dot(a, b):
        return lax.dot_general(a, b, (dims, ((), ())), preferred_element_type=F32)

    return dot(left[1], right[0]) + dot(left[0], right[1]) + dot(left[0], right[0])


def normalize_kernel(image_hbm, text_hbm, image_out, text_out, image_ref, text_ref, sems):
    copies = [
        pltpu.make_async_copy(text_hbm, text_ref, sems.at[0]),
        pltpu.make_async_copy(image_hbm, image_ref, sems.at[1]),
    ]
    for copy in copies:
        copy.start()
    copies[0].wait()
    text_unit = normalize(text_ref[...])[0]
    for y in range(NY):
        text_out[pl.ds(y * ROWS, ROWS), :] = text_unit
    copies[1].wait()
    image_out[...] = normalize(image_ref[...])[0]


def spread_kernel(*refs):
    for x in range(NX):
        for k, part in enumerate(refs[:-1]):
            refs[-1][pl.ds((x * NZH + k) * ROWS, ROWS), :] = part[...]


def tie_kernel(*refs):
    pass


def tile_kernel(place, image_hbm, a_hbm, b_hbm, c_hbm, d_hbm, other_out, a_out, b_out, *refs):
    x_outs, (image_ref, texts_ref, sems) = refs[:NX], refs[NX:]
    count, quarter = image_ref.shape[0], a_out.shape[0]
    rows = count // NX
    copies = []
    for k in range(NX):
        start = pl.multiple_of(place[1 + k] * rows, rows)
        copies.append((image_hbm.at[pl.ds(start, rows), :], image_ref.at[pl.ds(k * rows, rows), :]))
    for k, ref in enumerate((a_hbm, b_hbm, c_hbm, d_hbm)):
        copies.append((ref, texts_ref.at[k]))
    copies = [pltpu.make_async_copy(*ends, sems.at[k]) for k, ends in enumerate(copies)]
    for copy in copies:
        copy.start()
    for copy in copies[:NX]:
        copy.wait()
    image = halves(image_ref[...])
    row = lax.broadcasted_iota(jnp.int32, (count, quarter), 0)
    column = lax.broadcasted_iota(jnp.int32, (count, quarter), 1) - place[0]
    matched = (row == column) & (row < ROWS)
    lower, upper = other_out.at[pl.ds(0, quarter), :], other_out.at[pl.ds(quarter, quarter), :]
    total = jnp.zeros((), F32)
    image_dir = None
    for k, out in enumerate((a_out, b_out, lower, upper)):
        copies[NX + k].wait()
        text = halves(texts_ref[k])
        logits = LOGIT_MULT * dot3(image, text, ((1,), (1,))) + LOGIT_SHIFT
        if k == 0:
            logits = jnp.where(matched, -logits, logits)
        small = jnp.exp(-jnp.abs(logits))
        total += jnp.sum(jnp.maximum(logits, 0.0) + jnp.log1p(small))
        slope = jnp.where(logits >= 0.0, 1.0, small) / (1.0 + small) * (LOGIT_MULT / PAIRS)
        if k == 0:
            slope = jnp.where(matched, -slope, slope)
        slope = halves(slope)
        out[...] = dot3(slope, image, ((0,), (0,)))
        term = dot3(slope, text, ((1,), (0,)))
        image_dir = term if image_dir is None else image_dir + term
    for k, out in enumerate(x_outs):
        out[...] = image_dir[k * rows : (k + 1) * rows]
    other_out[pl.ds(2 * quarter, 8), :] = jnp.full((8, FEATURES), total)


def add_kernel(a_ref, b_ref, other_ref, received_ref, back_ref, relay_ref, keep_out, send_out, back_out, loss_out):
    quarter = b_ref.shape[0]
    keep_out[...] = a_ref[...] + received_ref[pl.ds(0, quarter), :]
    rows, lanes = pl.ds(2 * quarter, 8), pl.ds(0, LANES)
    loss = other_ref[rows, lanes] + received_ref[rows, lanes]
    for k in range(loss_out.shape[0] // 8):
        loss_out[pl.ds(8 * k, 8), :] = loss
    send_out[...] = b_ref[...] + received_ref[pl.ds(quarter, quarter), :]
    back_out[...] = back_ref[...] + relay_ref[...]


def relay_kernel(left, right, out):
    out[...] = left[...] + right[...]


def join_kernel(x0, x1, x2, keep_ref, plane_ref, losses_ref, packed_out, *zs):
    for k, out in enumerate(zs):
        rows = pl.ds(k * ROWS, ROWS)
        out[...] = x0[rows, :] + (x1[rows, :] + x2[rows, :])
    loss = jnp.sum(losses_ref[:, 0:1])
    for y in range(NY):
        rows = pl.ds(y * ROWS, ROWS)
        for k in range(COLS):
            lanes = pl.ds(k * LANES, LANES)
            packed_out[y, pl.ds(k * ROWS, ROWS), :] = keep_ref[rows, lanes] + plane_ref[rows, lanes]
        packed_out[y, pl.ds(PACK, 8), :] = jnp.full((8, LANES), loss)


def image_grad_kernel(emb_ref, z0, z1, z2, out):
    unit, length = normalize(emb_ref[...])
    out[...] = project_back(unit, z0[...] + (z1[...] + z2[...]), length)


def text_grad_kernel(emb_ref, packed_ref, out, loss_out):
    unit, length = normalize(emb_ref[...])
    total = packed_ref[0]
    for y in range(1, NY):
        total = total + packed_ref[y]
    direction = jnp.concatenate([total[k * ROWS : (k + 1) * ROWS] for k in range(COLS)], axis=1)
    out[...] = project_back(unit, direction, length)
    loss_out[0, 0] = jnp.max(total[PACK:]) / PAIRS


def on_device(image_emb, text_emb):
    rows, features = image_emb.shape
    image_unit, text_tiled = call(
        normalize_kernel,
        (image_emb, text_emb),
        [shape(rows, features), shape(NY * rows, features)],
        in_specs=[HBM] * 2,
        scratch_shapes=[pltpu.VMEM((rows, features), F32)] * 2 + [pltpu.SemaphoreType.DMA((2,))],
    )
    text_a = exchange(text_tiled, "y")
    (image_tiled,) = call(spread_kernel, ring_gather(image_unit, "zh"), [shape(NX * NZH * rows, features)])
    (text_a,) = call(
        tie_kernel, (text_a, image_tiled), [shape(*text_a.shape)], [ANY] * 2, [ANY], input_output_aliases={0: 0}
    )
    image = exchange(image_tiled, "x")
    text_b = planes(text_a, -1)
    texts = (text_a, text_b, other_core(text_a), other_core(text_b))

    count, quarter = image.shape[0], text_a.shape[0]
    part = count // NX
    x, turn = lax.axis_index("x"), 1 - 2 * lax.axis_index("c")
    blocks = [x, (x - turn) % NX, (x + turn) % NX, (x + 2) % NX]
    place = jnp.stack([lax.axis_index("y") * rows, *blocks]).astype(jnp.int32)
    product = 2 * count * quarter * features * 3
    other, text_a, text_b, *xs = call(
        tile_kernel,
        (place, image, *texts),
        [shape(2 * quarter + 8, features)] + [shape(quarter, features)] * 2 + [shape(part, features)] * NX,
        in_specs=[SMEM] + [ANY] * 5,
        scratch_shapes=[
            pltpu.VMEM((count, features), F32),
            pltpu.VMEM((4, quarter, features), F32),
            pltpu.SemaphoreType.DMA((NX + 4,)),
        ],
        flops=12 * product,
        vmem=24,
    )
    received = other_core(other)
    relay = turned(xs[3], "x", -1)
    keep, send, relay, loss = call(
        add_kernel,
        (text_a, text_b, other, received, xs[1], relay),
        [shape(quarter, features)] * 2 + [shape(part, features), shape(32, LANES)],
    )
    losses = exchange(loss, ("zl", "zh", "x"))
    plane = planes(send, 1)
    back = turned(relay, "x", -1)
    ahead = turned(xs[2], "x", 1)
    packed, *zs = call(
        join_kernel,
        (xs[0], back, ahead, keep, plane, losses),
        [shape(NY, PACK + 8, LANES)] + [shape(rows, features)] * NZH,
    )
    packed = exchange(packed, "y")
    relay = turned(zs[3], "zh", -1)
    ahead = turned(zs[2], "zh", 1)
    (relay,) = call(relay_kernel, (zs[1], relay), [shape(rows, features)])
    back = turned(relay, "zh", -1)
    (image_grad,) = call(image_grad_kernel, (image_emb, zs[0], back, ahead), [shape(rows, features)])
    text_grad, loss = call(
        text_grad_kernel,
        (text_emb, packed),
        [shape(rows, features), shape(1, 1)],
        out_specs=[VMEM, SMEM],
    )
    return loss.reshape(()), image_grad, text_grad


def solution(mesh):
    split = Mesh(mesh.devices.reshape(SIZES), AXES)
    return jax.shard_map(
        on_device,
        mesh=split,
        in_specs=(P(AXES, None), P(AXES, None)),
        out_specs=(P(), P(AXES, None), P(AXES, None)),
        check_vma=False,
    )
```

```python
import jax
import jax.numpy as jnp
from jax import lax
from jax.experimental import pallas as pl
from jax.experimental.pallas import tpu as pltpu
from jax.sharding import Mesh, PartitionSpec as P

LOGIT_MULT = 16.0
LOGIT_SHIFT = -10.0
EPSILON = 1e-06

AXES = ("y", "zl", "c", "zh", "x")
SIZES = (8, 2, 2, 4, 4)
NY, NZH, NX = 8, 4, 4
ROWS, FEATURES, LANES = 16, 1152, 128
COLS = FEATURES // LANES
PACK = COLS * ROWS
PAIRS = 8192
F32, BF16 = jnp.float32, jnp.bfloat16

VMEM = pl.BlockSpec(memory_space=pltpu.VMEM)
ANY = pl.BlockSpec(memory_space=pl.ANY)
SMEM = pl.BlockSpec(memory_space=pltpu.SMEM)
HBM = pl.BlockSpec(memory_space=pltpu.HBM)


def shape(*dims):
    return jax.ShapeDtypeStruct(dims, F32)


def call(kernel, ins, outs, in_specs=None, out_specs=None, flops=0, vmem=8, **kw):
    moved = 4 * sum(a.size for a in list(ins) + list(outs))
    return pl.pallas_call(
        kernel,
        out_shape=outs,
        in_specs=in_specs or [VMEM] * len(ins),
        out_specs=out_specs or [VMEM] * len(outs),
        cost_estimate=pl.CostEstimate(flops=flops, bytes_accessed=moved, transcendentals=0),
        compiler_params=pltpu.CompilerParams(vmem_limit_bytes=vmem * 2**20),
        **kw,
    )(*ins)


def exchange(values, axes):
    return lax.all_to_all(values, axes, 0, 0, tiled=True)


def turned(values, axis, step):
    count = lax.axis_size(axis)
    pairs = [(c * count + i, c * count + (i + (1 - 2 * c) * step) % count) for c in range(2) for i in range(count)]
    return lax.ppermute(values, ("c", axis), pairs)


def planes(values, step):
    pairs = []
    for c in range(2):
        for z in range(2 * NZH):
            to = (z + (1 - 2 * c) * step) % (2 * NZH)
            pairs.append((((z % 2) * 2 + c) * NZH + z // 2, ((to % 2) * 2 + c) * NZH + to // 2))
    return lax.ppermute(values, ("zl", "c", "zh"), pairs)


def other_core(values):
    return lax.ppermute(values, "c", [(0, 1), (1, 0)])


def ring_gather(values, axis):
    back = turned(values, axis, 1)
    ahead = turned(values, axis, -1)
    return values, back, ahead, turned(back, axis, 1)


def normalize(values):
    length = jnp.sqrt(jnp.sum(values * values, axis=1, keepdims=True) + EPSILON)
    return values / length, length


def project_back(unit, direction, length):
    inner = jnp.sum(unit * direction, axis=1, keepdims=True)
    return (direction - unit * inner) / length


def halves(values):
    high = values.astype(BF16)
    return high, (values - high.astype(F32)).astype(BF16)


def dot3(left, right, dims):
    def dot(a, b):
        return lax.dot_general(a, b, (dims, ((), ())), preferred_element_type=F32)

    return dot(left[1], right[0]) + dot(left[0], right[1]) + dot(left[0], right[0])


def normalize_kernel(image_hbm, text_hbm, image_out, text_out, image_ref, text_ref, sems):
    copies = [
        pltpu.make_async_copy(text_hbm, text_ref, sems.at[0]),
        pltpu.make_async_copy(image_hbm, image_ref, sems.at[1]),
    ]
    for copy in copies:
        copy.start()
    copies[0].wait()
    text_unit = normalize(text_ref[...])[0]
    for y in range(NY):
        text_out[pl.ds(y * ROWS, ROWS), :] = text_unit
    copies[1].wait()
    image_out[...] = normalize(image_ref[...])[0]


def spread_kernel(*refs):
    for x in range(NX):
        for k, part in enumerate(refs[:-1]):
            refs[-1][pl.ds((x * NZH + k) * ROWS, ROWS), :] = part[...]


def tie_kernel(*refs):
    pass


def in_turn(place, image_ref):
    rows = image_ref.shape[0] // NX
    starts = [pl.multiple_of(place[1 + k] * rows, rows) for k in range(NX)]
    return halves(jnp.concatenate([image_ref[pl.ds(start, rows), :] for start in starts], axis=0))


def tile_kernel(place, image_ref, a_ref, b_ref, c_ref, d_ref, slope_out, other_out):
    image = in_turn(place, image_ref)
    quarter = a_ref.shape[0]
    count = image_ref.shape[0]
    row = lax.broadcasted_iota(jnp.int32, (count, quarter), 0)
    column = lax.broadcasted_iota(jnp.int32, (count, quarter), 1) - place[0]
    matched = (row == column) & (row < ROWS)
    total = jnp.zeros((), F32)
    for k, ref in ((2, c_ref), (3, d_ref), (0, a_ref), (1, b_ref)):
        logits = LOGIT_MULT * dot3(image, halves(ref[...]), ((1,), (1,))) + LOGIT_SHIFT
        if k == 0:
            logits = jnp.where(matched, -logits, logits)
        small = jnp.exp(-jnp.abs(logits))
        total += jnp.sum(jnp.maximum(logits, 0.0) + jnp.log1p(small))
        slope = jnp.where(logits >= 0.0, 1.0, small) / (1.0 + small) * (LOGIT_MULT / PAIRS)
        if k == 0:
            slope = jnp.where(matched, -slope, slope)
        slope_out[:, pl.ds(k * quarter, quarter)] = slope
        if k >= 2:
            other_out[pl.ds((k - 2) * quarter, quarter), :] = dot3(halves(slope), image, ((0,), (0,)))
    other_out[pl.ds(2 * quarter, 8), :] = jnp.full((8, FEATURES), total)


def image_kernel(slope_ref, a_ref, b_ref, c_ref, d_ref, *outs):
    quarter = a_ref.shape[0]
    total = None
    for k, ref in enumerate((a_ref, b_ref, c_ref, d_ref)):
        slope = slope_ref[:, pl.ds(k * quarter, quarter)]
        term = dot3(halves(slope), halves(ref[...]), ((1,), (0,)))
        total = term if total is None else total + term
    rows = total.shape[0] // NX
    for k, out in enumerate(outs):
        out[...] = total[k * rows : (k + 1) * rows]


def text_kernel(place, slope_ref, image_ref, other_ref, received_ref, x0, keep_out, send_out):
    image = in_turn(place, image_ref)
    quarter = keep_out.shape[0] - 8
    last = pl.ds(2 * quarter, 8)
    loss = other_ref[last, :] + received_ref[last, :]
    for k, out in ((1, send_out), (0, keep_out)):
        rows = pl.ds(k * quarter, quarter)
        out[pl.ds(0, quarter), :] = dot3(halves(slope_ref[:, rows]), image, ((0,), (0,))) + received_ref[rows, :]
        out[pl.ds(quarter, 8), :] = loss


def relay_kernel(left, right, out):
    out[...] = left[...] + right[...]


def join_kernel(x0, x1, x2, keep_ref, plane_ref, packed_out, *zs):
    for k, out in enumerate(zs):
        rows = pl.ds(k * ROWS, ROWS)
        out[...] = x0[rows, :] + (x1[rows, :] + x2[rows, :])
    last, first = pl.ds(NY * ROWS, 8), pl.ds(0, LANES)
    loss = keep_ref[last, first] + plane_ref[last, first]
    for y in range(NY):
        rows = pl.ds(y * ROWS, ROWS)
        for k in range(COLS):
            lanes = pl.ds(k * LANES, LANES)
            packed_out[y, pl.ds(k * ROWS, ROWS), :] = keep_ref[rows, lanes] + plane_ref[rows, lanes]
        packed_out[y, pl.ds(PACK, 8), :] = loss


def loss_kernel(packed_ref, out):
    total = packed_ref[0, pl.ds(PACK, 8), :]
    for y in range(1, NY):
        total = total + packed_ref[y, pl.ds(PACK, 8), :]
    for k in range(out.shape[0] // 8):
        out[pl.ds(8 * k, 8), :] = total


def mean_kernel(losses_ref, out):
    out[0, 0] = jnp.sum(losses_ref[:, 0:1]) / PAIRS


def image_grad_kernel(emb_ref, z0, z1, z2, out):
    unit, length = normalize(emb_ref[...])
    out[...] = project_back(unit, z0[...] + (z1[...] + z2[...]), length)


def text_grad_kernel(emb_ref, packed_ref, out):
    unit, length = normalize(emb_ref[...])
    total = packed_ref[0]
    for y in range(1, NY):
        total = total + packed_ref[y]
    direction = jnp.concatenate([total[k * ROWS : (k + 1) * ROWS] for k in range(COLS)], axis=1)
    out[...] = project_back(unit, direction, length)


def on_device(image_emb, text_emb):
    rows, features = image_emb.shape
    image_unit, text_tiled = call(
        normalize_kernel,
        (image_emb, text_emb),
        [shape(rows, features), shape(NY * rows, features)],
        in_specs=[HBM] * 2,
        scratch_shapes=[pltpu.VMEM((rows, features), F32)] * 2 + [pltpu.SemaphoreType.DMA((2,))],
    )
    text_a = exchange(text_tiled, "y")
    (image_tiled,) = call(spread_kernel, ring_gather(image_unit, "zh"), [shape(NX * NZH * rows, features)])
    (text_a,) = call(
        tie_kernel, (text_a, image_tiled), [shape(*text_a.shape)], [ANY] * 2, [ANY], input_output_aliases={0: 0}
    )
    image = exchange(image_tiled, "x")
    text_b = planes(text_a, -1)
    texts = (text_a, text_b, other_core(text_a), other_core(text_b))

    count, quarter = image.shape[0], text_a.shape[0]
    part = count // NX
    x, turn = lax.axis_index("x"), 1 - 2 * lax.axis_index("c")
    blocks = [x, (x - turn) % NX, (x + turn) % NX, (x + 2) % NX]
    place = jnp.stack([lax.axis_index("y") * rows, *blocks]).astype(jnp.int32)
    product = 2 * count * quarter * features * 3
    slope, other = call(
        tile_kernel,
        (place, image, *texts),
        [shape(count, 4 * quarter), shape(2 * quarter + 8, features)],
        in_specs=[SMEM] + [VMEM] * 5,
        flops=6 * product,
        vmem=20,
    )
    received = other_core(other)
    xs = call(image_kernel, (slope, *texts), [shape(part, features)] * NX, flops=4 * product, vmem=20)
    relay = turned(xs[3], "x", -1)
    ahead = turned(xs[2], "x", 1)
    keep, send = call(
        text_kernel,
        (place, slope, image, other, received, xs[0]),
        [shape(quarter + 8, features)] * 2,
        in_specs=[SMEM] + [VMEM] * 4 + [ANY],
        flops=2 * product,
        vmem=20,
    )
    plane = planes(send, 1)
    (relay,) = call(relay_kernel, (xs[1], relay), [shape(part, features)])
    back = turned(relay, "x", -1)
    packed, *zs = call(
        join_kernel,
        (xs[0], back, ahead, keep, plane),
        [shape(NY, PACK + 8, LANES)] + [shape(rows, features)] * NZH,
    )
    packed = exchange(packed, "y")
    relay = turned(zs[3], "zh", -1)
    ahead = turned(zs[2], "zh", 1)
    (relay,) = call(relay_kernel, (zs[1], relay), [shape(rows, features)])
    back = turned(relay, "zh", -1)
    (image_grad,) = call(image_grad_kernel, (image_emb, zs[0], back, ahead), [shape(rows, features)])
    (loss,) = call(loss_kernel, (packed,), [shape(NZH * NX, LANES)])
    losses = exchange(loss, ("zh", "x"))
    (text_grad,) = call(text_grad_kernel, (text_emb, packed), [shape(rows, features)])
    (loss,) = call(mean_kernel, (losses,), [shape(1, 1)], out_specs=[SMEM])
    return loss.reshape(()), image_grad, text_grad


def solution(mesh):
    split = Mesh(mesh.devices.reshape(SIZES), AXES)
    return jax.shard_map(
        on_device,
        mesh=split,
        in_specs=(P(AXES, None), P(AXES, None)),
        out_specs=(P(), P(AXES, None), P(AXES, None)),
        check_vma=False,
    )
```

```python
import jax
import jax.numpy as jnp
from jax import lax
from jax.experimental import pallas as pl
from jax.experimental.pallas import tpu as pltpu
from jax.sharding import Mesh, PartitionSpec as P

LOGIT_MULT = 16.0
LOGIT_SHIFT = -10.0
EPSILON = 1e-06

AXES = ("y", "zl", "c", "zh", "x")
SIZES = (8, 2, 2, 4, 4)
NY, NZH, NX = 8, 4, 4
ROWS, FEATURES, LANES = 16, 1152, 128
COLS = FEATURES // LANES
PACK = COLS * ROWS
PAIRS = 8192
F32, BF16 = jnp.float32, jnp.bfloat16

VMEM = pl.BlockSpec(memory_space=pltpu.VMEM)
ANY = pl.BlockSpec(memory_space=pl.ANY)
SMEM = pl.BlockSpec(memory_space=pltpu.SMEM)
HBM = pl.BlockSpec(memory_space=pltpu.HBM)


def shape(*dims):
    return jax.ShapeDtypeStruct(dims, F32)


def call(kernel, ins, outs, in_specs=None, out_specs=None, flops=0, vmem=8, **kw):
    moved = 4 * sum(a.size for a in list(ins) + list(outs))
    return pl.pallas_call(
        kernel,
        out_shape=outs,
        in_specs=in_specs or [VMEM] * len(ins),
        out_specs=out_specs or [VMEM] * len(outs),
        cost_estimate=pl.CostEstimate(flops=flops, bytes_accessed=moved, transcendentals=0),
        compiler_params=pltpu.CompilerParams(vmem_limit_bytes=vmem * 2**20),
        **kw,
    )(*ins)


def exchange(values, axes):
    return lax.all_to_all(values, axes, 0, 0, tiled=True)


def turned(values, axis, step):
    count = lax.axis_size(axis)
    pairs = [(c * count + i, c * count + (i + (1 - 2 * c) * step) % count) for c in range(2) for i in range(count)]
    return lax.ppermute(values, ("c", axis), pairs)


def planes(values, step):
    pairs = []
    for c in range(2):
        for z in range(2 * NZH):
            to = (z + (1 - 2 * c) * step) % (2 * NZH)
            pairs.append((((z % 2) * 2 + c) * NZH + z // 2, ((to % 2) * 2 + c) * NZH + to // 2))
    return lax.ppermute(values, ("zl", "c", "zh"), pairs)


def other_core(values):
    return lax.ppermute(values, "c", [(0, 1), (1, 0)])


def normalize(values):
    length = jnp.sqrt(jnp.sum(values * values, axis=1, keepdims=True) + EPSILON)
    return values / length, length


def project_back(unit, direction, length):
    inner = jnp.sum(unit * direction, axis=1, keepdims=True)
    return (direction - unit * inner) / length


def halves(values):
    high = values.astype(BF16)
    return high, (values - high.astype(F32)).astype(BF16)


def dot3(left, right, dims):
    def dot(a, b):
        return lax.dot_general(a, b, (dims, ((), ())), preferred_element_type=F32)

    return dot(left[1], right[0]) + dot(left[0], right[1]) + dot(left[0], right[0])


def normalize_kernel(image_hbm, text_hbm, image_out, text_out, image_ref, text_ref, sems):
    copies = [
        pltpu.make_async_copy(text_hbm, text_ref, sems.at[0]),
        pltpu.make_async_copy(image_hbm, image_ref, sems.at[1]),
    ]
    for copy in copies:
        copy.start()
    copies[0].wait()
    text_unit = normalize(text_ref[...])[0]
    for y in range(NY):
        text_out[pl.ds(y * ROWS, ROWS), :] = text_unit
    copies[1].wait()
    image_out[...] = normalize(image_ref[...])[0]


def tie_kernel(*refs):
    pass


def tile_kernel(place, image_ref, a_ref, b_ref, c_ref, d_ref, slope_out, other_out):
    image = halves(image_ref[...])
    quarter = a_ref.shape[0]
    count = image_ref.shape[0]
    row = lax.broadcasted_iota(jnp.int32, (count, quarter), 0) - place[0]
    column = lax.broadcasted_iota(jnp.int32, (count, quarter), 1) - place[1]
    matched = (row == column) & (row >= 0) & (row < ROWS)
    total = jnp.zeros((), F32)
    for k, ref in ((2, c_ref), (3, d_ref), (0, a_ref), (1, b_ref)):
        logits = LOGIT_MULT * dot3(image, halves(ref[...]), ((1,), (1,))) + LOGIT_SHIFT
        if k == 0:
            logits = jnp.where(matched, -logits, logits)
        small = jnp.exp(-jnp.abs(logits))
        total += jnp.sum(jnp.maximum(logits, 0.0) + jnp.log1p(small))
        slope = jnp.where(logits >= 0.0, 1.0, small) / (1.0 + small) * (LOGIT_MULT / PAIRS)
        if k == 0:
            slope = jnp.where(matched, -slope, slope)
        slope_out[:, pl.ds(k * quarter, quarter)] = slope
        if k >= 2:
            other_out[pl.ds((k - 2) * quarter, quarter), :] = dot3(halves(slope), image, ((0,), (0,)))
    other_out[pl.ds(2 * quarter, 8), :] = jnp.full((8, FEATURES), total)


def image_kernel(slope_ref, a_ref, b_ref, c_ref, d_ref, out):
    quarter = a_ref.shape[0]
    total = None
    for k, ref in enumerate((a_ref, b_ref, c_ref, d_ref)):
        slope = slope_ref[:, pl.ds(k * quarter, quarter)]
        term = dot3(halves(slope), halves(ref[...]), ((1,), (0,)))
        total = term if total is None else total + term
    out[...] = total


def text_kernel(slope_ref, image_ref, other_ref, received_ref, image_sums, keep_out, send_out):
    image = halves(image_ref[...])
    quarter = keep_out.shape[0] - 8
    last = pl.ds(2 * quarter, 8)
    loss = other_ref[last, :] + received_ref[last, :]
    for k, out in ((1, send_out), (0, keep_out)):
        rows = pl.ds(k * quarter, quarter)
        out[pl.ds(0, quarter), :] = dot3(halves(slope_ref[:, rows]), image, ((0,), (0,))) + received_ref[rows, :]
        out[pl.ds(quarter, 8), :] = loss


def relay_kernel(left, right, out):
    out[...] = left[...] + right[...]


def split_kernel(place, image_ref, *outs):
    for k, out in enumerate(outs):
        out[...] = image_ref[pl.ds(pl.multiple_of(place[2 + k] * ROWS, ROWS), ROWS), :]


def pack_kernel(keep_ref, plane_ref, packed_out):
    last, first = pl.ds(NY * ROWS, 8), pl.ds(0, LANES)
    loss = keep_ref[last, first] + plane_ref[last, first]
    for y in range(NY):
        rows = pl.ds(y * ROWS, ROWS)
        for k in range(COLS):
            lanes = pl.ds(k * LANES, LANES)
            packed_out[y, pl.ds(k * ROWS, ROWS), :] = keep_ref[rows, lanes] + plane_ref[rows, lanes]
        packed_out[y, pl.ds(PACK, 8), :] = loss


def loss_kernel(packed_ref, out):
    total = packed_ref[0, pl.ds(PACK, 8), :]
    for y in range(1, NY):
        total = total + packed_ref[y, pl.ds(PACK, 8), :]
    for k in range(out.shape[0] // 8):
        out[pl.ds(8 * k, 8), :] = total


def mean_kernel(losses_ref, out):
    out[0, 0] = jnp.sum(losses_ref[:, 0:1]) / PAIRS


def image_grad_kernel(emb_ref, z0, z1, z2, out):
    unit, length = normalize(emb_ref[...])
    out[...] = project_back(unit, z0[...] + (z1[...] + z2[...]), length)


def text_grad_kernel(emb_ref, packed_ref, out):
    unit, length = normalize(emb_ref[...])
    total = packed_ref[0]
    for y in range(1, NY):
        total = total + packed_ref[y]
    direction = jnp.concatenate([total[k * ROWS : (k + 1) * ROWS] for k in range(COLS)], axis=1)
    out[...] = project_back(unit, direction, length)


def on_device(image_emb, text_emb):
    rows, features = image_emb.shape
    image_unit, text_tiled = call(
        normalize_kernel,
        (image_emb, text_emb),
        [shape(rows, features), shape(NY * rows, features)],
        in_specs=[HBM] * 2,
        scratch_shapes=[pltpu.VMEM((rows, features), F32)] * 2 + [pltpu.SemaphoreType.DMA((2,))],
    )
    text_a = exchange(text_tiled, "y")
    image_z = lax.all_gather(image_unit, "zh", axis=0, tiled=True)
    image = lax.all_gather(image_z, "x", axis=0, tiled=True)
    (text_a,) = call(
        tie_kernel, (text_a, image_z), [shape(*text_a.shape)], [ANY] * 2, [ANY], input_output_aliases={0: 0}
    )
    text_b = planes(text_a, -1)
    texts = (text_a, text_b, other_core(text_a), other_core(text_b))

    count, quarter = image.shape[0], text_a.shape[0]
    zh, turn = lax.axis_index("zh"), 1 - 2 * lax.axis_index("c")
    blocks = [zh, (zh - turn) % NZH, (zh + turn) % NZH, (zh + 2) % NZH]
    own = (lax.axis_index("x") * NZH + zh) * rows
    place = jnp.stack([own, lax.axis_index("y") * rows, *blocks]).astype(jnp.int32)
    product = 2 * count * quarter * features * 3
    slope, other = call(
        tile_kernel,
        (place, image, *texts),
        [shape(count, 4 * quarter), shape(2 * quarter + 8, features)],
        in_specs=[SMEM] + [VMEM] * 5,
        flops=6 * product,
        vmem=20,
    )
    received = other_core(other)
    (image_sums,) = call(image_kernel, (slope, *texts), [shape(count, features)], flops=4 * product, vmem=20)
    image_x = lax.psum_scatter(image_sums, "x", scatter_dimension=0, tiled=True)
    keep, send = call(
        text_kernel,
        (slope, image, other, received, image_sums),
        [shape(quarter + 8, features)] * 2,
        in_specs=[VMEM] * 4 + [ANY],
        flops=2 * product,
        vmem=20,
    )
    plane = planes(send, 1)
    (packed,) = call(pack_kernel, (keep, plane), [shape(NY, PACK + 8, LANES)])
    packed = exchange(packed, "y")
    zs = call(split_kernel, (place, image_x), [shape(rows, features)] * NZH, in_specs=[SMEM, VMEM])
    relay = turned(zs[3], "zh", -1)
    ahead = turned(zs[2], "zh", 1)
    (relay,) = call(relay_kernel, (zs[1], relay), [shape(rows, features)])
    back = turned(relay, "zh", -1)
    (image_grad,) = call(image_grad_kernel, (image_emb, zs[0], back, ahead), [shape(rows, features)])
    (loss,) = call(loss_kernel, (packed,), [shape(NZH * NX, LANES)])
    losses = exchange(loss, ("zh", "x"))
    (text_grad,) = call(text_grad_kernel, (text_emb, packed), [shape(rows, features)])
    (loss,) = call(mean_kernel, (losses,), [shape(1, 1)], out_specs=[SMEM])
    return loss.reshape(()), image_grad, text_grad


def solution(mesh):
    split = Mesh(mesh.devices.reshape(SIZES), AXES)
    return jax.shard_map(
        on_device,
        mesh=split,
        in_specs=(P(AXES, None), P(AXES, None)),
        out_specs=(P(), P(AXES, None), P(AXES, None)),
        check_vma=False,
    )
```

```python
import jax
import jax.numpy as jnp
from jax import lax
from jax.experimental import pallas as pl
from jax.experimental.pallas import tpu as pltpu
from jax.sharding import Mesh, PartitionSpec as P

LOGIT_MULT = 16.0
LOGIT_SHIFT = -10.0
EPSILON = 1e-06

AXES = ("y", "zl", "c", "zh", "x")
SIZES = (8, 2, 2, 4, 4)
NY, NZH, NX = 8, 4, 4
ROWS, FEATURES, LANES = 16, 1152, 128
COLS = FEATURES // LANES
PACK = COLS * ROWS
PAIRS = 8192
F32, BF16 = jnp.float32, jnp.bfloat16

VMEM = pl.BlockSpec(memory_space=pltpu.VMEM)
ANY = pl.BlockSpec(memory_space=pl.ANY)
SMEM = pl.BlockSpec(memory_space=pltpu.SMEM)
HBM = pl.BlockSpec(memory_space=pltpu.HBM)


def shape(*dims):
    return jax.ShapeDtypeStruct(dims, F32)


def call(kernel, ins, outs, in_specs=None, out_specs=None, flops=0, vmem=8, **kw):
    moved = 4 * sum(a.size for a in list(ins) + list(outs))
    return pl.pallas_call(
        kernel,
        out_shape=outs,
        in_specs=in_specs or [VMEM] * len(ins),
        out_specs=out_specs or [VMEM] * len(outs),
        cost_estimate=pl.CostEstimate(flops=flops, bytes_accessed=moved, transcendentals=0),
        compiler_params=pltpu.CompilerParams(vmem_limit_bytes=vmem * 2**20),
        **kw,
    )(*ins)


def exchange(values, axes):
    return lax.all_to_all(values, axes, 0, 0, tiled=True)


def turned(values, axis, step):
    count = lax.axis_size(axis)
    pairs = [(c * count + i, c * count + (i + (1 - 2 * c) * step) % count) for c in range(2) for i in range(count)]
    return lax.ppermute(values, ("c", axis), pairs)


def planes(values, step):
    pairs = []
    for c in range(2):
        for z in range(2 * NZH):
            to = (z + (1 - 2 * c) * step) % (2 * NZH)
            pairs.append((((z % 2) * 2 + c) * NZH + z // 2, ((to % 2) * 2 + c) * NZH + to // 2))
    return lax.ppermute(values, ("zl", "c", "zh"), pairs)


def other_core(values):
    return lax.ppermute(values, "c", [(0, 1), (1, 0)])


def normalize(values):
    length = jnp.sqrt(jnp.sum(values * values, axis=1, keepdims=True) + EPSILON)
    return values / length, length


def project_back(unit, direction, length):
    inner = jnp.sum(unit * direction, axis=1, keepdims=True)
    return (direction - unit * inner) / length


def halves(values):
    high = values.astype(BF16)
    return high, (values - high.astype(F32)).astype(BF16)


def dot3(left, right, dims):
    def dot(a, b):
        return lax.dot_general(a, b, (dims, ((), ())), preferred_element_type=F32)

    return dot(left[1], right[0]) + dot(left[0], right[1]) + dot(left[0], right[0])


def image_unit_kernel(image_ref, out):
    unit = normalize(image_ref[...])[0]
    for x in range(NX):
        out[pl.ds(x * NZH * ROWS, NZH * ROWS), :] = unit


def text_unit_kernel(text_ref, image_units, out):
    out[...] = normalize(text_ref[...])[0]


def in_turn(place, image_ref):
    rows = image_ref.shape[0] // NX
    starts = [pl.multiple_of(place[2 + k] * rows, rows) for k in range(NX)]
    return halves(jnp.concatenate([image_ref[pl.ds(start, rows), :] for start in starts], axis=0))


def tile_kernel(place, image_ref, a_ref, b_ref, c_ref, d_ref, slope_out, other_out):
    image = in_turn(place, image_ref)
    quarter = a_ref.shape[0]
    count = image_ref.shape[0]
    row = lax.broadcasted_iota(jnp.int32, (count, quarter), 0) - place[0]
    column = lax.broadcasted_iota(jnp.int32, (count, quarter), 1) - place[1]
    matched = (row == column) & (row >= 0) & (row < ROWS)
    total = jnp.zeros((), F32)
    for k, ref in ((2, c_ref), (3, d_ref), (0, a_ref), (1, b_ref)):
        logits = LOGIT_MULT * dot3(image, halves(ref[...]), ((1,), (1,))) + LOGIT_SHIFT
        if k == 0:
            logits = jnp.where(matched, -logits, logits)
        small = jnp.exp(-jnp.abs(logits))
        total += jnp.sum(jnp.maximum(logits, 0.0) + jnp.log1p(small))
        slope = jnp.where(logits >= 0.0, 1.0, small) / (1.0 + small) * (LOGIT_MULT / PAIRS)
        if k == 0:
            slope = jnp.where(matched, -slope, slope)
        slope_out[:, pl.ds(k * quarter, quarter)] = slope
        if k >= 2:
            other_out[pl.ds((k - 2) * quarter, quarter), :] = dot3(halves(slope), image, ((0,), (0,)))
    other_out[pl.ds(2 * quarter, 8), :] = jnp.full((8, FEATURES), total)


def image_kernel(slope_ref, a_ref, b_ref, c_ref, d_ref, *outs):
    quarter = a_ref.shape[0]
    total = None
    for k, ref in enumerate((a_ref, b_ref, c_ref, d_ref)):
        slope = slope_ref[:, pl.ds(k * quarter, quarter)]
        term = dot3(halves(slope), halves(ref[...]), ((1,), (0,)))
        total = term if total is None else total + term
    rows = total.shape[0] // NX
    for k, out in enumerate(outs):
        out[...] = total[k * rows : (k + 1) * rows]


def text_kernel(place, slope_ref, image_ref, other_ref, received_ref, x0, keep_out, send_out):
    image = in_turn(place, image_ref)
    quarter = keep_out.shape[0] - 8
    last = pl.ds(2 * quarter, 8)
    loss = other_ref[last, :] + received_ref[last, :]
    for k, out in ((1, send_out), (0, keep_out)):
        rows = pl.ds(k * quarter, quarter)
        out[pl.ds(0, quarter), :] = dot3(halves(slope_ref[:, rows]), image, ((0,), (0,))) + received_ref[rows, :]
        out[pl.ds(quarter, 8), :] = loss


def relay_kernel(left, right, out):
    out[...] = left[...] + right[...]


def split_kernel(place, x0, x1, x2, *outs):
    for k, out in enumerate(outs):
        rows = pl.ds(pl.multiple_of(place[2 + NX + k] * ROWS, ROWS), ROWS)
        out[...] = x0[rows, :] + (x1[rows, :] + x2[rows, :])


def pack_kernel(keep_ref, plane_ref, relay_ref, ahead_ref, packed_out):
    last, first = pl.ds(NY * ROWS, 8), pl.ds(0, LANES)
    loss = keep_ref[last, first] + plane_ref[last, first]
    for y in range(NY):
        rows = pl.ds(y * ROWS, ROWS)
        for k in range(COLS):
            lanes = pl.ds(k * LANES, LANES)
            packed_out[y, pl.ds(k * ROWS, ROWS), :] = keep_ref[rows, lanes] + plane_ref[rows, lanes]
        packed_out[y, pl.ds(PACK, 8), :] = loss


def loss_kernel(packed_ref, out):
    total = packed_ref[0, pl.ds(PACK, 8), :]
    for y in range(1, NY):
        total = total + packed_ref[y, pl.ds(PACK, 8), :]
    for k in range(out.shape[0] // 8):
        out[pl.ds(8 * k, 8), :] = total


def mean_kernel(losses_ref, out):
    out[0, 0] = jnp.sum(losses_ref[:, 0:1]) / PAIRS


def image_grad_kernel(emb_ref, z0, z1, z2, out):
    unit, length = normalize(emb_ref[...])
    out[...] = project_back(unit, z0[...] + (z1[...] + z2[...]), length)


def text_grad_kernel(emb_ref, packed_ref, out):
    unit, length = normalize(emb_ref[...])
    total = packed_ref[0]
    for y in range(1, NY):
        total = total + packed_ref[y]
    direction = jnp.concatenate([total[k * ROWS : (k + 1) * ROWS] for k in range(COLS)], axis=1)
    out[...] = project_back(unit, direction, length)


def on_device(image_emb, text_emb):
    rows, features = image_emb.shape
    text_y = exchange(jnp.tile(text_emb, (NY, 1)), "y")
    image_z = lax.all_gather(image_emb, "zh", axis=0, tiled=True)
    (image_tiled,) = call(image_unit_kernel, (image_z,), [shape(NX * NZH * rows, features)])
    (text_a,) = call(
        text_unit_kernel, (text_y, image_tiled), [shape(*text_y.shape)], in_specs=[VMEM, ANY]
    )
    image = exchange(image_tiled, "x")
    text_b = planes(text_a, -1)
    texts = (text_a, text_b, other_core(text_a), other_core(text_b))

    count, quarter = image.shape[0], text_a.shape[0]
    part = count // NX
    x, zh, turn = lax.axis_index("x"), lax.axis_index("zh"), 1 - 2 * lax.axis_index("c")
    blocks = [(at + step) % NX for at in (x, zh) for step in (0, -turn, turn, 2)]
    place = jnp.stack([zh * rows, lax.axis_index("y") * rows, *blocks]).astype(jnp.int32)
    product = 2 * count * quarter * features * 3
    slope, other = call(
        tile_kernel,
        (place, image, *texts),
        [shape(count, 4 * quarter), shape(2 * quarter + 8, features)],
        in_specs=[SMEM] + [VMEM] * 5,
        flops=6 * product,
        vmem=20,
    )
    received = other_core(other)
    xs = call(image_kernel, (slope, *texts), [shape(part, features)] * NX, flops=4 * product, vmem=20)
    relay = turned(xs[3], "x", -1)
    ahead = turned(xs[2], "x", 1)
    keep, send = call(
        text_kernel,
        (place, slope, image, other, received, xs[0]),
        [shape(quarter + 8, features)] * 2,
        in_specs=[SMEM] + [VMEM] * 4 + [ANY],
        flops=2 * product,
        vmem=20,
    )
    plane = planes(send, 1)
    (relay,) = call(relay_kernel, (xs[1], relay), [shape(part, features)])
    back = turned(relay, "x", -1)
    (packed,) = call(
        pack_kernel,
        (keep, plane, relay, ahead),
        [shape(NY, PACK + 8, LANES)],
        in_specs=[VMEM] * 2 + [ANY] * 2,
    )
    zs = call(
        split_kernel,
        (place, xs[0], back, ahead),
        [shape(rows, features)] * NZH,
        in_specs=[SMEM] + [VMEM] * 3,
    )
    packed = exchange(packed, "y")
    relay = turned(zs[3], "zh", -1)
    ahead = turned(zs[2], "zh", 1)
    (relay,) = call(relay_kernel, (zs[1], relay), [shape(rows, features)])
    back = turned(relay, "zh", -1)
    (image_grad,) = call(image_grad_kernel, (image_emb, zs[0], back, ahead), [shape(rows, features)])
    (loss,) = call(loss_kernel, (packed,), [shape(NZH * NX, LANES)])
    losses = exchange(loss, ("zh", "x"))
    (text_grad,) = call(text_grad_kernel, (text_emb, packed), [shape(rows, features)])
    (loss,) = call(mean_kernel, (losses,), [shape(1, 1)], out_specs=[SMEM])
    return loss.reshape(()), image_grad, text_grad


def solution(mesh):
    split = Mesh(mesh.devices.reshape(SIZES), AXES)
    return jax.shard_map(
        on_device,
        mesh=split,
        in_specs=(P(AXES, None), P(AXES, None)),
        out_specs=(P(), P(AXES, None), P(AXES, None)),
        check_vma=False,
    )
```

```python
import jax
import jax.numpy as jnp
from jax import lax
from jax.experimental import pallas as pl
from jax.experimental.pallas import tpu as pltpu
from jax.sharding import Mesh, PartitionSpec as P

LOGIT_MULT = 16.0
LOGIT_SHIFT = -10.0
EPSILON = 1e-06

AXES = ("y", "zl", "c", "zh", "x")
SIZES = (8, 2, 2, 4, 4)
NY, NZH, NX = 8, 4, 4
ROWS, FEATURES, LANES = 16, 1152, 128
COLS = FEATURES // LANES
PACK = COLS * ROWS
PAIRS = 8192
F32, BF16 = jnp.float32, jnp.bfloat16

VMEM = pl.BlockSpec(memory_space=pltpu.VMEM)
ANY = pl.BlockSpec(memory_space=pl.ANY)
SMEM = pl.BlockSpec(memory_space=pltpu.SMEM)
HBM = pl.BlockSpec(memory_space=pltpu.HBM)


def shape(*dims):
    return jax.ShapeDtypeStruct(dims, F32)


def call(kernel, ins, outs, in_specs=None, out_specs=None, flops=0, vmem=8, **kw):
    moved = 4 * sum(a.size for a in list(ins) + list(outs))
    return pl.pallas_call(
        kernel,
        out_shape=outs,
        in_specs=in_specs or [VMEM] * len(ins),
        out_specs=out_specs or [VMEM] * len(outs),
        cost_estimate=pl.CostEstimate(flops=flops, bytes_accessed=moved, transcendentals=0),
        compiler_params=pltpu.CompilerParams(vmem_limit_bytes=vmem * 2**20),
        **kw,
    )(*ins)


def exchange(values, axes):
    return lax.all_to_all(values, axes, 0, 0, tiled=True)


def turned(values, axis, step):
    count = lax.axis_size(axis)
    pairs = [(c * count + i, c * count + (i + (1 - 2 * c) * step) % count) for c in range(2) for i in range(count)]
    return lax.ppermute(values, ("c", axis), pairs)


def planes(values, step):
    pairs = []
    for c in range(2):
        for z in range(2 * NZH):
            to = (z + (1 - 2 * c) * step) % (2 * NZH)
            pairs.append((((z % 2) * 2 + c) * NZH + z // 2, ((to % 2) * 2 + c) * NZH + to // 2))
    return lax.ppermute(values, ("zl", "c", "zh"), pairs)


def other_core(values):
    return lax.ppermute(values, "c", [(0, 1), (1, 0)])


def normalize(values):
    length = jnp.sqrt(jnp.sum(values * values, axis=1, keepdims=True) + EPSILON)
    return values / length, length


def project_back(unit, direction, length):
    inner = jnp.sum(unit * direction, axis=1, keepdims=True)
    return (direction - unit * inner) / length


def halves(values):
    high = values.astype(BF16)
    return high, (values - high.astype(F32)).astype(BF16)


def dot3(left, right, dims):
    def dot(a, b):
        return lax.dot_general(a, b, (dims, ((), ())), preferred_element_type=F32)

    return dot(left[1], right[0]) + dot(left[0], right[1]) + dot(left[0], right[0])


def tie_kernel(*refs):
    pass


def after(values, other):
    out = [shape(*values.shape)]
    return call(tie_kernel, (values, other), out, [ANY] * 2, [ANY], input_output_aliases={0: 0})[0]


def image_unit_kernel(image_ref, out):
    unit = normalize(image_ref[...])[0]
    for x in range(NX):
        out[pl.ds(x * NZH * ROWS, NZH * ROWS), :] = unit


def text_unit_kernel(text_ref, image_units, out):
    out[...] = normalize(text_ref[...])[0]


def in_turn(place, image_ref):
    rows = image_ref.shape[0] // NX
    starts = [pl.multiple_of(place[2 + k] * rows, rows) for k in range(NX)]
    return halves(jnp.concatenate([image_ref[pl.ds(start, rows), :] for start in starts], axis=0))


def tile_kernel(place, image_ref, a_ref, b_ref, c_ref, d_ref, slope_out, other_out, loss_out):
    image = in_turn(place, image_ref)
    quarter = a_ref.shape[0]
    count = image_ref.shape[0]
    row = lax.broadcasted_iota(jnp.int32, (count, quarter), 0) - place[0]
    column = lax.broadcasted_iota(jnp.int32, (count, quarter), 1) - place[1]
    matched = (row == column) & (row >= 0) & (row < ROWS)
    total = jnp.zeros((), F32)
    for k, ref in ((2, c_ref), (3, d_ref), (0, a_ref), (1, b_ref)):
        logits = LOGIT_MULT * dot3(image, halves(ref[...]), ((1,), (1,))) + LOGIT_SHIFT
        if k == 0:
            logits = jnp.where(matched, -logits, logits)
        small = jnp.exp(-jnp.abs(logits))
        total += jnp.sum(jnp.maximum(logits, 0.0) + jnp.log1p(small))
        slope = jnp.where(logits >= 0.0, 1.0, small) / (1.0 + small) * (LOGIT_MULT / PAIRS)
        if k == 0:
            slope = jnp.where(matched, -slope, slope)
        slope_out[:, pl.ds(k * quarter, quarter)] = slope
        if k >= 2:
            other_out[pl.ds((k - 2) * quarter, quarter), :] = dot3(halves(slope), image, ((0,), (0,)))
    loss_out[...] = jnp.full(loss_out.shape, total)


def image_kernel(slope_ref, a_ref, b_ref, c_ref, d_ref, *outs):
    quarter = a_ref.shape[0]
    total = None
    for k, ref in enumerate((a_ref, b_ref, c_ref, d_ref)):
        slope = slope_ref[:, pl.ds(k * quarter, quarter)]
        term = dot3(halves(slope), halves(ref[...]), ((1,), (0,)))
        total = term if total is None else total + term
    rows = total.shape[0] // NX
    for k, out in enumerate(outs):
        out[...] = total[k * rows : (k + 1) * rows]


def text_kernel(place, slope_ref, image_ref, received_ref, x0, loss_ref, keep_out, send_out):
    image = in_turn(place, image_ref)
    quarter = keep_out.shape[0]
    for k, out in ((1, send_out), (0, keep_out)):
        rows = pl.ds(k * quarter, quarter)
        out[...] = dot3(halves(slope_ref[:, rows]), image, ((0,), (0,))) + received_ref[rows, :]


def relay_kernel(left, right, out):
    out[...] = left[...] + right[...]


def split_kernel(place, x0, x1, x2, *outs):
    for k, out in enumerate(outs):
        rows = pl.ds(pl.multiple_of(place[2 + NX + k] * ROWS, ROWS), ROWS)
        out[...] = x0[rows, :] + (x1[rows, :] + x2[rows, :])


def pack_kernel(keep_ref, plane_ref, loss_ref, relay_ref, ahead_ref, packed_out):
    for y in range(NY):
        rows = pl.ds(y * ROWS, ROWS)
        for k in range(COLS):
            lanes = pl.ds(k * LANES, LANES)
            packed_out[y, pl.ds(k * ROWS, ROWS), :] = keep_ref[rows, lanes] + plane_ref[rows, lanes]
        packed_out[y, pl.ds(PACK, 8), :] = loss_ref[...]


def image_grad_kernel(emb_ref, z0, z1, z2, out):
    unit, length = normalize(emb_ref[...])
    out[...] = project_back(unit, z0[...] + (z1[...] + z2[...]), length)


def text_grad_kernel(emb_ref, packed_ref, out, loss_out):
    unit, length = normalize(emb_ref[...])
    total = packed_ref[0]
    for y in range(1, NY):
        total = total + packed_ref[y]
    direction = jnp.concatenate([total[k * ROWS : (k + 1) * ROWS] for k in range(COLS)], axis=1)
    out[...] = project_back(unit, direction, length)
    loss_out[0, 0] = jnp.max(total[PACK:]) / PAIRS


def on_device(image_emb, text_emb):
    rows, features = image_emb.shape
    text_y = exchange(jnp.tile(text_emb, (NY, 1)), "y")
    image_z = lax.all_gather(image_emb, "zh", axis=0, tiled=True)
    (image_tiled,) = call(image_unit_kernel, (image_z,), [shape(NX * NZH * rows, features)])
    (text_a,) = call(
        text_unit_kernel, (text_y, image_tiled), [shape(*text_y.shape)], in_specs=[VMEM, ANY]
    )
    image = exchange(image_tiled, "x")
    text_b = planes(text_a, -1)
    texts = (text_a, text_b, other_core(text_a), other_core(text_b))

    count, quarter = image.shape[0], text_a.shape[0]
    part = count // NX
    x, zh, turn = lax.axis_index("x"), lax.axis_index("zh"), 1 - 2 * lax.axis_index("c")
    blocks = [(at + step) % NX for at in (x, zh) for step in (0, -turn, turn, 2)]
    place = jnp.stack([zh * rows, lax.axis_index("y") * rows, *blocks]).astype(jnp.int32)
    product = 2 * count * quarter * features * 3
    slope, other, loss = call(
        tile_kernel,
        (place, image, *texts),
        [shape(count, 4 * quarter), shape(2 * quarter, features), shape(8, LANES)],
        in_specs=[SMEM] + [VMEM] * 5,
        flops=6 * product,
        vmem=20,
    )
    sums = [loss]
    for axis, step in (("zl", 1), ("zh", 1), ("zh", 2), ("x", 1), ("x", 2), ("c", 1)):
        pairs = [(i, i ^ step) for i in range(lax.axis_size(axis))]
        sums.append(sums[-1] + lax.ppermute(sums[-1], axis, pairs))
    received = other_core(other)
    xs = call(image_kernel, (slope, *texts), [shape(part, features)] * NX, flops=4 * product, vmem=20)
    relay = turned(after(xs[3], sums[2]), "x", -1)
    ahead = turned(after(xs[2], sums[3]), "x", 1)
    keep, send = call(
        text_kernel,
        (place, slope, image, received, xs[0], sums[1]),
        [shape(quarter, features)] * 2,
        in_specs=[SMEM] + [VMEM] * 3 + [ANY] * 2,
        flops=2 * product,
        vmem=20,
    )
    plane = planes(send, 1)
    (relay,) = call(relay_kernel, (xs[1], after(relay, sums[4])), [shape(part, features)])
    back = turned(relay, "x", -1)
    (packed,) = call(
        pack_kernel,
        (keep, plane, sums[-1], relay, ahead),
        [shape(NY, PACK + 8, LANES)],
        in_specs=[VMEM] * 3 + [ANY] * 2,
    )
    zs = call(
        split_kernel,
        (place, xs[0], back, ahead),
        [shape(rows, features)] * NZH,
        in_specs=[SMEM] + [VMEM] * 3,
    )
    packed = exchange(packed, "y")
    relay = turned(zs[3], "zh", -1)
    ahead = turned(zs[2], "zh", 1)
    (relay,) = call(relay_kernel, (zs[1], relay), [shape(rows, features)])
    back = turned(relay, "zh", -1)
    (image_grad,) = call(image_grad_kernel, (image_emb, zs[0], back, ahead), [shape(rows, features)])
    text_grad, loss = call(
        text_grad_kernel,
        (text_emb, packed),
        [shape(rows, features), shape(1, 1)],
        out_specs=[VMEM, SMEM],
    )
    return loss.reshape(()), image_grad, text_grad


def solution(mesh):
    split = Mesh(mesh.devices.reshape(SIZES), AXES)
    return jax.shard_map(
        on_device,
        mesh=split,
        in_specs=(P(AXES, None), P(AXES, None)),
        out_specs=(P(), P(AXES, None), P(AXES, None)),
        check_vma=False,
    )
```

```python
import jax
import jax.numpy as jnp
from jax import lax
from jax.experimental import pallas as pl
from jax.experimental.pallas import tpu as pltpu
from jax.sharding import Mesh, PartitionSpec as P

LOGIT_MULT = 16.0
LOGIT_SHIFT = -10.0
EPSILON = 1e-06

AXES = ("y", "zl", "c", "zh", "x")
SIZES = (8, 2, 2, 4, 4)
NY, NZH, NX = 8, 4, 4
ROWS, FEATURES, LANES = 16, 1152, 128
COLS = FEATURES // LANES
PACK = COLS * ROWS
PAIRS = 8192
F32, BF16 = jnp.float32, jnp.bfloat16

VMEM = pl.BlockSpec(memory_space=pltpu.VMEM)
ANY = pl.BlockSpec(memory_space=pl.ANY)
SMEM = pl.BlockSpec(memory_space=pltpu.SMEM)
HBM = pl.BlockSpec(memory_space=pltpu.HBM)


def shape(*dims):
    return jax.ShapeDtypeStruct(dims, F32)


def call(kernel, ins, outs, in_specs=None, out_specs=None, flops=0, vmem=8, **kw):
    moved = 4 * sum(a.size for a in list(ins) + list(outs))
    return pl.pallas_call(
        kernel,
        out_shape=outs,
        in_specs=in_specs or [VMEM] * len(ins),
        out_specs=out_specs or [VMEM] * len(outs),
        cost_estimate=pl.CostEstimate(flops=flops, bytes_accessed=moved, transcendentals=0),
        compiler_params=pltpu.CompilerParams(vmem_limit_bytes=vmem * 2**20),
        **kw,
    )(*ins)


def exchange(values, axes):
    return lax.all_to_all(values, axes, 0, 0, tiled=True)


def turned(values, axis, step):
    count = lax.axis_size(axis)
    pairs = [(c * count + i, c * count + (i + (1 - 2 * c) * step) % count) for c in range(2) for i in range(count)]
    return lax.ppermute(values, ("c", axis), pairs)


def planes(values, step):
    pairs = []
    for c in range(2):
        for z in range(2 * NZH):
            to = (z + (1 - 2 * c) * step) % (2 * NZH)
            pairs.append((((z % 2) * 2 + c) * NZH + z // 2, ((to % 2) * 2 + c) * NZH + to // 2))
    return lax.ppermute(values, ("zl", "c", "zh"), pairs)


def other_core(values):
    return lax.ppermute(values, "c", [(0, 1), (1, 0)])


def normalize(values):
    length = jnp.sqrt(jnp.sum(values * values, axis=1, keepdims=True) + EPSILON)
    return values / length, length


def project_back(unit, direction, length):
    inner = jnp.sum(unit * direction, axis=1, keepdims=True)
    return (direction - unit * inner) / length


def halves(values):
    high = values.astype(BF16)
    return high, (values - high.astype(F32)).astype(BF16)


def dot3(left, right, dims):
    def dot(a, b):
        return lax.dot_general(a, b, (dims, ((), ())), preferred_element_type=F32)

    return dot(left[1], right[0]) + dot(left[0], right[1]) + dot(left[0], right[0])


def image_unit_kernel(image_ref, out):
    unit = normalize(image_ref[...])[0]
    for x in range(NX):
        out[pl.ds(x * NZH * ROWS, NZH * ROWS), :] = unit


def text_unit_kernel(text_ref, image_ref, out):
    out[...] = normalize(text_ref[...])[0]


def in_turn(place, image_ref):
    rows = image_ref.shape[0] // NX
    starts = [pl.multiple_of(place[2 + k] * rows, rows) for k in range(NX)]
    return halves(jnp.concatenate([image_ref[pl.ds(start, rows), :] for start in starts], axis=0))


def tile_kernel(place, image_ref, a_ref, b_ref, c_ref, d_ref, slope_out, other_out):
    image = in_turn(place, image_ref)
    quarter = a_ref.shape[0]
    count = image_ref.shape[0]
    row = lax.broadcasted_iota(jnp.int32, (count, quarter), 0) - place[0]
    column = lax.broadcasted_iota(jnp.int32, (count, quarter), 1) - place[1]
    matched = (row == column) & (row >= 0) & (row < ROWS)
    total = jnp.zeros((), F32)
    for k, ref in ((2, c_ref), (3, d_ref), (0, a_ref), (1, b_ref)):
        logits = LOGIT_MULT * dot3(image, halves(ref[...]), ((1,), (1,))) + LOGIT_SHIFT
        if k == 0:
            logits = jnp.where(matched, -logits, logits)
        small = jnp.exp(-jnp.abs(logits))
        total += jnp.sum(jnp.maximum(logits, 0.0) + jnp.log1p(small))
        slope = jnp.where(logits >= 0.0, 1.0, small) / (1.0 + small) * (LOGIT_MULT / PAIRS)
        if k == 0:
            slope = jnp.where(matched, -slope, slope)
        slope_out[:, pl.ds(k * quarter, quarter)] = slope
        if k >= 2:
            other_out[pl.ds((k - 2) * quarter, quarter), :] = dot3(halves(slope), image, ((0,), (0,)))
    other_out[pl.ds(2 * quarter, 8), :] = jnp.full((8, FEATURES), total)


def image_kernel(slope_ref, a_ref, b_ref, c_ref, d_ref, *outs):
    quarter = a_ref.shape[0]
    total = None
    for k, ref in enumerate((a_ref, b_ref, c_ref, d_ref)):
        slope = slope_ref[:, pl.ds(k * quarter, quarter)]
        term = dot3(halves(slope), halves(ref[...]), ((1,), (0,)))
        total = term if total is None else total + term
    rows = total.shape[0] // NX
    for k, out in enumerate(outs):
        out[...] = total[k * rows : (k + 1) * rows]


def text_kernel(place, slope_ref, image_ref, other_ref, received_ref, x0, keep_out, send_out):
    image = in_turn(place, image_ref)
    quarter = keep_out.shape[0] - 8
    last = pl.ds(2 * quarter, 8)
    loss = other_ref[last, :] + received_ref[last, :]
    for k, out in ((1, send_out), (0, keep_out)):
        rows = pl.ds(k * quarter, quarter)
        out[pl.ds(0, quarter), :] = dot3(halves(slope_ref[:, rows]), image, ((0,), (0,))) + received_ref[rows, :]
        out[pl.ds(quarter, 8), :] = loss


def relay_kernel(left, right, out):
    out[...] = left[...] + right[...]


def split_kernel(place, x0, x1, x2, *outs):
    for k, out in enumerate(outs):
        rows = pl.ds(pl.multiple_of(place[2 + NX + k] * ROWS, ROWS), ROWS)
        out[...] = x0[rows, :] + (x1[rows, :] + x2[rows, :])


def pack_kernel(keep_ref, plane_ref, relay_ref, packed_out):
    last, first = pl.ds(NY * ROWS, 8), pl.ds(0, LANES)
    loss = keep_ref[last, first] + plane_ref[last, first]
    for y in range(NY):
        rows = pl.ds(y * ROWS, ROWS)
        for k in range(COLS):
            lanes = pl.ds(k * LANES, LANES)
            packed_out[y, pl.ds(k * ROWS, ROWS), :] = keep_ref[rows, lanes] + plane_ref[rows, lanes]
        packed_out[y, pl.ds(PACK, 8), :] = loss


def loss_kernel(packed_ref, out):
    total = packed_ref[0, pl.ds(PACK, 8), :]
    for y in range(1, NY):
        total = total + packed_ref[y, pl.ds(PACK, 8), :]
    for k in range(out.shape[0] // 8):
        out[pl.ds(8 * k, 8), :] = total


def mean_kernel(losses_ref, out):
    out[0, 0] = jnp.sum(losses_ref[:, 0:1]) / PAIRS


def image_grad_kernel(emb_ref, z0, z1, z2, out):
    unit, length = normalize(emb_ref[...])
    out[...] = project_back(unit, z0[...] + (z1[...] + z2[...]), length)


def text_grad_kernel(emb_ref, packed_ref, out):
    unit, length = normalize(emb_ref[...])
    total = packed_ref[0]
    for y in range(1, NY):
        total = total + packed_ref[y]
    direction = jnp.concatenate([total[k * ROWS : (k + 1) * ROWS] for k in range(COLS)], axis=1)
    out[...] = project_back(unit, direction, length)


def on_device(image_emb, text_emb):
    rows, features = image_emb.shape
    text_y = exchange(jnp.tile(text_emb, (NY, 1)), "y")
    image_z = lax.all_gather(image_emb, "zh", axis=0, tiled=True)
    (image_tiled,) = call(image_unit_kernel, (image_z,), [shape(NX * NZH * rows, features)])
    (text_a,) = call(
        text_unit_kernel, (text_y, image_z), [shape(*text_y.shape)], in_specs=[VMEM, ANY]
    )
    image = exchange(image_tiled, "x")
    text_b = planes(text_a, -1)
    texts = (text_a, text_b, other_core(text_a), other_core(text_b))

    count, quarter = image.shape[0], text_a.shape[0]
    part = count // NX
    x, zh, turn = lax.axis_index("x"), lax.axis_index("zh"), 1 - 2 * lax.axis_index("c")
    blocks = [(at + step) % NX for at in (x, zh) for step in (0, -turn, turn, 2)]
    place = jnp.stack([zh * rows, lax.axis_index("y") * rows, *blocks]).astype(jnp.int32)
    product = 2 * count * quarter * features * 3
    slope, other = call(
        tile_kernel,
        (place, image, *texts),
        [shape(count, 4 * quarter), shape(2 * quarter + 8, features)],
        in_specs=[SMEM] + [VMEM] * 5,
        flops=6 * product,
        vmem=20,
    )
    received = other_core(other)
    xs = call(image_kernel, (slope, *texts), [shape(part, features)] * NX, flops=4 * product, vmem=20)
    relay = turned(xs[3], "x", -1)
    ahead = turned(xs[2], "x", 1)
    keep, send = call(
        text_kernel,
        (place, slope, image, other, received, xs[0]),
        [shape(quarter + 8, features)] * 2,
        in_specs=[SMEM] + [VMEM] * 4 + [ANY],
        flops=2 * product,
        vmem=20,
    )
    plane = planes(send, 1)
    (packed,) = call(
        pack_kernel,
        (keep, plane, relay),
        [shape(NY, PACK + 8, LANES)],
        in_specs=[VMEM] * 2 + [ANY],
    )
    (relay,) = call(relay_kernel, (xs[1], relay), [shape(part, features)])
    back = turned(relay, "x", -1)
    zs = call(
        split_kernel,
        (place, xs[0], back, ahead),
        [shape(rows, features)] * NZH,
        in_specs=[SMEM] + [VMEM] * 3,
    )
    packed = exchange(packed, "y")
    relay = turned(zs[3], "zh", -1)
    ahead = turned(zs[2], "zh", 1)
    (relay,) = call(relay_kernel, (zs[1], relay), [shape(rows, features)])
    back = turned(relay, "zh", -1)
    (image_grad,) = call(image_grad_kernel, (image_emb, zs[0], back, ahead), [shape(rows, features)])
    (loss,) = call(loss_kernel, (packed,), [shape(NZH * NX, LANES)])
    losses = exchange(loss, ("zh", "x"))
    (text_grad,) = call(text_grad_kernel, (text_emb, packed), [shape(rows, features)])
    (loss,) = call(mean_kernel, (losses,), [shape(1, 1)], out_specs=[SMEM])
    return loss.reshape(()), image_grad, text_grad


def solution(mesh):
    split = Mesh(mesh.devices.reshape(SIZES), AXES)
    return jax.shard_map(
        on_device,
        mesh=split,
        in_specs=(P(AXES, None), P(AXES, None)),
        out_specs=(P(), P(AXES, None), P(AXES, None)),
        check_vma=False,
    )
```

```python
import jax
import jax.numpy as jnp
from jax import lax
from jax.experimental import pallas as pl
from jax.experimental.pallas import tpu as pltpu
from jax.sharding import Mesh, PartitionSpec as P

LOGIT_MULT = 16.0
LOGIT_SHIFT = -10.0
EPSILON = 1e-06

AXES = ("y", "zl", "c", "zh", "x")
SIZES = (8, 2, 2, 4, 4)
NY, NZH, NX = 8, 4, 4
ROWS, FEATURES, LANES = 16, 1152, 128
COLS = FEATURES // LANES
PACK = COLS * ROWS
PAIRS = 8192
F32, BF16 = jnp.float32, jnp.bfloat16

VMEM = pl.BlockSpec(memory_space=pltpu.VMEM)
ANY = pl.BlockSpec(memory_space=pl.ANY)
SMEM = pl.BlockSpec(memory_space=pltpu.SMEM)
HBM = pl.BlockSpec(memory_space=pltpu.HBM)


def shape(*dims):
    return jax.ShapeDtypeStruct(dims, F32)


def call(kernel, ins, outs, in_specs=None, out_specs=None, flops=0, vmem=8, **kw):
    moved = 4 * sum(a.size for a in list(ins) + list(outs))
    return pl.pallas_call(
        kernel,
        out_shape=outs,
        in_specs=in_specs or [VMEM] * len(ins),
        out_specs=out_specs or [VMEM] * len(outs),
        cost_estimate=pl.CostEstimate(flops=flops, bytes_accessed=moved, transcendentals=0),
        compiler_params=pltpu.CompilerParams(vmem_limit_bytes=vmem * 2**20),
        **kw,
    )(*ins)


def exchange(values, axes):
    return lax.all_to_all(values, axes, 0, 0, tiled=True)


def planes(values, step):
    pairs = []
    for c in range(2):
        for z in range(2 * NZH):
            to = (z + (1 - 2 * c) * step) % (2 * NZH)
            pairs.append((((z % 2) * 2 + c) * NZH + z // 2, ((to % 2) * 2 + c) * NZH + to // 2))
    return lax.ppermute(values, ("zl", "c", "zh"), pairs)


def other_core(values):
    return lax.ppermute(values, "c", [(0, 1), (1, 0)])


def normalize(values):
    length = jnp.sqrt(jnp.sum(values * values, axis=1, keepdims=True) + EPSILON)
    return values / length, length


def project_back(unit, direction, length):
    inner = jnp.sum(unit * direction, axis=1, keepdims=True)
    return (direction - unit * inner) / length


def halves(values):
    high = values.astype(BF16)
    return high, (values - high.astype(F32)).astype(BF16)


def dot3(left, right, dims):
    def dot(a, b):
        return lax.dot_general(a, b, (dims, ((), ())), preferred_element_type=F32)

    return dot(left[1], right[0]) + dot(left[0], right[1]) + dot(left[0], right[0])


def image_unit_kernel(image_ref, out):
    unit = normalize(image_ref[...])[0]
    for x in range(NX):
        out[pl.ds(x * NZH * ROWS, NZH * ROWS), :] = unit


def text_unit_kernel(text_ref, image_ref, out):
    out[...] = normalize(text_ref[...])[0]


def tile_kernel(place, image_ref, a_ref, b_ref, c_ref, d_ref, slope_out, other_out):
    image = halves(image_ref[...])
    quarter = a_ref.shape[0]
    count = image_ref.shape[0]
    row = lax.broadcasted_iota(jnp.int32, (count, quarter), 0) - place[0]
    column = lax.broadcasted_iota(jnp.int32, (count, quarter), 1) - place[1]
    matched = (row == column) & (row >= 0) & (row < ROWS)
    total = jnp.zeros((), F32)
    for k, ref in ((2, c_ref), (3, d_ref), (0, a_ref), (1, b_ref)):
        logits = LOGIT_MULT * dot3(image, halves(ref[...]), ((1,), (1,))) + LOGIT_SHIFT
        if k == 0:
            logits = jnp.where(matched, -logits, logits)
        small = jnp.exp(-jnp.abs(logits))
        total += jnp.sum(jnp.maximum(logits, 0.0) + jnp.log1p(small))
        slope = jnp.where(logits >= 0.0, 1.0, small) / (1.0 + small) * (LOGIT_MULT / PAIRS)
        if k == 0:
            slope = jnp.where(matched, -slope, slope)
        slope_out[:, pl.ds(k * quarter, quarter)] = slope
        if k >= 2:
            other_out[pl.ds((k - 2) * quarter, quarter), :] = dot3(halves(slope), image, ((0,), (0,)))
    other_out[pl.ds(2 * quarter, 8), :] = jnp.full((8, FEATURES), total)


def image_kernel(slope_ref, a_ref, b_ref, c_ref, d_ref, out):
    quarter = a_ref.shape[0]
    total = None
    for k, ref in enumerate((a_ref, b_ref, c_ref, d_ref)):
        slope = slope_ref[:, pl.ds(k * quarter, quarter)]
        term = dot3(halves(slope), halves(ref[...]), ((1,), (0,)))
        total = term if total is None else total + term
    out[...] = total


def text_kernel(slope_ref, image_ref, other_ref, received_ref, x0, keep_out, send_out):
    image = halves(image_ref[...])
    quarter = keep_out.shape[0] - 8
    last = pl.ds(2 * quarter, 8)
    loss = other_ref[last, :] + received_ref[last, :]
    for k, out in ((1, send_out), (0, keep_out)):
        rows = pl.ds(k * quarter, quarter)
        out[pl.ds(0, quarter), :] = dot3(halves(slope_ref[:, rows]), image, ((0,), (0,))) + received_ref[rows, :]
        out[pl.ds(quarter, 8), :] = loss


def sum_kernel(parts_ref, out):
    rows = out.shape[0]
    parts = [parts_ref[pl.ds(x * rows, rows), :] for x in range(NX)]
    out[...] = (parts[0] + parts[1]) + (parts[2] + parts[3])


def pack_kernel(keep_ref, plane_ref, image_ref, packed_out):
    last, first = pl.ds(NY * ROWS, 8), pl.ds(0, LANES)
    loss = keep_ref[last, first] + plane_ref[last, first]
    for y in range(NY):
        rows = pl.ds(y * ROWS, ROWS)
        for k in range(COLS):
            lanes = pl.ds(k * LANES, LANES)
            packed_out[y, pl.ds(k * ROWS, ROWS), :] = keep_ref[rows, lanes] + plane_ref[rows, lanes]
        packed_out[y, pl.ds(PACK, 8), :] = loss


def loss_kernel(packed_ref, out):
    total = packed_ref[0, pl.ds(PACK, 8), :]
    for y in range(1, NY):
        total = total + packed_ref[y, pl.ds(PACK, 8), :]
    for k in range(out.shape[0] // 8):
        out[pl.ds(8 * k, 8), :] = total


def mean_kernel(losses_ref, out):
    out[0, 0] = jnp.sum(losses_ref[:, 0:1]) / PAIRS


def image_grad_kernel(emb_ref, direction_ref, out):
    unit, length = normalize(emb_ref[...])
    out[...] = project_back(unit, direction_ref[...], length)


def text_grad_kernel(emb_ref, packed_ref, out):
    unit, length = normalize(emb_ref[...])
    total = packed_ref[0]
    for y in range(1, NY):
        total = total + packed_ref[y]
    direction = jnp.concatenate([total[k * ROWS : (k + 1) * ROWS] for k in range(COLS)], axis=1)
    out[...] = project_back(unit, direction, length)


def on_device(image_emb, text_emb):
    rows, features = image_emb.shape
    text_y = exchange(jnp.tile(text_emb, (NY, 1)), "y")
    image_z = lax.all_gather(image_emb, "zh", axis=0, tiled=True)
    (image_tiled,) = call(image_unit_kernel, (image_z,), [shape(NX * NZH * rows, features)])
    (text_a,) = call(
        text_unit_kernel, (text_y, image_z), [shape(*text_y.shape)], in_specs=[VMEM, ANY]
    )
    image = exchange(image_tiled, "x")
    text_b = planes(text_a, -1)
    texts = (text_a, text_b, other_core(text_a), other_core(text_b))

    count, quarter = image.shape[0], text_a.shape[0]
    own = (lax.axis_index("x") * NZH + lax.axis_index("zh")) * rows
    place = jnp.stack([own, lax.axis_index("y") * rows]).astype(jnp.int32)
    product = 2 * count * quarter * features * 3
    slope, other = call(
        tile_kernel,
        (place, image, *texts),
        [shape(count, 4 * quarter), shape(2 * quarter + 8, features)],
        in_specs=[SMEM] + [VMEM] * 5,
        flops=6 * product,
        vmem=20,
    )
    received = other_core(other)
    (image_sums,) = call(image_kernel, (slope, *texts), [shape(count, features)], flops=4 * product, vmem=20)
    keep, send = call(
        text_kernel,
        (slope, image, other, received, image_sums),
        [shape(quarter + 8, features)] * 2,
        in_specs=[VMEM] * 4 + [ANY],
        flops=2 * product,
        vmem=20,
    )
    plane = planes(send, 1)
    image_parts = exchange(image_sums, "x")
    (image_x,) = call(sum_kernel, (image_parts,), [shape(count // NX, features)])
    image_dir = lax.psum_scatter(image_x, "zh", scatter_dimension=0, tiled=True)
    (packed,) = call(
        pack_kernel,
        (keep, plane, image_x),
        [shape(NY, PACK + 8, LANES)],
        in_specs=[VMEM] * 2 + [ANY],
    )
    packed = exchange(packed, "y")
    (image_grad,) = call(image_grad_kernel, (image_emb, image_dir), [shape(rows, features)])
    (loss,) = call(loss_kernel, (packed,), [shape(NZH * NX, LANES)])
    losses = exchange(loss, ("zh", "x"))
    (text_grad,) = call(text_grad_kernel, (text_emb, packed), [shape(rows, features)])
    (loss,) = call(mean_kernel, (losses,), [shape(1, 1)], out_specs=[SMEM])
    return loss.reshape(()), image_grad, text_grad


def solution(mesh):
    split = Mesh(mesh.devices.reshape(SIZES), AXES)
    return jax.shard_map(
        on_device,
        mesh=split,
        in_specs=(P(AXES, None), P(AXES, None)),
        out_specs=(P(), P(AXES, None), P(AXES, None)),
        check_vma=False,
    )
```

```python
import jax
import jax.numpy as jnp
from jax import lax
from jax.experimental import pallas as pl
from jax.experimental.pallas import tpu as pltpu
from jax.sharding import Mesh, PartitionSpec as P

LOGIT_MULT = 16.0
LOGIT_SHIFT = -10.0
EPSILON = 1e-06

AXES = ("y", "zl", "c", "zh", "x")
SIZES = (8, 2, 2, 4, 4)
NY, NZH, NX = 8, 4, 4
ROWS, FEATURES, LANES = 16, 1152, 128
COLS = FEATURES // LANES
PACK = COLS * ROWS
PAIRS = 8192
F32, BF16 = jnp.float32, jnp.bfloat16

VMEM = pl.BlockSpec(memory_space=pltpu.VMEM)
ANY = pl.BlockSpec(memory_space=pl.ANY)
SMEM = pl.BlockSpec(memory_space=pltpu.SMEM)
HBM = pl.BlockSpec(memory_space=pltpu.HBM)


def shape(*dims):
    return jax.ShapeDtypeStruct(dims, F32)


def call(kernel, ins, outs, in_specs=None, out_specs=None, flops=0, vmem=8, **kw):
    moved = 4 * sum(a.size for a in list(ins) + list(outs))
    return pl.pallas_call(
        kernel,
        out_shape=outs,
        in_specs=in_specs or [VMEM] * len(ins),
        out_specs=out_specs or [VMEM] * len(outs),
        cost_estimate=pl.CostEstimate(flops=flops, bytes_accessed=moved, transcendentals=0),
        compiler_params=pltpu.CompilerParams(vmem_limit_bytes=vmem * 2**20),
        **kw,
    )(*ins)


def exchange(values, axes):
    return lax.all_to_all(values, axes, 0, 0, tiled=True)


def turned(values, axis, step):
    count = lax.axis_size(axis)
    pairs = [(c * count + i, c * count + (i + (1 - 2 * c) * step) % count) for c in range(2) for i in range(count)]
    return lax.ppermute(values, ("c", axis), pairs)


def planes(values, step):
    pairs = []
    for c in range(2):
        for z in range(2 * NZH):
            to = (z + (1 - 2 * c) * step) % (2 * NZH)
            pairs.append((((z % 2) * 2 + c) * NZH + z // 2, ((to % 2) * 2 + c) * NZH + to // 2))
    return lax.ppermute(values, ("zl", "c", "zh"), pairs)


def other_core(values):
    return lax.ppermute(values, "c", [(0, 1), (1, 0)])


def normalize(values):
    length = jnp.sqrt(jnp.sum(values * values, axis=1, keepdims=True) + EPSILON)
    return values / length, length


def project_back(unit, direction, length):
    inner = jnp.sum(unit * direction, axis=1, keepdims=True)
    return (direction - unit * inner) / length


def halves(values):
    high = values.astype(BF16)
    return high, (values - high.astype(F32)).astype(BF16)


def dot3(left, right, dims):
    def dot(a, b):
        return lax.dot_general(a, b, (dims, ((), ())), preferred_element_type=F32)

    return dot(left[1], right[0]) + dot(left[0], right[1]) + dot(left[0], right[0])


def tie_kernel(*refs):
    pass


def after(values, other):
    out = [shape(*values.shape)]
    return call(tie_kernel, (values, other), out, [ANY] * 2, [ANY], input_output_aliases={0: 0})[0]


def image_unit_kernel(image_ref, out):
    unit = normalize(image_ref[...])[0]
    for x in range(NX):
        out[pl.ds(x * NZH * ROWS, NZH * ROWS), :] = unit


def text_unit_kernel(text_ref, image_units, out):
    out[...] = normalize(text_ref[...])[0]


def in_turn(place, image_ref):
    rows = image_ref.shape[0] // NX
    starts = [pl.multiple_of(place[2 + k] * rows, rows) for k in range(NX)]
    return halves(jnp.concatenate([image_ref[pl.ds(start, rows), :] for start in starts], axis=0))


def tile_kernel(place, image_ref, a_ref, b_ref, c_ref, d_ref, slope_out, other_out):
    image = in_turn(place, image_ref)
    quarter = a_ref.shape[0]
    count = image_ref.shape[0]
    row = lax.broadcasted_iota(jnp.int32, (count, quarter), 0) - place[0]
    column = lax.broadcasted_iota(jnp.int32, (count, quarter), 1) - place[1]
    matched = (row == column) & (row >= 0) & (row < ROWS)
    total = jnp.zeros((), F32)
    for k, ref in ((2, c_ref), (3, d_ref), (0, a_ref), (1, b_ref)):
        logits = LOGIT_MULT * dot3(image, halves(ref[...]), ((1,), (1,))) + LOGIT_SHIFT
        if k == 0:
            logits = jnp.where(matched, -logits, logits)
        small = jnp.exp(-jnp.abs(logits))
        total += jnp.sum(jnp.maximum(logits, 0.0) + jnp.log1p(small))
        slope = jnp.where(logits >= 0.0, 1.0, small) / (1.0 + small) * (LOGIT_MULT / PAIRS)
        if k == 0:
            slope = jnp.where(matched, -slope, slope)
        slope_out[:, pl.ds(k * quarter, quarter)] = slope
        if k >= 2:
            other_out[pl.ds((k - 2) * quarter, quarter), :] = dot3(halves(slope), image, ((0,), (0,)))
    other_out[pl.ds(2 * quarter, 8), :] = jnp.full((8, FEATURES), total)


def image_kernel(slope_ref, a_ref, b_ref, c_ref, d_ref, *outs):
    quarter = a_ref.shape[0]
    total = None
    for k, ref in enumerate((a_ref, b_ref, c_ref, d_ref)):
        slope = slope_ref[:, pl.ds(k * quarter, quarter)]
        term = dot3(halves(slope), halves(ref[...]), ((1,), (0,)))
        total = term if total is None else total + term
    rows = total.shape[0] // NX
    for k, out in enumerate(outs):
        out[pl.ds(0, rows), :] = total[k * rows : (k + 1) * rows]


def text_kernel(place, slope_ref, image_ref, other_ref, received_ref, *refs):
    keep_out, send_out = refs[NX : NX + 2]
    blocks, (loss_ref, sems) = refs[NX + 2 : 2 * NX + 2], refs[2 * NX + 2 :]
    image = in_turn(place, image_ref)
    quarter = keep_out.shape[0]
    last = pl.ds(2 * quarter, 8)
    loss_ref[...] = other_ref[last, :] + received_ref[last, :]
    copies = [
        pltpu.make_async_copy(loss_ref, block.at[pl.ds(block.shape[0] - 8, 8), :], sems.at[k])
        for k, block in enumerate(blocks)
    ]
    for copy in copies:
        copy.start()
    for k, out in ((1, send_out), (0, keep_out)):
        rows = pl.ds(k * quarter, quarter)
        out[...] = dot3(halves(slope_ref[:, rows]), image, ((0,), (0,))) + received_ref[rows, :]
    for copy in copies:
        copy.wait()


def relay_kernel(left, right, out):
    out[...] = left[...] + right[...]


def split_kernel(place, x0, x1, x2, *outs):
    last = pl.ds(NZH * ROWS, 8)
    loss = x0[last, :] + (x1[last, :] + x2[last, :])
    for k, out in enumerate(outs):
        rows = pl.ds(pl.multiple_of(place[2 + NX + k] * ROWS, ROWS), ROWS)
        out[pl.ds(0, ROWS), :] = x0[rows, :] + (x1[rows, :] + x2[rows, :])
        out[pl.ds(ROWS, 8), :] = loss


def pack_kernel(keep_ref, plane_ref, image_ref, packed_out):
    for y in range(NY):
        rows = pl.ds(y * ROWS, ROWS)
        for k in range(COLS):
            lanes = pl.ds(k * LANES, LANES)
            packed_out[y, pl.ds(k * ROWS, ROWS), :] = keep_ref[rows, lanes] + plane_ref[rows, lanes]


def mean_kernel(losses_ref, out):
    out[0, 0] = jnp.sum(losses_ref[:, 0:1]) / PAIRS


def image_grad_kernel(emb_ref, z0, z1, z2, out, loss_out):
    unit, length = normalize(emb_ref[...])
    total = z0[...] + (z1[...] + z2[...])
    out[...] = project_back(unit, total[:ROWS], length)
    loss_out[...] = total[ROWS:, :LANES]


def text_grad_kernel(emb_ref, packed_ref, out):
    unit, length = normalize(emb_ref[...])
    total = packed_ref[0]
    for y in range(1, NY):
        total = total + packed_ref[y]
    direction = jnp.concatenate([total[k * ROWS : (k + 1) * ROWS] for k in range(COLS)], axis=1)
    out[...] = project_back(unit, direction, length)


def on_device(image_emb, text_emb):
    rows, features = image_emb.shape
    text_y = exchange(jnp.tile(text_emb, (NY, 1)), "y")
    image_z = lax.all_gather(image_emb, "zh", axis=0, tiled=True)
    (image_tiled,) = call(image_unit_kernel, (image_z,), [shape(NX * NZH * rows, features)])
    (text_a,) = call(
        text_unit_kernel, (text_y, image_tiled), [shape(*text_y.shape)], in_specs=[VMEM, ANY]
    )
    image = exchange(image_tiled, "x")
    text_b = planes(text_a, -1)
    texts = (text_a, text_b, other_core(text_a), other_core(text_b))

    count, quarter = image.shape[0], text_a.shape[0]
    part = count // NX
    x, zh, turn = lax.axis_index("x"), lax.axis_index("zh"), 1 - 2 * lax.axis_index("c")
    blocks = [(at + step) % NX for at in (x, zh) for step in (0, -turn, turn, 2)]
    place = jnp.stack([zh * rows, lax.axis_index("y") * rows, *blocks]).astype(jnp.int32)
    product = 2 * count * quarter * features * 3
    slope, other = call(
        tile_kernel,
        (place, image, *texts),
        [shape(count, 4 * quarter), shape(2 * quarter + 8, features)],
        in_specs=[SMEM] + [VMEM] * 5,
        flops=6 * product,
        vmem=20,
    )
    received = other_core(other)
    xs = call(image_kernel, (slope, *texts), [shape(part + 8, features)] * NX, flops=4 * product, vmem=20)
    keep, send, *xs = call(
        text_kernel,
        (place, slope, image, other, received, *xs),
        [shape(quarter, features)] * 2 + [shape(part + 8, features)] * NX,
        in_specs=[SMEM] + [VMEM] * 4 + [ANY] * NX,
        out_specs=[VMEM] * 2 + [ANY] * NX,
        input_output_aliases={5 + k: 2 + k for k in range(NX)},
        scratch_shapes=[pltpu.VMEM((8, features), F32), pltpu.SemaphoreType.DMA((NX,))],
        flops=2 * product,
        vmem=20,
    )
    relay = turned(xs[3], "x", -1)
    ahead = turned(xs[2], "x", 1)
    plane = planes(send, 1)
    (relay,) = call(relay_kernel, (xs[1], relay), [shape(part + 8, features)])
    back = turned(relay, "x", -1)
    zs = call(
        split_kernel,
        (place, xs[0], back, ahead),
        [shape(rows + 8, features)] * NZH,
        in_specs=[SMEM] + [VMEM] * 3,
    )
    (packed,) = call(pack_kernel, (keep, plane, zs[0]), [shape(NY, PACK, LANES)], in_specs=[VMEM] * 2 + [ANY])
    packed = exchange(packed, "y")
    relay = turned(zs[3], "zh", -1)
    ahead = turned(zs[2], "zh", 1)
    (relay,) = call(relay_kernel, (zs[1], relay), [shape(rows + 8, features)])
    back = turned(relay, "zh", -1)
    image_grad, loss = call(
        image_grad_kernel, (image_emb, zs[0], back, ahead), [shape(rows, features), shape(8, LANES)]
    )
    loss = loss + lax.ppermute(loss, "zl", [(0, 1), (1, 0)])
    losses = exchange(after(loss, packed), "y")
    (text_grad,) = call(text_grad_kernel, (text_emb, packed), [shape(rows, features)])
    (loss,) = call(mean_kernel, (losses,), [shape(1, 1)], out_specs=[SMEM])
    return loss.reshape(()), image_grad, text_grad


def solution(mesh):
    split = Mesh(mesh.devices.reshape(SIZES), AXES)
    return jax.shard_map(
        on_device,
        mesh=split,
        in_specs=(P(AXES, None), P(AXES, None)),
        out_specs=(P(), P(AXES, None), P(AXES, None)),
        check_vma=False,
    )
```

```python
import jax
import jax.numpy as jnp
from jax import lax
from jax.experimental import pallas as pl
from jax.experimental.pallas import tpu as pltpu
from jax.sharding import Mesh, PartitionSpec as P

LOGIT_MULT = 16.0
LOGIT_SHIFT = -10.0
EPSILON = 1e-06

AXES = ("y", "zl", "c", "zh", "x")
SIZES = (8, 2, 2, 4, 4)
NY, NZH, NX = 8, 4, 4
ROWS, FEATURES, LANES = 16, 1152, 128
COLS = FEATURES // LANES
PACK = COLS * ROWS
PAIRS = 8192
F32, BF16 = jnp.float32, jnp.bfloat16

VMEM = pl.BlockSpec(memory_space=pltpu.VMEM)
ANY = pl.BlockSpec(memory_space=pl.ANY)
SMEM = pl.BlockSpec(memory_space=pltpu.SMEM)
HBM = pl.BlockSpec(memory_space=pltpu.HBM)


def shape(*dims):
    return jax.ShapeDtypeStruct(dims, F32)


def call(kernel, ins, outs, in_specs=None, out_specs=None, flops=0, vmem=8, **kw):
    moved = 4 * sum(a.size for a in list(ins) + list(outs))
    return pl.pallas_call(
        kernel,
        out_shape=outs,
        in_specs=in_specs or [VMEM] * len(ins),
        out_specs=out_specs or [VMEM] * len(outs),
        cost_estimate=pl.CostEstimate(flops=flops, bytes_accessed=moved, transcendentals=0),
        compiler_params=pltpu.CompilerParams(vmem_limit_bytes=vmem * 2**20),
        **kw,
    )(*ins)


def exchange(values, axes):
    return lax.all_to_all(values, axes, 0, 0, tiled=True)


def turned(values, axis, step):
    count = lax.axis_size(axis)
    pairs = [(c * count + i, c * count + (i + (1 - 2 * c) * step) % count) for c in range(2) for i in range(count)]
    return lax.ppermute(values, ("c", axis), pairs)


def planes(values, step):
    pairs = []
    for c in range(2):
        for z in range(2 * NZH):
            to = (z + (1 - 2 * c) * step) % (2 * NZH)
            pairs.append((((z % 2) * 2 + c) * NZH + z // 2, ((to % 2) * 2 + c) * NZH + to // 2))
    return lax.ppermute(values, ("zl", "c", "zh"), pairs)


def other_core(values):
    return lax.ppermute(values, "c", [(0, 1), (1, 0)])


def normalize(values):
    length = jnp.sqrt(jnp.sum(values * values, axis=1, keepdims=True) + EPSILON)
    return values / length, length


def project_back(unit, direction, length):
    inner = jnp.sum(unit * direction, axis=1, keepdims=True)
    return (direction - unit * inner) / length


def halves(values):
    high = values.astype(BF16)
    return high, (values - high.astype(F32)).astype(BF16)


def dot3(left, right, dims):
    def dot(a, b):
        return lax.dot_general(a, b, (dims, ((), ())), preferred_element_type=F32)

    return dot(left[1], right[0]) + dot(left[0], right[1]) + dot(left[0], right[0])


def image_unit_kernel(image_ref, out):
    unit = normalize(image_ref[...])[0]
    for x in range(NX):
        out[pl.ds(x * NZH * ROWS, NZH * ROWS), :] = unit


def text_unit_kernel(text_ref, image_units, out):
    out[...] = normalize(text_ref[...])[0]


def in_turn(place, image_ref):
    rows = image_ref.shape[0] // NX
    starts = [pl.multiple_of(place[2 + k] * rows, rows) for k in range(NX)]
    return halves(jnp.concatenate([image_ref[pl.ds(start, rows), :] for start in starts], axis=0))


def tile_kernel(place, image_ref, a_ref, b_ref, c_ref, d_ref, slope_out, other_out):
    image = in_turn(place, image_ref)
    quarter = a_ref.shape[0]
    count = image_ref.shape[0]
    row = lax.broadcasted_iota(jnp.int32, (count, quarter), 0) - place[0]
    column = lax.broadcasted_iota(jnp.int32, (count, quarter), 1) - place[1]
    matched = (row == column) & (row >= 0) & (row < ROWS)
    total = jnp.zeros((), F32)
    for k, ref in ((2, c_ref), (3, d_ref), (0, a_ref), (1, b_ref)):
        logits = LOGIT_MULT * dot3(image, halves(ref[...]), ((1,), (1,))) + LOGIT_SHIFT
        if k == 0:
            logits = jnp.where(matched, -logits, logits)
        small = jnp.exp(-jnp.abs(logits))
        total += jnp.sum(jnp.maximum(logits, 0.0) + jnp.log1p(small))
        slope = jnp.where(logits >= 0.0, 1.0, small) / (1.0 + small) * (LOGIT_MULT / PAIRS)
        if k == 0:
            slope = jnp.where(matched, -slope, slope)
        slope_out[:, pl.ds(k * quarter, quarter)] = slope
        if k >= 2:
            other_out[pl.ds((k - 2) * quarter, quarter), :] = dot3(halves(slope), image, ((0,), (0,)))
    other_out[pl.ds(2 * quarter, 8), :] = jnp.full((8, FEATURES), total)


def image_kernel(slope_ref, a_ref, b_ref, c_ref, d_ref, *outs):
    quarter = a_ref.shape[0]
    total = None
    for k, ref in enumerate((a_ref, b_ref, c_ref, d_ref)):
        slope = slope_ref[:, pl.ds(k * quarter, quarter)]
        term = dot3(halves(slope), halves(ref[...]), ((1,), (0,)))
        total = term if total is None else total + term
    rows = total.shape[0] // NX
    for k, out in enumerate(outs):
        out[...] = total[k * rows : (k + 1) * rows]


def text_kernel(place, slope_ref, image_ref, other_ref, received_ref, x0, keep_out, send_out, loss_out):
    image = in_turn(place, image_ref)
    quarter = keep_out.shape[0]
    for k, out in ((1, send_out), (0, keep_out)):
        rows = pl.ds(k * quarter, quarter)
        out[...] = dot3(halves(slope_ref[:, rows]), image, ((0,), (0,))) + received_ref[rows, :]
    last, first = pl.ds(2 * quarter, 8), pl.ds(0, LANES)
    for k in range(loss_out.shape[0] // 8):
        loss_out[pl.ds(8 * k, 8), :] = other_ref[last, first] + received_ref[last, first]


def relay_kernel(left, right, out):
    out[...] = left[...] + right[...]


def split_kernel(place, x0, x1, x2, *outs):
    for k, out in enumerate(outs):
        rows = pl.ds(pl.multiple_of(place[2 + NX + k] * ROWS, ROWS), ROWS)
        out[...] = x0[rows, :] + (x1[rows, :] + x2[rows, :])


def pack_kernel(keep_ref, plane_ref, losses_ref, back_ref, ahead_ref, packed_out):
    loss = jnp.full((8, LANES), jnp.sum(losses_ref[:, 0:1]))
    for y in range(NY):
        rows = pl.ds(y * ROWS, ROWS)
        for k in range(COLS):
            lanes = pl.ds(k * LANES, LANES)
            packed_out[y, pl.ds(k * ROWS, ROWS), :] = keep_ref[rows, lanes] + plane_ref[rows, lanes]
        packed_out[y, pl.ds(PACK, 8), :] = loss


def image_grad_kernel(emb_ref, z0, z1, z2, out):
    unit, length = normalize(emb_ref[...])
    out[...] = project_back(unit, z0[...] + (z1[...] + z2[...]), length)


def text_grad_kernel(emb_ref, packed_ref, out, loss_out):
    unit, length = normalize(emb_ref[...])
    total = packed_ref[0]
    for y in range(1, NY):
        total = total + packed_ref[y]
    direction = jnp.concatenate([total[k * ROWS : (k + 1) * ROWS] for k in range(COLS)], axis=1)
    out[...] = project_back(unit, direction, length)
    loss_out[0, 0] = jnp.max(total[PACK:]) / PAIRS


def on_device(image_emb, text_emb):
    rows, features = image_emb.shape
    text_y = exchange(jnp.tile(text_emb, (NY, 1)), "y")
    image_z = lax.all_gather(image_emb, "zh", axis=0, tiled=True)
    (image_tiled,) = call(image_unit_kernel, (image_z,), [shape(NX * NZH * rows, features)])
    (text_a,) = call(
        text_unit_kernel, (text_y, image_tiled), [shape(*text_y.shape)], in_specs=[VMEM, ANY]
    )
    image = exchange(image_tiled, "x")
    text_b = planes(text_a, -1)
    texts = (text_a, text_b, other_core(text_a), other_core(text_b))

    count, quarter = image.shape[0], text_a.shape[0]
    part = count // NX
    x, zh, turn = lax.axis_index("x"), lax.axis_index("zh"), 1 - 2 * lax.axis_index("c")
    blocks = [(at + step) % NX for at in (x, zh) for step in (0, -turn, turn, 2)]
    place = jnp.stack([zh * rows, lax.axis_index("y") * rows, *blocks]).astype(jnp.int32)
    product = 2 * count * quarter * features * 3
    slope, other = call(
        tile_kernel,
        (place, image, *texts),
        [shape(count, 4 * quarter), shape(2 * quarter + 8, features)],
        in_specs=[SMEM] + [VMEM] * 5,
        flops=6 * product,
        vmem=20,
    )
    received = other_core(other)
    xs = call(image_kernel, (slope, *texts), [shape(part, features)] * NX, flops=4 * product, vmem=20)
    keep, send, loss = call(
        text_kernel,
        (place, slope, image, other, received, xs[0]),
        [shape(quarter, features)] * 2 + [shape(32, LANES)],
        in_specs=[SMEM] + [VMEM] * 4 + [ANY],
        flops=2 * product,
        vmem=20,
    )
    losses = exchange(loss, ("zl", "zh", "x"))
    relay = turned(xs[3], "x", -1)
    ahead = turned(xs[2], "x", 1)
    plane = planes(send, 1)
    (relay,) = call(relay_kernel, (xs[1], relay), [shape(part, features)])
    back = turned(relay, "x", -1)
    zs = call(
        split_kernel,
        (place, xs[0], back, ahead),
        [shape(rows, features)] * NZH,
        in_specs=[SMEM] + [VMEM] * 3,
    )
    (packed,) = call(
        pack_kernel,
        (keep, plane, losses, back, ahead),
        [shape(NY, PACK + 8, LANES)],
        in_specs=[VMEM] * 3 + [ANY] * 2,
    )
    packed = exchange(packed, "y")
    relay = turned(zs[3], "zh", -1)
    ahead = turned(zs[2], "zh", 1)
    (relay,) = call(relay_kernel, (zs[1], relay), [shape(rows, features)])
    back = turned(relay, "zh", -1)
    (image_grad,) = call(image_grad_kernel, (image_emb, zs[0], back, ahead), [shape(rows, features)])
    text_grad, loss = call(
        text_grad_kernel,
        (text_emb, packed),
        [shape(rows, features), shape(1, 1)],
        out_specs=[VMEM, SMEM],
    )
    return loss.reshape(()), image_grad, text_grad


def solution(mesh):
    split = Mesh(mesh.devices.reshape(SIZES), AXES)
    return jax.shard_map(
        on_device,
        mesh=split,
        in_specs=(P(AXES, None), P(AXES, None)),
        out_specs=(P(), P(AXES, None), P(AXES, None)),
        check_vma=False,
    )
```

```python
import jax
import jax.numpy as jnp
from jax import lax
from jax.experimental import pallas as pl
from jax.experimental.pallas import tpu as pltpu
from jax.sharding import Mesh, PartitionSpec as P

LOGIT_MULT = 16.0
LOGIT_SHIFT = -10.0
EPSILON = 1e-06

AXES = ("y", "zl", "c", "zh", "x")
SIZES = (8, 2, 2, 4, 4)
NY, NZH, NX = 8, 4, 4
ROWS, FEATURES, LANES = 16, 1152, 128
COLS = FEATURES // LANES
PACK = COLS * ROWS
PAIRS = 8192
F32, BF16 = jnp.float32, jnp.bfloat16

VMEM = pl.BlockSpec(memory_space=pltpu.VMEM)
ANY = pl.BlockSpec(memory_space=pl.ANY)
SMEM = pl.BlockSpec(memory_space=pltpu.SMEM)
HBM = pl.BlockSpec(memory_space=pltpu.HBM)


def shape(*dims):
    return jax.ShapeDtypeStruct(dims, F32)


def call(kernel, ins, outs, in_specs=None, out_specs=None, flops=0, vmem=8, **kw):
    moved = 4 * sum(a.size for a in list(ins) + list(outs))
    return pl.pallas_call(
        kernel,
        out_shape=outs,
        in_specs=in_specs or [VMEM] * len(ins),
        out_specs=out_specs or [VMEM] * len(outs),
        cost_estimate=pl.CostEstimate(flops=flops, bytes_accessed=moved, transcendentals=0),
        compiler_params=pltpu.CompilerParams(vmem_limit_bytes=vmem * 2**20),
        **kw,
    )(*ins)


def exchange(values, axes):
    return lax.all_to_all(values, axes, 0, 0, tiled=True)


def turned(values, axis, step):
    count = lax.axis_size(axis)
    pairs = [(c * count + i, c * count + (i + (1 - 2 * c) * step) % count) for c in range(2) for i in range(count)]
    return lax.ppermute(values, ("c", axis), pairs)


def planes(values, step):
    pairs = []
    for c in range(2):
        for z in range(2 * NZH):
            to = (z + (1 - 2 * c) * step) % (2 * NZH)
            pairs.append((((z % 2) * 2 + c) * NZH + z // 2, ((to % 2) * 2 + c) * NZH + to // 2))
    return lax.ppermute(values, ("zl", "c", "zh"), pairs)


def other_core(values):
    return lax.ppermute(values, "c", [(0, 1), (1, 0)])


def normalize(values):
    length = jnp.sqrt(jnp.sum(values * values, axis=1, keepdims=True) + EPSILON)
    return values / length, length


def project_back(unit, direction, length):
    inner = jnp.sum(unit * direction, axis=1, keepdims=True)
    return (direction - unit * inner) / length


def halves(values):
    high = values.astype(BF16)
    return high, (values - high.astype(F32)).astype(BF16)


def dot3(left, right, dims):
    def dot(a, b):
        return lax.dot_general(a, b, (dims, ((), ())), preferred_element_type=F32)

    return dot(left[1], right[0]) + dot(left[0], right[1]) + dot(left[0], right[0])


def image_unit_kernel(image_ref, out):
    unit = normalize(image_ref[...])[0]
    for x in range(NX):
        out[pl.ds(x * NZH * ROWS, NZH * ROWS), :] = unit


def text_unit_kernel(text_ref, image_units, out):
    out[...] = normalize(text_ref[...])[0]


def in_turn(place, image_ref):
    rows = image_ref.shape[0] // NX
    starts = [pl.multiple_of(place[2 + k] * rows, rows) for k in range(NX)]
    return halves(jnp.concatenate([image_ref[pl.ds(start, rows), :] for start in starts], axis=0))


def tile_kernel(place, image_ref, a_ref, b_ref, c_ref, d_ref, slope_out, other_out):
    image = in_turn(place, image_ref)
    quarter = a_ref.shape[0]
    count = image_ref.shape[0]
    row = lax.broadcasted_iota(jnp.int32, (count, quarter), 0) - place[0]
    column = lax.broadcasted_iota(jnp.int32, (count, quarter), 1) - place[1]
    matched = (row == column) & (row >= 0) & (row < ROWS)
    total = jnp.zeros((), F32)
    for k, ref in ((2, c_ref), (3, d_ref), (0, a_ref), (1, b_ref)):
        logits = LOGIT_MULT * dot3(image, halves(ref[...]), ((1,), (1,))) + LOGIT_SHIFT
        if k == 0:
            logits = jnp.where(matched, -logits, logits)
        small = jnp.exp(-jnp.abs(logits))
        total += jnp.sum(jnp.maximum(logits, 0.0) + jnp.log1p(small))
        slope = jnp.where(logits >= 0.0, 1.0, small) / (1.0 + small) * (LOGIT_MULT / PAIRS)
        if k == 0:
            slope = jnp.where(matched, -slope, slope)
        slope_out[:, pl.ds(k * quarter, quarter)] = slope
        if k >= 2:
            other_out[pl.ds((k - 2) * quarter, quarter), :] = dot3(halves(slope), image, ((0,), (0,)))
    other_out[pl.ds(2 * quarter, 8), :] = jnp.full((8, FEATURES), total)


def image_kernel(slope_ref, a_ref, b_ref, c_ref, d_ref, *outs):
    quarter = a_ref.shape[0]
    total = None
    for k, ref in enumerate((a_ref, b_ref, c_ref, d_ref)):
        slope = slope_ref[:, pl.ds(k * quarter, quarter)]
        term = dot3(halves(slope), halves(ref[...]), ((1,), (0,)))
        total = term if total is None else total + term
    rows = total.shape[0] // NX
    for k, out in enumerate(outs):
        out[...] = total[k * rows : (k + 1) * rows]


def text_kernel(place, slope_ref, image_ref, other_ref, received_ref, x0, keep_out, send_out, loss_out):
    image = in_turn(place, image_ref)
    quarter = keep_out.shape[0]
    for k, out in ((1, send_out), (0, keep_out)):
        rows = pl.ds(k * quarter, quarter)
        out[...] = dot3(halves(slope_ref[:, rows]), image, ((0,), (0,))) + received_ref[rows, :]
    last, first = pl.ds(2 * quarter, 8), pl.ds(0, LANES)
    for k in range(loss_out.shape[0] // 8):
        loss_out[pl.ds(8 * k, 8), :] = other_ref[last, first] + received_ref[last, first]


def relay_kernel(left, right, out):
    out[...] = left[...] + right[...]


def split_kernel(place, x0, x1, x2, *outs):
    for k, out in enumerate(outs):
        rows = pl.ds(pl.multiple_of(place[2 + NX + k] * ROWS, ROWS), ROWS)
        out[...] = x0[rows, :] + (x1[rows, :] + x2[rows, :])


def pack_kernel(keep_ref, plane_ref, losses_ref, back_ref, ahead_ref, packed_out):
    loss = jnp.full((8, LANES), jnp.sum(losses_ref[:, 0:1]))
    for y in range(NY):
        rows = pl.ds(y * ROWS, ROWS)
        for k in range(COLS):
            lanes = pl.ds(k * LANES, LANES)
            packed_out[y, pl.ds(k * ROWS, ROWS), :] = keep_ref[rows, lanes] + plane_ref[rows, lanes]
        packed_out[y, pl.ds(PACK, 8), :] = loss


def image_grad_kernel(emb_ref, z0, z1, z2, z3, out):
    unit, length = normalize(emb_ref[...])
    out[...] = project_back(unit, (z0[...] + z1[...]) + (z2[...] + z3[...]), length)


def text_grad_kernel(emb_ref, packed_ref, out, loss_out):
    unit, length = normalize(emb_ref[...])
    total = packed_ref[0]
    for y in range(1, NY):
        total = total + packed_ref[y]
    direction = jnp.concatenate([total[k * ROWS : (k + 1) * ROWS] for k in range(COLS)], axis=1)
    out[...] = project_back(unit, direction, length)
    loss_out[0, 0] = jnp.max(total[PACK:]) / PAIRS


def on_device(image_emb, text_emb):
    rows, features = image_emb.shape
    text_y = exchange(jnp.tile(text_emb, (NY, 1)), "y")
    image_z = lax.all_gather(image_emb, "zh", axis=0, tiled=True)
    (image_tiled,) = call(image_unit_kernel, (image_z,), [shape(NX * NZH * rows, features)])
    (text_a,) = call(
        text_unit_kernel, (text_y, image_tiled), [shape(*text_y.shape)], in_specs=[VMEM, ANY]
    )
    image = exchange(image_tiled, "x")
    text_b = planes(text_a, -1)
    texts = (text_a, text_b, other_core(text_a), other_core(text_b))

    count, quarter = image.shape[0], text_a.shape[0]
    part = count // NX
    x, zh, turn = lax.axis_index("x"), lax.axis_index("zh"), 1 - 2 * lax.axis_index("c")
    blocks = [(at + step) % NX for at in (x, zh) for step in (0, -turn, turn, 2)]
    place = jnp.stack([zh * rows, lax.axis_index("y") * rows, *blocks]).astype(jnp.int32)
    product = 2 * count * quarter * features * 3
    slope, other = call(
        tile_kernel,
        (place, image, *texts),
        [shape(count, 4 * quarter), shape(2 * quarter + 8, features)],
        in_specs=[SMEM] + [VMEM] * 5,
        flops=6 * product,
        vmem=20,
    )
    received = other_core(other)
    xs = call(image_kernel, (slope, *texts), [shape(part, features)] * NX, flops=4 * product, vmem=20)
    keep, send, loss = call(
        text_kernel,
        (place, slope, image, other, received, xs[0]),
        [shape(quarter, features)] * 2 + [shape(32, LANES)],
        in_specs=[SMEM] + [VMEM] * 4 + [ANY],
        flops=2 * product,
        vmem=20,
    )
    losses = exchange(loss, ("zl", "zh", "x"))
    relay = turned(xs[3], "x", -1)
    ahead = turned(xs[2], "x", 1)
    plane = planes(send, 1)
    (relay,) = call(relay_kernel, (xs[1], relay), [shape(part, features)])
    back = turned(relay, "x", -1)
    zs = call(
        split_kernel,
        (place, xs[0], back, ahead),
        [shape(rows, features)] * NZH,
        in_specs=[SMEM] + [VMEM] * 3,
    )
    (packed,) = call(
        pack_kernel,
        (keep, plane, losses, back, ahead),
        [shape(NY, PACK + 8, LANES)],
        in_specs=[VMEM] * 3 + [ANY] * 2,
    )
    packed = exchange(packed, "y")
    zs = [zs[0], turned(zs[3], "zh", 2), turned(zs[1], "zh", -1), turned(zs[2], "zh", 1)]
    (image_grad,) = call(image_grad_kernel, (image_emb, *zs), [shape(rows, features)])
    text_grad, loss = call(
        text_grad_kernel,
        (text_emb, packed),
        [shape(rows, features), shape(1, 1)],
        out_specs=[VMEM, SMEM],
    )
    return loss.reshape(()), image_grad, text_grad


def solution(mesh):
    split = Mesh(mesh.devices.reshape(SIZES), AXES)
    return jax.shard_map(
        on_device,
        mesh=split,
        in_specs=(P(AXES, None), P(AXES, None)),
        out_specs=(P(), P(AXES, None), P(AXES, None)),
        check_vma=False,
    )
```

```python
import jax
import jax.numpy as jnp
from jax import lax
from jax.experimental import pallas as pl
from jax.experimental.pallas import tpu as pltpu
from jax.sharding import Mesh, PartitionSpec as P

LOGIT_MULT = 16.0
LOGIT_SHIFT = -10.0
EPSILON = 1e-06

AXES = ("y", "zl", "c", "zh", "x")
SIZES = (8, 2, 2, 4, 4)
NY, NZH, NX = 8, 4, 4
ROWS, FEATURES, LANES = 16, 1152, 128
COLS = FEATURES // LANES
PACK = COLS * ROWS
PAIRS = 8192
F32, BF16 = jnp.float32, jnp.bfloat16

VMEM = pl.BlockSpec(memory_space=pltpu.VMEM)
ANY = pl.BlockSpec(memory_space=pl.ANY)
SMEM = pl.BlockSpec(memory_space=pltpu.SMEM)
HBM = pl.BlockSpec(memory_space=pltpu.HBM)


def shape(*dims):
    return jax.ShapeDtypeStruct(dims, F32)


def call(kernel, ins, outs, in_specs=None, out_specs=None, flops=0, vmem=8, **kw):
    moved = 4 * sum(a.size for a in list(ins) + list(outs))
    return pl.pallas_call(
        kernel,
        out_shape=outs,
        in_specs=in_specs or [VMEM] * len(ins),
        out_specs=out_specs or [VMEM] * len(outs),
        cost_estimate=pl.CostEstimate(flops=flops, bytes_accessed=moved, transcendentals=0),
        compiler_params=pltpu.CompilerParams(vmem_limit_bytes=vmem * 2**20),
        **kw,
    )(*ins)


def exchange(values, axes):
    return lax.all_to_all(values, axes, 0, 0, tiled=True)


def turned(values, axis, step):
    count = lax.axis_size(axis)
    pairs = [(c * count + i, c * count + (i + (1 - 2 * c) * step) % count) for c in range(2) for i in range(count)]
    return lax.ppermute(values, ("c", axis), pairs)


def planes(values, step):
    pairs = []
    for c in range(2):
        for z in range(2 * NZH):
            to = (z + (1 - 2 * c) * step) % (2 * NZH)
            pairs.append((((z % 2) * 2 + c) * NZH + z // 2, ((to % 2) * 2 + c) * NZH + to // 2))
    return lax.ppermute(values, ("zl", "c", "zh"), pairs)


def other_core(values):
    return lax.ppermute(values, "c", [(0, 1), (1, 0)])


def normalize(values):
    length = jnp.sqrt(jnp.sum(values * values, axis=1, keepdims=True) + EPSILON)
    return values / length, length


def project_back(unit, direction, length):
    inner = jnp.sum(unit * direction, axis=1, keepdims=True)
    return (direction - unit * inner) / length


def halves(values):
    high = values.astype(BF16)
    return high, (values - high.astype(F32)).astype(BF16)


def dot3(left, right, dims):
    def dot(a, b):
        return lax.dot_general(a, b, (dims, ((), ())), preferred_element_type=F32)

    return dot(left[1], right[0]) + dot(left[0], right[1]) + dot(left[0], right[0])


def image_unit_kernel(image_ref, out):
    unit = normalize(image_ref[...])[0]
    for x in range(NX):
        out[pl.ds(x * NZH * ROWS, NZH * ROWS), :] = unit


def text_unit_kernel(text_ref, image_units, out):
    out[...] = normalize(text_ref[...])[0]


def in_turn(place, image_ref):
    rows = image_ref.shape[0] // NX
    starts = [pl.multiple_of(place[2 + k] * rows, rows) for k in range(NX)]
    return halves(jnp.concatenate([image_ref[pl.ds(start, rows), :] for start in starts], axis=0))


def tile_kernel(place, image_ref, a_ref, b_ref, c_ref, d_ref, slope_out, other_out):
    image = in_turn(place, image_ref)
    quarter = a_ref.shape[0]
    count = image_ref.shape[0]
    row = lax.broadcasted_iota(jnp.int32, (count, quarter), 0) - place[0]
    column = lax.broadcasted_iota(jnp.int32, (count, quarter), 1) - place[1]
    matched = (row == column) & (row >= 0) & (row < ROWS)
    total = jnp.zeros((), F32)
    for k, ref in ((2, c_ref), (3, d_ref), (0, a_ref), (1, b_ref)):
        logits = LOGIT_MULT * dot3(image, halves(ref[...]), ((1,), (1,))) + LOGIT_SHIFT
        if k == 0:
            logits = jnp.where(matched, -logits, logits)
        small = jnp.exp(-jnp.abs(logits))
        total += jnp.sum(jnp.maximum(logits, 0.0) + jnp.log1p(small))
        slope = jnp.where(logits >= 0.0, 1.0, small) / (1.0 + small) * (LOGIT_MULT / PAIRS)
        if k == 0:
            slope = jnp.where(matched, -slope, slope)
        slope_out[:, pl.ds(k * quarter, quarter)] = slope
        if k >= 2:
            other_out[pl.ds((k - 2) * quarter, quarter), :] = dot3(halves(slope), image, ((0,), (0,)))
    other_out[pl.ds(2 * quarter, 8), :] = jnp.full((8, FEATURES), total)


def image_kernel(slope_ref, a_ref, b_ref, c_ref, d_ref, *outs):
    quarter = a_ref.shape[0]
    total = None
    for k, ref in enumerate((a_ref, b_ref, c_ref, d_ref)):
        slope = slope_ref[:, pl.ds(k * quarter, quarter)]
        term = dot3(halves(slope), halves(ref[...]), ((1,), (0,)))
        total = term if total is None else total + term
    rows = total.shape[0] // NX
    for k, out in enumerate(outs):
        out[...] = total[k * rows : (k + 1) * rows]


def text_kernel(place, slope_ref, image_ref, other_ref, received_ref, x0, keep_out, send_out, loss_out):
    image = in_turn(place, image_ref)
    quarter = keep_out.shape[0]
    for k, out in ((1, send_out), (0, keep_out)):
        rows = pl.ds(k * quarter, quarter)
        out[...] = dot3(halves(slope_ref[:, rows]), image, ((0,), (0,))) + received_ref[rows, :]
    last, first = pl.ds(2 * quarter, 8), pl.ds(0, LANES)
    for k in range(loss_out.shape[0] // 8):
        loss_out[pl.ds(8 * k, 8), :] = other_ref[last, first] + received_ref[last, first]


def relay_kernel(left, right, out):
    out[...] = left[...] + right[...]


def split_kernel(place, x0, x1, x2, *outs):
    for k, out in enumerate(outs):
        rows = pl.ds(pl.multiple_of(place[2 + NX + k] * ROWS, ROWS), ROWS)
        out[...] = x0[rows, :] + (x1[rows, :] + x2[rows, :])


def pack_kernel(keep_ref, plane_ref, losses_ref, first_ref, ahead_ref, packed_out):
    loss = jnp.full((8, LANES), jnp.sum(losses_ref[:, 0:1]))
    for y in range(NY):
        rows = pl.ds(y * ROWS, ROWS)
        for k in range(COLS):
            lanes = pl.ds(k * LANES, LANES)
            packed_out[y, pl.ds(k * ROWS, ROWS), :] = keep_ref[rows, lanes] + plane_ref[rows, lanes]
        packed_out[y, pl.ds(PACK, 8), :] = loss


def image_grad_kernel(emb_ref, z0, z1, z2, z3, out):
    unit, length = normalize(emb_ref[...])
    out[...] = project_back(unit, (z0[...] + z1[...]) + (z2[...] + z3[...]), length)


def text_grad_kernel(emb_ref, packed_ref, out, loss_out):
    unit, length = normalize(emb_ref[...])
    total = packed_ref[0]
    for y in range(1, NY):
        total = total + packed_ref[y]
    direction = jnp.concatenate([total[k * ROWS : (k + 1) * ROWS] for k in range(COLS)], axis=1)
    out[...] = project_back(unit, direction, length)
    loss_out[0, 0] = jnp.max(total[PACK:]) / PAIRS


def on_device(image_emb, text_emb):
    rows, features = image_emb.shape
    text_y = exchange(jnp.tile(text_emb, (NY, 1)), "y")
    image_z = lax.all_gather(image_emb, "zh", axis=0, tiled=True)
    (image_tiled,) = call(image_unit_kernel, (image_z,), [shape(NX * NZH * rows, features)])
    (text_a,) = call(
        text_unit_kernel, (text_y, image_tiled), [shape(*text_y.shape)], in_specs=[VMEM, ANY]
    )
    image = exchange(image_tiled, "x")
    text_b = planes(text_a, -1)
    texts = (text_a, text_b, other_core(text_a), other_core(text_b))

    count, quarter = image.shape[0], text_a.shape[0]
    part = count // NX
    x, zh, turn = lax.axis_index("x"), lax.axis_index("zh"), 1 - 2 * lax.axis_index("c")
    blocks = [(at + step) % NX for at in (x, zh) for step in (0, -turn, turn, 2)]
    place = jnp.stack([zh * rows, lax.axis_index("y") * rows, *blocks]).astype(jnp.int32)
    product = 2 * count * quarter * features * 3
    slope, other = call(
        tile_kernel,
        (place, image, *texts),
        [shape(count, 4 * quarter), shape(2 * quarter + 8, features)],
        in_specs=[SMEM] + [VMEM] * 5,
        flops=6 * product,
        vmem=20,
    )
    received = other_core(other)
    xs = call(image_kernel, (slope, *texts), [shape(part, features)] * NX, flops=4 * product, vmem=20)
    keep, send, loss = call(
        text_kernel,
        (place, slope, image, other, received, xs[0]),
        [shape(quarter, features)] * 2 + [shape(32, LANES)],
        in_specs=[SMEM] + [VMEM] * 4 + [ANY],
        flops=2 * product,
        vmem=20,
    )
    losses = exchange(loss, ("zl", "zh", "x"))
    first = turned(xs[3], "x", -1)
    ahead = turned(xs[2], "x", 1)
    plane = planes(send, 1)
    (relay,) = call(relay_kernel, (xs[1], first), [shape(part, features)])
    back = turned(relay, "x", -1)
    zs = call(
        split_kernel,
        (place, xs[0], back, ahead),
        [shape(rows, features)] * NZH,
        in_specs=[SMEM] + [VMEM] * 3,
    )
    (packed,) = call(
        pack_kernel,
        (keep, plane, losses, first, ahead),
        [shape(NY, PACK + 8, LANES)],
        in_specs=[VMEM] * 3 + [ANY] * 2,
    )
    packed = exchange(packed, "y")
    zs = [zs[0], turned(zs[3], "zh", 2), turned(zs[1], "zh", -1), turned(zs[2], "zh", 1)]
    (image_grad,) = call(image_grad_kernel, (image_emb, *zs), [shape(rows, features)])
    text_grad, loss = call(
        text_grad_kernel,
        (text_emb, packed),
        [shape(rows, features), shape(1, 1)],
        out_specs=[VMEM, SMEM],
    )
    return loss.reshape(()), image_grad, text_grad


def solution(mesh):
    split = Mesh(mesh.devices.reshape(SIZES), AXES)
    return jax.shard_map(
        on_device,
        mesh=split,
        in_specs=(P(AXES, None), P(AXES, None)),
        out_specs=(P(), P(AXES, None), P(AXES, None)),
        check_vma=False,
    )
```

```python
import jax
import jax.numpy as jnp
from jax import lax
from jax.experimental import pallas as pl
from jax.experimental.pallas import tpu as pltpu
from jax.sharding import Mesh, PartitionSpec as P

LOGIT_MULT = 16.0
LOGIT_SHIFT = -10.0
EPSILON = 1e-06

AXES = ("y", "zl", "c", "zh", "x")
SIZES = (8, 2, 2, 4, 4)
NY, NZH, NX = 8, 4, 4
ROWS, FEATURES, LANES = 16, 1152, 128
COLS = FEATURES // LANES
PACK = COLS * ROWS
PAIRS = 8192
F32, BF16 = jnp.float32, jnp.bfloat16

VMEM = pl.BlockSpec(memory_space=pltpu.VMEM)
ANY = pl.BlockSpec(memory_space=pl.ANY)
SMEM = pl.BlockSpec(memory_space=pltpu.SMEM)
HBM = pl.BlockSpec(memory_space=pltpu.HBM)


def shape(*dims):
    return jax.ShapeDtypeStruct(dims, F32)


def call(kernel, ins, outs, in_specs=None, out_specs=None, flops=0, vmem=8, **kw):
    moved = 4 * sum(a.size for a in list(ins) + list(outs))
    return pl.pallas_call(
        kernel,
        out_shape=outs,
        in_specs=in_specs or [VMEM] * len(ins),
        out_specs=out_specs or [VMEM] * len(outs),
        cost_estimate=pl.CostEstimate(flops=flops, bytes_accessed=moved, transcendentals=0),
        compiler_params=pltpu.CompilerParams(vmem_limit_bytes=vmem * 2**20),
        **kw,
    )(*ins)


def exchange(values, axes):
    return lax.all_to_all(values, axes, 0, 0, tiled=True)


def turned(values, axis, step):
    count = lax.axis_size(axis)
    pairs = [(c * count + i, c * count + (i + (1 - 2 * c) * step) % count) for c in range(2) for i in range(count)]
    return lax.ppermute(values, ("c", axis), pairs)


def planes(values, step):
    pairs = []
    for c in range(2):
        for z in range(2 * NZH):
            to = (z + (1 - 2 * c) * step) % (2 * NZH)
            pairs.append((((z % 2) * 2 + c) * NZH + z // 2, ((to % 2) * 2 + c) * NZH + to // 2))
    return lax.ppermute(values, ("zl", "c", "zh"), pairs)


def other_core(values):
    return lax.ppermute(values, "c", [(0, 1), (1, 0)])


def normalize(values):
    length = jnp.sqrt(jnp.sum(values * values, axis=1, keepdims=True) + EPSILON)
    return values / length, length


def project_back(unit, direction, length):
    inner = jnp.sum(unit * direction, axis=1, keepdims=True)
    return (direction - unit * inner) / length


def halves(values):
    high = values.astype(BF16)
    return high, (values - high.astype(F32)).astype(BF16)


def dot3(left, right, dims):
    def dot(a, b):
        return lax.dot_general(a, b, (dims, ((), ())), preferred_element_type=F32)

    return dot(left[1], right[0]) + dot(left[0], right[1]) + dot(left[0], right[0])


def image_unit_kernel(image_ref, out):
    unit = normalize(image_ref[...])[0]
    for x in range(NX):
        out[pl.ds(x * NZH * ROWS, NZH * ROWS), :] = unit


def text_unit_kernel(text_ref, image_units, out):
    out[...] = normalize(text_ref[...])[0]


def in_turn(place, image_ref):
    rows = image_ref.shape[0] // NX
    starts = [pl.multiple_of(place[2 + k] * rows, rows) for k in range(NX)]
    return halves(jnp.concatenate([image_ref[pl.ds(start, rows), :] for start in starts], axis=0))


def tile_kernel(place, image_ref, a_ref, b_ref, c_ref, d_ref, slope_out, other_out):
    image = in_turn(place, image_ref)
    quarter = a_ref.shape[0]
    count = image_ref.shape[0]
    row = lax.broadcasted_iota(jnp.int32, (count, quarter), 0) - place[0]
    column = lax.broadcasted_iota(jnp.int32, (count, quarter), 1) - place[1]
    matched = (row == column) & (row >= 0) & (row < ROWS)
    total = jnp.zeros((), F32)
    for k, ref in ((2, c_ref), (3, d_ref), (0, a_ref), (1, b_ref)):
        logits = LOGIT_MULT * dot3(image, halves(ref[...]), ((1,), (1,))) + LOGIT_SHIFT
        if k == 0:
            logits = jnp.where(matched, -logits, logits)
        small = jnp.exp(-jnp.abs(logits))
        total += jnp.sum(jnp.maximum(logits, 0.0) + jnp.log1p(small))
        slope = jnp.where(logits >= 0.0, 1.0, small) / (1.0 + small) * (LOGIT_MULT / PAIRS)
        if k == 0:
            slope = jnp.where(matched, -slope, slope)
        slope_out[:, pl.ds(k * quarter, quarter)] = slope
        if k >= 2:
            other_out[pl.ds((k - 2) * quarter, quarter), :] = dot3(halves(slope), image, ((0,), (0,)))
    other_out[pl.ds(2 * quarter, 8), :] = jnp.full((8, FEATURES), total)


def image_kernel(slope_ref, a_ref, b_ref, c_ref, d_ref, *outs):
    quarter = a_ref.shape[0]
    total = None
    for k, ref in enumerate((a_ref, b_ref, c_ref, d_ref)):
        slope = slope_ref[:, pl.ds(k * quarter, quarter)]
        term = dot3(halves(slope), halves(ref[...]), ((1,), (0,)))
        total = term if total is None else total + term
    rows = total.shape[0] // NX
    for k, out in enumerate(outs):
        out[...] = total[k * rows : (k + 1) * rows]


def text_kernel(place, slope_ref, image_ref, other_ref, received_ref, x0, keep_out, send_out, loss_out):
    image = in_turn(place, image_ref)
    quarter = keep_out.shape[0]
    for k, out in ((1, send_out), (0, keep_out)):
        rows = pl.ds(k * quarter, quarter)
        out[...] = dot3(halves(slope_ref[:, rows]), image, ((0,), (0,))) + received_ref[rows, :]
    last, first = pl.ds(2 * quarter, 8), pl.ds(0, LANES)
    for k in range(loss_out.shape[0] // 8):
        loss_out[pl.ds(8 * k, 8), :] = other_ref[last, first] + received_ref[last, first]


def relay_kernel(left, right, *refs):
    refs[-1][...] = left[...] + right[...]


def split_kernel(place, x0, x1, x2, *outs):
    for k, out in enumerate(outs):
        rows = pl.ds(pl.multiple_of(place[2 + NX + k] * ROWS, ROWS), ROWS)
        out[...] = x0[rows, :] + (x1[rows, :] + x2[rows, :])


def pack_kernel(keep_ref, plane_ref, losses_ref, back_ref, ahead_ref, packed_out):
    loss = jnp.full((8, LANES), jnp.sum(losses_ref[:, 0:1]))
    for y in range(NY):
        rows = pl.ds(y * ROWS, ROWS)
        for k in range(COLS):
            lanes = pl.ds(k * LANES, LANES)
            packed_out[y, pl.ds(k * ROWS, ROWS), :] = keep_ref[rows, lanes] + plane_ref[rows, lanes]
        packed_out[y, pl.ds(PACK, 8), :] = loss


def image_grad_kernel(emb_ref, z0, z1, z2, out):
    unit, length = normalize(emb_ref[...])
    out[...] = project_back(unit, z0[...] + (z1[...] + z2[...]), length)


def text_grad_kernel(emb_ref, packed_ref, out, loss_out):
    unit, length = normalize(emb_ref[...])
    total = packed_ref[0]
    for y in range(1, NY):
        total = total + packed_ref[y]
    direction = jnp.concatenate([total[k * ROWS : (k + 1) * ROWS] for k in range(COLS)], axis=1)
    out[...] = project_back(unit, direction, length)
    loss_out[0, 0] = jnp.max(total[PACK:]) / PAIRS


def on_device(image_emb, text_emb):
    rows, features = image_emb.shape
    text_y = exchange(jnp.tile(text_emb, (NY, 1)), "y")
    image_z = lax.all_gather(image_emb, "zh", axis=0, tiled=True)
    (image_tiled,) = call(image_unit_kernel, (image_z,), [shape(NX * NZH * rows, features)])
    (text_a,) = call(
        text_unit_kernel, (text_y, image_tiled), [shape(*text_y.shape)], in_specs=[VMEM, ANY]
    )
    image = exchange(image_tiled, "x")
    text_b = planes(text_a, -1)
    texts = (text_a, text_b, other_core(text_a), other_core(text_b))

    count, quarter = image.shape[0], text_a.shape[0]
    part = count // NX
    x, zh, turn = lax.axis_index("x"), lax.axis_index("zh"), 1 - 2 * lax.axis_index("c")
    blocks = [(at + step) % NX for at in (x, zh) for step in (0, -turn, turn, 2)]
    place = jnp.stack([zh * rows, lax.axis_index("y") * rows, *blocks]).astype(jnp.int32)
    product = 2 * count * quarter * features * 3
    slope, other = call(
        tile_kernel,
        (place, image, *texts),
        [shape(count, 4 * quarter), shape(2 * quarter + 8, features)],
        in_specs=[SMEM] + [VMEM] * 5,
        flops=6 * product,
        vmem=20,
    )
    received = other_core(other)
    xs = call(image_kernel, (slope, *texts), [shape(part, features)] * NX, flops=4 * product, vmem=20)
    keep, send, loss = call(
        text_kernel,
        (place, slope, image, other, received, xs[0]),
        [shape(quarter, features)] * 2 + [shape(32, LANES)],
        in_specs=[SMEM] + [VMEM] * 4 + [ANY],
        flops=2 * product,
        vmem=20,
    )
    losses = exchange(loss, ("zl", "zh", "x"))
    relay = turned(xs[3], "x", -1)
    ahead = turned(xs[2], "x", 1)
    plane = planes(send, 1)
    (relay,) = call(
        relay_kernel, (xs[1], relay, losses), [shape(part, features)], in_specs=[VMEM] * 2 + [ANY]
    )
    back = turned(relay, "x", -1)
    zs = call(
        split_kernel,
        (place, xs[0], back, ahead),
        [shape(rows, features)] * NZH,
        in_specs=[SMEM] + [VMEM] * 3,
    )
    (packed,) = call(
        pack_kernel,
        (keep, plane, losses, back, ahead),
        [shape(NY, PACK + 8, LANES)],
        in_specs=[VMEM] * 3 + [ANY] * 2,
    )
    packed = exchange(packed, "y")
    relay = turned(zs[3], "zh", -1)
    ahead = turned(zs[2], "zh", 1)
    (relay,) = call(relay_kernel, (zs[1], relay), [shape(rows, features)])
    back = turned(relay, "zh", -1)
    (image_grad,) = call(image_grad_kernel, (image_emb, zs[0], back, ahead), [shape(rows, features)])
    text_grad, loss = call(
        text_grad_kernel,
        (text_emb, packed),
        [shape(rows, features), shape(1, 1)],
        out_specs=[VMEM, SMEM],
    )
    return loss.reshape(()), image_grad, text_grad


def solution(mesh):
    split = Mesh(mesh.devices.reshape(SIZES), AXES)
    return jax.shard_map(
        on_device,
        mesh=split,
        in_specs=(P(AXES, None), P(AXES, None)),
        out_specs=(P(), P(AXES, None), P(AXES, None)),
        check_vma=False,
    )
```

```python
import jax
import jax.numpy as jnp
from jax import lax
from jax.experimental import pallas as pl
from jax.experimental.pallas import tpu as pltpu
from jax.sharding import Mesh, PartitionSpec as P

LOGIT_MULT = 16.0
LOGIT_SHIFT = -10.0
EPSILON = 1e-06

AXES = ("y", "zl", "c", "zh", "x")
SIZES = (8, 2, 2, 4, 4)
NY, NZH, NX = 8, 4, 4
ROWS, FEATURES, LANES = 16, 1152, 128
COLS = FEATURES // LANES
PACK = COLS * ROWS
PAIRS = 8192
F32, BF16 = jnp.float32, jnp.bfloat16

VMEM = pl.BlockSpec(memory_space=pltpu.VMEM)
ANY = pl.BlockSpec(memory_space=pl.ANY)
SMEM = pl.BlockSpec(memory_space=pltpu.SMEM)
HBM = pl.BlockSpec(memory_space=pltpu.HBM)


def shape(*dims):
    return jax.ShapeDtypeStruct(dims, F32)


def call(kernel, ins, outs, in_specs=None, out_specs=None, flops=0, vmem=8, **kw):
    moved = 4 * sum(a.size for a in list(ins) + list(outs))
    return pl.pallas_call(
        kernel,
        out_shape=outs,
        in_specs=in_specs or [VMEM] * len(ins),
        out_specs=out_specs or [VMEM] * len(outs),
        cost_estimate=pl.CostEstimate(flops=flops, bytes_accessed=moved, transcendentals=0),
        compiler_params=pltpu.CompilerParams(vmem_limit_bytes=vmem * 2**20),
        **kw,
    )(*ins)


def exchange(values, axes):
    return lax.all_to_all(values, axes, 0, 0, tiled=True)


def turned(values, axis, step):
    count = lax.axis_size(axis)
    pairs = [(c * count + i, c * count + (i + (1 - 2 * c) * step) % count) for c in range(2) for i in range(count)]
    return lax.ppermute(values, ("c", axis), pairs)


def planes(values, step):
    pairs = []
    for c in range(2):
        for z in range(2 * NZH):
            to = (z + (1 - 2 * c) * step) % (2 * NZH)
            pairs.append((((z % 2) * 2 + c) * NZH + z // 2, ((to % 2) * 2 + c) * NZH + to // 2))
    return lax.ppermute(values, ("zl", "c", "zh"), pairs)


def other_core(values):
    return lax.ppermute(values, "c", [(0, 1), (1, 0)])


def normalize(values):
    length = jnp.sqrt(jnp.sum(values * values, axis=1, keepdims=True) + EPSILON)
    return values / length, length


def project_back(unit, direction, length):
    inner = jnp.sum(unit * direction, axis=1, keepdims=True)
    return (direction - unit * inner) / length


def halves(values):
    high = values.astype(BF16)
    return high, (values - high.astype(F32)).astype(BF16)


def dot3(left, right, dims):
    def dot(a, b):
        return lax.dot_general(a, b, (dims, ((), ())), preferred_element_type=F32)

    return dot(left[1], right[0]) + dot(left[0], right[1]) + dot(left[0], right[0])


def image_unit_kernel(image_ref, out):
    unit = normalize(image_ref[...])[0]
    for x in range(NX):
        out[pl.ds(x * NZH * ROWS, NZH * ROWS), :] = unit


def text_unit_kernel(text_ref, image_units, out):
    out[...] = normalize(text_ref[...])[0]


def in_turn(place, image_ref):
    rows = image_ref.shape[0] // NX
    starts = [pl.multiple_of(place[2 + k] * rows, rows) for k in range(NX)]
    return halves(jnp.concatenate([image_ref[pl.ds(start, rows), :] for start in starts], axis=0))


def tile_kernel(place, image_ref, a_ref, b_ref, c_ref, d_ref, slope_out, other_out):
    image = in_turn(place, image_ref)
    quarter = a_ref.shape[0]
    count = image_ref.shape[0]
    row = lax.broadcasted_iota(jnp.int32, (count, quarter), 0) - place[0]
    column = lax.broadcasted_iota(jnp.int32, (count, quarter), 1) - place[1]
    matched = (row == column) & (row >= 0) & (row < ROWS)
    total = jnp.zeros((), F32)
    for k, ref in ((2, c_ref), (3, d_ref), (0, a_ref), (1, b_ref)):
        logits = LOGIT_MULT * dot3(image, halves(ref[...]), ((1,), (1,))) + LOGIT_SHIFT
        if k == 0:
            logits = jnp.where(matched, -logits, logits)
        small = jnp.exp(-jnp.abs(logits))
        total += jnp.sum(jnp.maximum(logits, 0.0) + jnp.log1p(small))
        slope = jnp.where(logits >= 0.0, 1.0, small) / (1.0 + small) * (LOGIT_MULT / PAIRS)
        if k == 0:
            slope = jnp.where(matched, -slope, slope)
        slope_out[:, pl.ds(k * quarter, quarter)] = slope
        if k >= 2:
            other_out[pl.ds((k - 2) * quarter, quarter), :] = dot3(halves(slope), image, ((0,), (0,)))
    other_out[pl.ds(2 * quarter, 8), :] = jnp.full((8, FEATURES), total)


def image_kernel(slope_ref, a_ref, b_ref, c_ref, d_ref, *outs):
    quarter = a_ref.shape[0]
    total = None
    for k, ref in enumerate((a_ref, b_ref, c_ref, d_ref)):
        slope = slope_ref[:, pl.ds(k * quarter, quarter)]
        term = dot3(halves(slope), halves(ref[...]), ((1,), (0,)))
        total = term if total is None else total + term
    rows = total.shape[0] // NX
    for k, out in enumerate(outs):
        out[...] = total[k * rows : (k + 1) * rows]


def text_kernel(place, slope_ref, image_ref, other_ref, received_ref, x0, keep_out, send_out, loss_out):
    image = in_turn(place, image_ref)
    quarter = keep_out.shape[0]
    for k, out in ((1, send_out), (0, keep_out)):
        rows = pl.ds(k * quarter, quarter)
        out[...] = dot3(halves(slope_ref[:, rows]), image, ((0,), (0,))) + received_ref[rows, :]
    last, first = pl.ds(2 * quarter, 8), pl.ds(0, LANES)
    for k in range(loss_out.shape[0] // 8):
        loss_out[pl.ds(8 * k, 8), :] = other_ref[last, first] + received_ref[last, first]


def relay_kernel(left, right, out):
    out[...] = left[...] + right[...]


def split_kernel(place, x0, x1, x2, *outs):
    for k, out in enumerate(outs):
        rows = pl.ds(pl.multiple_of(place[2 + NX + k] * ROWS, ROWS), ROWS)
        out[...] = x0[rows, :] + (x1[rows, :] + x2[rows, :])


def pack_kernel(keep_ref, plane_ref, losses_ref, image_ref, packed_out):
    loss = jnp.full((8, LANES), jnp.sum(losses_ref[:, 0:1]))
    for y in range(NY):
        rows = pl.ds(y * ROWS, ROWS)
        for k in range(COLS):
            lanes = pl.ds(k * LANES, LANES)
            packed_out[y, pl.ds(k * ROWS, ROWS), :] = keep_ref[rows, lanes] + plane_ref[rows, lanes]
        packed_out[y, pl.ds(PACK, 8), :] = loss


def image_grad_kernel(emb_ref, z0, z1, z2, out):
    unit, length = normalize(emb_ref[...])
    out[...] = project_back(unit, z0[...] + (z1[...] + z2[...]), length)


def text_grad_kernel(emb_ref, packed_ref, out, loss_out):
    unit, length = normalize(emb_ref[...])
    total = packed_ref[0]
    for y in range(1, NY):
        total = total + packed_ref[y]
    direction = jnp.concatenate([total[k * ROWS : (k + 1) * ROWS] for k in range(COLS)], axis=1)
    out[...] = project_back(unit, direction, length)
    loss_out[0, 0] = jnp.max(total[PACK:]) / PAIRS


def on_device(image_emb, text_emb):
    rows, features = image_emb.shape
    text_y = exchange(jnp.tile(text_emb, (NY, 1)), "y")
    image_z = lax.all_gather(image_emb, "zh", axis=0, tiled=True)
    (image_tiled,) = call(image_unit_kernel, (image_z,), [shape(NX * NZH * rows, features)])
    (text_a,) = call(
        text_unit_kernel, (text_y, image_tiled), [shape(*text_y.shape)], in_specs=[VMEM, ANY]
    )
    image = exchange(image_tiled, "x")
    text_b = planes(text_a, -1)
    texts = (text_a, text_b, other_core(text_a), other_core(text_b))

    count, quarter = image.shape[0], text_a.shape[0]
    part = count // NX
    x, zh, turn = lax.axis_index("x"), lax.axis_index("zh"), 1 - 2 * lax.axis_index("c")
    blocks = [(at + step) % NX for at in (x, zh) for step in (0, -turn, turn, 2)]
    place = jnp.stack([zh * rows, lax.axis_index("y") * rows, *blocks]).astype(jnp.int32)
    product = 2 * count * quarter * features * 3
    slope, other = call(
        tile_kernel,
        (place, image, *texts),
        [shape(count, 4 * quarter), shape(2 * quarter + 8, features)],
        in_specs=[SMEM] + [VMEM] * 5,
        flops=6 * product,
        vmem=20,
    )
    received = other_core(other)
    xs = call(image_kernel, (slope, *texts), [shape(part, features)] * NX, flops=4 * product, vmem=20)
    keep, send, loss = call(
        text_kernel,
        (place, slope, image, other, received, xs[0]),
        [shape(quarter, features)] * 2 + [shape(32, LANES)],
        in_specs=[SMEM] + [VMEM] * 4 + [ANY],
        flops=2 * product,
        vmem=20,
    )
    losses = exchange(loss, ("zl", "zh", "x"))
    relay = turned(xs[3], "x", -1)
    ahead = turned(xs[2], "x", 1)
    plane = planes(send, 1)
    (relay,) = call(relay_kernel, (xs[1], relay), [shape(part, features)])
    back = turned(relay, "x", -1)
    zs = call(
        split_kernel,
        (place, xs[0], back, ahead),
        [shape(rows, features)] * NZH,
        in_specs=[SMEM] + [VMEM] * 3,
    )
    (packed,) = call(
        pack_kernel,
        (keep, plane, losses, zs[0]),
        [shape(NY, PACK + 8, LANES)],
        in_specs=[VMEM] * 3 + [ANY],
    )
    packed = exchange(packed, "y")
    relay = turned(zs[3], "zh", -1)
    ahead = turned(zs[2], "zh", 1)
    (relay,) = call(relay_kernel, (zs[1], relay), [shape(rows, features)])
    back = turned(relay, "zh", -1)
    (image_grad,) = call(image_grad_kernel, (image_emb, zs[0], back, ahead), [shape(rows, features)])
    text_grad, loss = call(
        text_grad_kernel,
        (text_emb, packed),
        [shape(rows, features), shape(1, 1)],
        out_specs=[VMEM, SMEM],
    )
    return loss.reshape(()), image_grad, text_grad


def solution(mesh):
    split = Mesh(mesh.devices.reshape(SIZES), AXES)
    return jax.shard_map(
        on_device,
        mesh=split,
        in_specs=(P(AXES, None), P(AXES, None)),
        out_specs=(P(), P(AXES, None), P(AXES, None)),
        check_vma=False,
    )
```

```python
import jax
import jax.numpy as jnp
from jax import lax
from jax.experimental import pallas as pl
from jax.experimental.pallas import tpu as pltpu
from jax.sharding import Mesh, PartitionSpec as P

LOGIT_MULT = 16.0
LOGIT_SHIFT = -10.0
EPSILON = 1e-06

AXES = ("y", "zl", "c", "zh", "x")
SIZES = (8, 2, 2, 4, 4)
NY, NZH, NX = 8, 4, 4
ROWS, FEATURES, LANES = 16, 1152, 128
COLS = FEATURES // LANES
PACK = COLS * ROWS
PAIRS = 8192
F32, BF16 = jnp.float32, jnp.bfloat16

VMEM = pl.BlockSpec(memory_space=pltpu.VMEM)
ANY = pl.BlockSpec(memory_space=pl.ANY)
SMEM = pl.BlockSpec(memory_space=pltpu.SMEM)
HBM = pl.BlockSpec(memory_space=pltpu.HBM)


def shape(*dims):
    return jax.ShapeDtypeStruct(dims, F32)


def call(kernel, ins, outs, in_specs=None, out_specs=None, flops=0, vmem=8, **kw):
    moved = 4 * sum(a.size for a in list(ins) + list(outs))
    return pl.pallas_call(
        kernel,
        out_shape=outs,
        in_specs=in_specs or [VMEM] * len(ins),
        out_specs=out_specs or [VMEM] * len(outs),
        cost_estimate=pl.CostEstimate(flops=flops, bytes_accessed=moved, transcendentals=0),
        compiler_params=pltpu.CompilerParams(vmem_limit_bytes=vmem * 2**20),
        **kw,
    )(*ins)


def exchange(values, axes):
    return lax.all_to_all(values, axes, 0, 0, tiled=True)


def turned(values, axis, step):
    count = lax.axis_size(axis)
    pairs = [(c * count + i, c * count + (i + (1 - 2 * c) * step) % count) for c in range(2) for i in range(count)]
    return lax.ppermute(values, ("c", axis), pairs)


def planes(values, step):
    pairs = []
    for c in range(2):
        for z in range(2 * NZH):
            to = (z + (1 - 2 * c) * step) % (2 * NZH)
            pairs.append((((z % 2) * 2 + c) * NZH + z // 2, ((to % 2) * 2 + c) * NZH + to // 2))
    return lax.ppermute(values, ("zl", "c", "zh"), pairs)


def other_core(values):
    return lax.ppermute(values, "c", [(0, 1), (1, 0)])


def normalize(values):
    length = jnp.sqrt(jnp.sum(values * values, axis=1, keepdims=True) + EPSILON)
    return values / length, length


def project_back(unit, direction, length):
    inner = jnp.sum(unit * direction, axis=1, keepdims=True)
    return (direction - unit * inner) / length


def halves(values):
    high = values.astype(BF16)
    return high, (values - high.astype(F32)).astype(BF16)


def dot3(left, right, dims):
    def dot(a, b):
        return lax.dot_general(a, b, (dims, ((), ())), preferred_element_type=F32)

    return dot(left[1], right[0]) + dot(left[0], right[1]) + dot(left[0], right[0])


def image_unit_kernel(image_ref, out):
    unit = normalize(image_ref[...])[0]
    for x in range(NX):
        out[pl.ds(x * NZH * ROWS, NZH * ROWS), :] = unit


def text_unit_kernel(text_ref, image_units, out):
    out[...] = normalize(text_ref[...])[0]


def in_turn(place, image_ref):
    rows = image_ref.shape[0] // NX
    starts = [pl.multiple_of(place[2 + k] * rows, rows) for k in range(NX)]
    return halves(jnp.concatenate([image_ref[pl.ds(start, rows), :] for start in starts], axis=0))


def tile_kernel(place, image_ref, a_ref, b_ref, c_ref, d_ref, slope_out, other_out):
    image = in_turn(place, image_ref)
    quarter = a_ref.shape[0]
    count = image_ref.shape[0]
    row = lax.broadcasted_iota(jnp.int32, (count, quarter), 0) - place[0]
    column = lax.broadcasted_iota(jnp.int32, (count, quarter), 1) - place[1]
    matched = (row == column) & (row >= 0) & (row < ROWS)
    total = jnp.zeros((), F32)
    for k, ref in ((2, c_ref), (3, d_ref), (0, a_ref), (1, b_ref)):
        logits = LOGIT_MULT * dot3(image, halves(ref[...]), ((1,), (1,))) + LOGIT_SHIFT
        if k == 0:
            logits = jnp.where(matched, -logits, logits)
        small = jnp.exp(-jnp.abs(logits))
        total += jnp.sum(jnp.maximum(logits, 0.0) + jnp.log1p(small))
        slope = jnp.where(logits >= 0.0, 1.0, small) / (1.0 + small) * (LOGIT_MULT / PAIRS)
        if k == 0:
            slope = jnp.where(matched, -slope, slope)
        slope_out[:, pl.ds(k * quarter, quarter)] = slope
        if k >= 2:
            other_out[pl.ds((k - 2) * quarter, quarter), :] = dot3(halves(slope), image, ((0,), (0,)))
    other_out[pl.ds(2 * quarter, 8), :] = jnp.full((8, FEATURES), total)


def image_kernel(slope_ref, a_ref, b_ref, c_ref, d_ref, *outs):
    quarter = a_ref.shape[0]
    total = None
    for k, ref in enumerate((a_ref, b_ref, c_ref, d_ref)):
        slope = slope_ref[:, pl.ds(k * quarter, quarter)]
        term = dot3(halves(slope), halves(ref[...]), ((1,), (0,)))
        total = term if total is None else total + term
    rows = total.shape[0] // NX
    for k, out in enumerate(outs):
        out[...] = total[k * rows : (k + 1) * rows]


def text_kernel(place, slope_ref, image_ref, other_ref, received_ref, x0, keep_out, send_out, loss_out):
    image = in_turn(place, image_ref)
    quarter = keep_out.shape[0]
    for k, out in ((1, send_out), (0, keep_out)):
        rows = pl.ds(k * quarter, quarter)
        out[...] = dot3(halves(slope_ref[:, rows]), image, ((0,), (0,))) + received_ref[rows, :]
    last, first = pl.ds(2 * quarter, 8), pl.ds(0, LANES)
    for k in range(loss_out.shape[0] // 8):
        loss_out[pl.ds(8 * k, 8), :] = other_ref[last, first] + received_ref[last, first]


def relay_kernel(left, right, out):
    out[...] = left[...] + right[...]


def split_kernel(place, x0, x1, x2, *outs):
    for k, out in enumerate(outs):
        rows = pl.ds(pl.multiple_of(place[2 + NX + k] * ROWS, ROWS), ROWS)
        out[...] = x0[rows, :] + (x1[rows, :] + x2[rows, :])


def pack_kernel(keep_ref, plane_ref, losses_ref, image_ref, packed_out):
    loss = jnp.full((8, LANES), jnp.sum(losses_ref[:, 0:1]))
    for y in range(NY):
        rows = pl.ds(y * ROWS, ROWS)
        for k in range(COLS):
            lanes = pl.ds(k * LANES, LANES)
            packed_out[y, pl.ds(k * ROWS, ROWS), :] = keep_ref[rows, lanes] + plane_ref[rows, lanes]
        packed_out[y, pl.ds(PACK, 8), :] = loss


def image_grad_kernel(emb_ref, z0, z1, z2, out):
    unit, length = normalize(emb_ref[...])
    out[...] = project_back(unit, z0[...] + (z1[...] + z2[...]), length)


def text_grad_kernel(emb_ref, packed_ref, out, loss_out):
    unit, length = normalize(emb_ref[...])
    total = packed_ref[0]
    for y in range(1, NY):
        total = total + packed_ref[y]
    direction = jnp.concatenate([total[k * ROWS : (k + 1) * ROWS] for k in range(COLS)], axis=1)
    out[...] = project_back(unit, direction, length)
    loss_out[0, 0] = jnp.max(total[PACK:]) / PAIRS


def on_device(image_emb, text_emb):
    rows, features = image_emb.shape
    text_y = exchange(jnp.tile(text_emb, (NY, 1)), "y")
    image_z = lax.all_gather(image_emb, "zh", axis=0, tiled=True)
    (image_tiled,) = call(image_unit_kernel, (image_z,), [shape(NX * NZH * rows, features)])
    (text_a,) = call(
        text_unit_kernel, (text_y, image_tiled), [shape(*text_y.shape)], in_specs=[VMEM, ANY]
    )
    image = exchange(image_tiled, "x")
    text_b = planes(text_a, -1)
    texts = (text_a, text_b, other_core(text_a), other_core(text_b))

    count, quarter = image.shape[0], text_a.shape[0]
    part = count // NX
    x, zh, turn = lax.axis_index("x"), lax.axis_index("zh"), 1 - 2 * lax.axis_index("c")
    blocks = [(at + step) % NX for at in (x, zh) for step in (0, -turn, turn, 2)]
    place = jnp.stack([zh * rows, lax.axis_index("y") * rows, *blocks]).astype(jnp.int32)
    product = 2 * count * quarter * features * 3
    slope, other = call(
        tile_kernel,
        (place, image, *texts),
        [shape(count, 4 * quarter), shape(2 * quarter + 8, features)],
        in_specs=[SMEM] + [VMEM] * 5,
        flops=6 * product,
        vmem=20,
    )
    received = other_core(other)
    xs = call(image_kernel, (slope, *texts), [shape(part, features)] * NX, flops=4 * product, vmem=20)
    keep, send, loss = call(
        text_kernel,
        (place, slope, image, other, received, xs[0]),
        [shape(quarter, features)] * 2 + [shape(32, LANES)],
        in_specs=[SMEM] + [VMEM] * 4 + [ANY],
        flops=2 * product,
        vmem=20,
    )
    losses = exchange(loss, ("zl", "zh", "x"))
    relay = turned(xs[3], "x", -1)
    ahead = turned(xs[2], "x", 1)
    plane = planes(send, 1)
    (relay,) = call(relay_kernel, (xs[1], relay), [shape(part, features)])
    back = turned(relay, "x", -1)
    zs = call(
        split_kernel,
        (place, xs[0], back, ahead),
        [shape(rows, features)] * NZH,
        in_specs=[SMEM] + [VMEM] * 3,
    )
    first = turned(zs[3], "zh", -1)
    (packed,) = call(
        pack_kernel,
        (keep, plane, losses, first),
        [shape(NY, PACK + 8, LANES)],
        in_specs=[VMEM] * 3 + [ANY],
    )
    packed = exchange(packed, "y")
    ahead = turned(zs[2], "zh", 1)
    (relay,) = call(relay_kernel, (zs[1], first), [shape(rows, features)])
    back = turned(relay, "zh", -1)
    (image_grad,) = call(image_grad_kernel, (image_emb, zs[0], back, ahead), [shape(rows, features)])
    text_grad, loss = call(
        text_grad_kernel,
        (text_emb, packed),
        [shape(rows, features), shape(1, 1)],
        out_specs=[VMEM, SMEM],
    )
    return loss.reshape(()), image_grad, text_grad


def solution(mesh):
    split = Mesh(mesh.devices.reshape(SIZES), AXES)
    return jax.shard_map(
        on_device,
        mesh=split,
        in_specs=(P(AXES, None), P(AXES, None)),
        out_specs=(P(), P(AXES, None), P(AXES, None)),
        check_vma=False,
    )
```
